128 devices in a mesh: seq: 32 (over x, z, core), head: 4 (over y).
Axes of the slice: x: 4, y: 4, z: 4, core: 2. Of those that a mesh axis runs over, the one named last changes fastest.
Arguments:
- tokens: bfloat16 [8192, 2048], P('seq'), may hold values from -6 to 6
- mixer_gain: float32 [2048], replicated, may hold values from 0.5 to 1.5
- in_weight: bfloat16 [2048, 16, 768], P('seq', 'head'), may hold values from -0.125 to 0.125
- rate_weight: bfloat16 [2048, 2, 16], P('seq', None, 'head'), may hold values from -0.125 to 0.125
- conv_weight: float32 [4, 16, 512], P(None, 'head'), may hold values from -2 to 2
- decay_log: float32 [16], P('head'), may hold values from -9 to -3
- decay_bias: float32 [16], P('head'), may hold values from -1 to 1
- out_gain: float32 [256], replicated, may hold values from 0.5 to 1.5
- out_weight: bfloat16 [2048, 16, 256], P('seq', 'head'), may hold values from -0.1875 to 0.1875
- ffn_gain: float32 [2048], replicated, may hold values from 0.5 to 1.5
- gate_up_weight: bfloat16 [2048, 2, 5632], P('seq', None, 'head'), may hold values from -0.125 to 0.125
- down_weight: bfloat16 [2048, 5632], P('seq', 'head'), may hold values from -0.078125 to 0.078125
- cotangent: bfloat16 [8192, 2048], P('seq'), may hold values from -6 to 6
Outputs:
- output: bfloat16 [8192, 2048], P('seq')
- grad_tokens: float32 [8192, 2048], P('seq')
- grad_mixer_gain: float32 [2048], replicated
- grad_in_weight: float32 [2048, 16, 768], P('seq', 'head')
- grad_rate_weight: float32 [2048, 2, 16], P('seq', None, 'head')
- grad_conv_weight: float32 [4, 16, 512], P(None, 'head')
- grad_decay_log: float32 [16], P('head')
- grad_decay_bias: float32 [16], P('head')
- grad_out_gain: float32 [256], replicated
- grad_out_weight: float32 [2048, 16, 256], P('seq', 'head')
- grad_ffn_gain: float32 [2048], replicated
- grad_gate_up_weight: float32 [2048, 2, 5632], P('seq', None, 'head')
- grad_down_weight: float32 [2048, 5632], P('seq', 'head')
The draws below stay inside these ranges and needn't reach their ends.
All inputs are finite; a program needn't handle non-finite values.
Results may differ from the reference program's by a relative error of at most 0.035.
Values may be sent and summed in bfloat16 or wider, within the bound.
A program may use at most 256 MiB of HBM per device.

```python
import jax
import jax.numpy as jnp
from jax import lax

D = 2048
HEADS = 16
DK = 128
DV = 256
FF = 5632
CH = 64
KW = 4
TOKENS = 8192
PROJ = 768
CONV = 512


def levels(own_key, dims, shards, low, largest):
    def one(dim, blocks):
        draws = jax.random.uniform(jax.random.fold_in(jax.random.fold_in(own_key, 6), dim), (blocks,), jnp.float32, low / len(shards), largest / len(shards))
        return jnp.repeat(jnp.exp(draws), dims[dim] // blocks).reshape((-1,) + (1,) * (len(dims) - dim - 1))

    level = one(*shards[0])
    for cut in shards[1:]:
        level = level * one(*cut)
    return level


def normal_values(rng, extent, deviation, bound, shards=(), kind=jnp.bfloat16):
    drawn = deviation * jax.random.normal(rng, extent, jnp.float32)
    if shards:
        drawn = drawn * levels(rng, extent, shards, -0.22, 0.18)
    return jnp.clip(drawn, -bound, bound).astype(kind)


def setup_inputs(seed: int = 0) -> dict:
    streams_of = jax.random.split(jax.random.key(seed), 14)
    return {
        "tokens": normal_values(streams_of[0], (TOKENS, D), 1.0, 6.0, ((0, 32),)),
        "mixer_gain": jnp.clip(1.0 + 0.1 * jax.random.normal(streams_of[1], (D,), jnp.float32), 0.5, 1.5),
        "in_weight": normal_values(streams_of[2], (D, HEADS, PROJ), D ** -0.5, 0.125, ((0, 32), (1, 4))),
        "rate_weight": normal_values(streams_of[3], (D, 2, HEADS), D ** -0.5, 0.125, ((0, 32), (2, 4))),
        "conv_weight": normal_values(streams_of[4], (KW, HEADS, CONV), 0.15, 2.0, ((1, 4),), jnp.float32),
        "decay_log": jnp.clip(-9.0 + 6.0 * jax.random.uniform(streams_of[5], (HEADS,), jnp.float32) ** levels(streams_of[5], (HEADS,), ((0, 4),), -0.2, 0.2), -9.0, -3.0),
        "decay_bias": jnp.clip(jax.random.uniform(streams_of[6], (HEADS,), jnp.float32, -1.0, 1.0) * levels(streams_of[6], (HEADS,), ((0, 4),), -0.4, 0.0), -1.0, 1.0),
        "out_gain": jnp.clip(1.0 + 0.1 * jax.random.normal(streams_of[7], (DV,), jnp.float32), 0.5, 1.5),
        "out_weight": normal_values(streams_of[8], (D, HEADS, DV), (HEADS * DV // 4) ** -0.5, 0.1875, ((0, 32), (1, 4))),
        "ffn_gain": jnp.clip(1.0 + 0.1 * jax.random.normal(streams_of[9], (D,), jnp.float32), 0.5, 1.5),
        "gate_up_weight": normal_values(streams_of[10], (D, 2, FF), D ** -0.5, 0.125, ((0, 32), (2, 4))),
        "down_weight": normal_values(streams_of[11], (D, FF), FF ** -0.5, 0.078125, ((0, 32), (1, 4))),
        "cotangent": normal_values(streams_of[12], (TOKENS, D), 1.0, 6.0, ((0, 32),)),
    }


HIGH = lax.Precision.HIGHEST

@jax.custom_vjp
def low(v):
    return lax.optimization_barrier(v.astype(jnp.bfloat16)).astype(jnp.float32)

@jax.custom_vjp
def low_back(v):
    return v

def low_keep(v):
    return (low(v), None)

def low_pass(kept, grad):
    return (grad,)

def back_keep(v):
    return (v, None)

def back_low(kept, grad):
    return (low(grad),)
low.defvjp(low_keep, low_pass)
low_back.defvjp(back_keep, back_low)

def rms(values, gain):
    return values * lax.rsqrt(lax.optimization_barrier(jnp.mean(values * values, axis=-1, keepdims=True)) + 1e-05) * gain

def out_norm(mixer_out, gate_pre, gain):
    return rms(mixer_out, gain) * jax.nn.silu(gate_pre)

def group_rule(state, queries, keys, values, beta, decay):
    size = queries.shape[0]
    gamma = jnp.cumsum(decay, axis=0).T
    rows = lax.broadcasted_iota(jnp.int32, (size, size), 0)
    columns = lax.broadcasted_iota(jnp.int32, (size, size), 1)
    inclusive = (columns <= rows).astype(jnp.float32)
    strict = (columns < rows).astype(jnp.float32)
    spread = gamma[:, :, None] - gamma[:, None, :]
    decays = jnp.exp(spread * inclusive) * inclusive
    head_queries = jnp.transpose(queries, (1, 0, 2))
    head_keys = jnp.transpose(keys, (1, 0, 2))
    head_values = jnp.transpose(values, (1, 0, 2))
    head_beta = beta.T[:, :, None]
    key_products = jnp.einsum('hcd,hed->hce', head_keys, head_keys, precision=HIGH)
    lower = head_beta * decays * strict * key_products
    identity = jnp.eye(size, dtype=jnp.float32)
    growth = jnp.exp(gamma)[:, :, None]
    targets = head_beta * (head_values - growth * jnp.einsum('hcd,hdw->hcw', head_keys, state, precision=HIGH))
    written = jax.scipy.linalg.solve_triangular(lower + identity, targets, lower=True, unit_diagonal=True)
    scores = jnp.einsum('hcd,hed->hce', head_queries, head_keys, precision=HIGH) * decays
    result = growth * jnp.einsum('hcd,hdw->hcw', head_queries, state, precision=HIGH)
    result = result + jnp.einsum('hce,hew->hcw', scores, written, precision=HIGH)
    final = gamma[:, -1]
    weights = jnp.exp(final[:, None] - gamma)[:, :, None]
    new_state = jnp.exp(final)[:, None, None] * state
    new_state = new_state + jnp.einsum('hcd,hcw->hdw', head_keys * weights, written, precision=HIGH)
    return (new_state, jnp.transpose(result, (1, 0, 2)))

def mixer_inputs(padded, rate_pre, conv_weight, decay_log, decay_bias):
    length = padded.shape[0] - (KW - 1)
    mixed = sum((conv_weight[j] * padded[j:j + length] for j in range(KW)))
    active = jax.nn.silu(mixed)
    query_part = active[..., :DK]
    key_part = active[..., DK:2 * DK]
    queries = query_part * lax.rsqrt(lax.optimization_barrier(jnp.sum(query_part * query_part, axis=-1, keepdims=True)) + 1e-06) * DK ** (-0.5)
    keys = key_part * lax.rsqrt(lax.optimization_barrier(jnp.sum(key_part * key_part, axis=-1, keepdims=True)) + 1e-06)
    values = active[..., 2 * DK:]
    beta = jax.nn.sigmoid(rate_pre[:, 1])
    decay = -jnp.exp(decay_log) * jax.nn.softplus(rate_pre[:, 0] + decay_bias)
    return (queries, keys, values, beta, decay)

def delta_rule(queries, keys, values, beta, decay):
    length = queries.shape[0]
    count = length // CH

    def split(array):
        return array.reshape((count, CH) + array.shape[1:])

    def block(state, pieces):
        return group_rule(state, *pieces)
    start = jnp.zeros((HEADS, DK, DV), jnp.float32)
    final, outputs = lax.scan(jax.checkpoint(block), start, (split(queries), split(keys), split(values), split(beta), split(decay)))
    return outputs.reshape((length, HEADS, DV))

def forward(tokens, mixer_gain, in_weight, rate_weight, conv_weight, decay_log, decay_bias, out_gain, out_weight, ffn_gain, gate_up_weight, down_weight):
    normed = low(rms(tokens, mixer_gain))
    projected = low_back(jnp.einsum('td,dhc->thc', normed, in_weight, precision=HIGH))
    rate_pre = low_back(jnp.einsum('td,dgh->tgh', normed, rate_weight, precision=HIGH))
    conv_in = low(projected[..., :CONV])
    gate_pre = projected[..., CONV:]
    padded = jnp.pad(conv_in, ((KW - 1, 0), (0, 0), (0, 0)))
    queries, keys, values, beta, decay = mixer_inputs(padded, rate_pre, conv_weight, decay_log, decay_bias)
    mixer_out = delta_rule(low(queries), low(keys), low(values), beta, decay)
    gated = low(out_norm(mixer_out, gate_pre, out_gain))
    branch = low_back(jnp.einsum('thw,dhw->td', gated, out_weight, precision=HIGH))
    middle = tokens + branch
    second = low(rms(middle, ffn_gain))
    gate_up = low_back(jnp.einsum('td,dgf->tgf', second, gate_up_weight, precision=HIGH))
    hidden = low(jax.nn.silu(gate_up[:, 0]) * gate_up[:, 1])
    return middle + jnp.einsum('tf,df->td', hidden, down_weight, precision=HIGH)

def reference(tokens, mixer_gain, in_weight, rate_weight, conv_weight, decay_log, decay_bias, out_gain, out_weight, ffn_gain, gate_up_weight, down_weight, cotangent):
    inputs = tuple((array.astype(jnp.float32) for array in (tokens, mixer_gain, in_weight, rate_weight, conv_weight, decay_log, decay_bias, out_gain, out_weight, ffn_gain, gate_up_weight, down_weight)))
    result, pullback = jax.vjp(forward, *inputs)
    grads = pullback(cotangent.astype(jnp.float32))
    return (result.astype(jnp.bfloat16), grads[0], grads[1], grads[2], grads[3], grads[4], grads[5], grads[6], grads[7], grads[8], grads[9], grads[10], grads[11])
```

```python
import functools

import jax
import jax.numpy as jnp
from jax import lax
from jax.experimental import pallas as pl
from jax.experimental.pallas import tpu as pltpu
from jax.sharding import PartitionSpec as P

DK = 128
DV = 256
KW = 4
CONV = 512
PROJ = 768
LANES = 128
HALO = 8
HALVES = DV // DK
MESH = pl.DeviceIdType.MESH

F32 = jnp.float32
BF16 = jnp.bfloat16
EXACT = lax.Precision.HIGHEST
FINE = lax.Precision.HIGH
VMEM_LIMIT = 56 * 1024 * 1024


def dot(a, b, dims, precision=None):
    return lax.dot_general(a, b, (dims, ((), ())), precision=precision, preferred_element_type=F32)


def mm(a, b, precision=None):
    return dot(a, b, ((1,), (0,)), precision)


def mmt(a, b, precision=None):
    return dot(a, b, ((1,), (1,)), precision)


def mtm(a, b, precision=None):
    return dot(a, b, ((0,), (0,)), precision)


def iota(shape, dim):
    return lax.broadcasted_iota(jnp.int32, shape, dim)


def softplus(x):
    return jnp.maximum(x, 0.0) + jnp.log1p(jnp.exp(-jnp.abs(x)))


def column(block, index):
    lanes = iota(block.shape, 1)
    return jnp.sum(jnp.where(lanes == index, block, 0.0), axis=1, keepdims=True)


def triangles(size):
    rows, columns = iota((size, size), 0), iota((size, size), 1)
    return rows, columns


def gates(rates, scales, head, heads):
    size = rates.shape[0]
    log_rate = column(scales[0:1], head)
    bias = column(scales[1:2], head)
    pre = column(rates, head) + bias
    beta = jax.nn.sigmoid(column(rates, heads + head))
    decay = -jnp.exp(log_rate) * softplus(pre)
    rows, columns = triangles(size)
    below = (columns <= rows).astype(F32)
    gamma_wide = mm(below, jnp.broadcast_to(decay, (size, LANES)), EXACT)
    gamma = gamma_wide[:, 0:1]
    gamma_row = gamma_wide.T[0:1, :]
    return beta, decay, gamma, gamma_row, pre


def decays_of(gamma, gamma_row):
    size = gamma.shape[0]
    rows, columns = triangles(size)
    inside = columns <= rows
    return jnp.where(inside, jnp.exp(jnp.where(inside, gamma - gamma_row, 0.0)), 0.0)


def inverse(lower):
    size = lower[0].shape[0]
    rows, columns = triangles(size)
    unit = (rows == columns).astype(F32)
    known = [unit - jnp.where(rows // 2 == columns // 2, a, 0.0) for a in lower]
    width = 2
    while width < size:
        fresh = (rows // (2 * width) == columns // (2 * width)) & (rows // width != columns // width)
        parts = [jnp.where(fresh, a, 0.0) for a in lower]
        first = [mm(c, x, FINE) for c, x in zip(parts, known)]
        known = [x - mm(x, y, FINE) for x, y in zip(known, first)]
        width *= 2
    return known


def convolved(extended, taps):
    length = extended.shape[0]
    total = None
    for j in range(KW):
        shift = KW - 1 - j
        moved = extended if shift == 0 else pltpu.roll(extended, shift, 0)
        term = taps[j : j + 1] * moved[HALO:]
        total = term if total is None else total + term
    return total


def unit_rows(values):
    return lax.rsqrt(jnp.sum(values * values, axis=-1, keepdims=True) + 1e-06)


def mixer_inputs(projected, taps):
    extended = projected[:, :CONV].astype(BF16).astype(F32)
    mixed = convolved(extended, taps)
    gate = jax.nn.sigmoid(mixed)
    active = mixed * gate
    q_raw, k_raw = active[:, :DK], active[:, DK : 2 * DK]
    q_scale, k_scale = unit_rows(q_raw), unit_rows(k_raw)
    queries = (q_raw * q_scale * DK ** (-0.5)).astype(BF16)
    keys = (k_raw * k_scale).astype(BF16)
    values = active[:, 2 * DK :].astype(BF16)
    return extended, mixed, gate, (q_raw, q_scale), (k_raw, k_scale), queries, keys, values


def local_forward(heads, proj_ref, taps_ref, scales_ref, q_ref, k_ref, v_ref, inv_ref, out_ref, map_ref, sum_ref):
    size = proj_ref.shape[0] - HALO
    rows, columns = triangles(size)
    rates = proj_ref[HALO:, heads * PROJ :]
    scales = scales_ref[...]
    lower, kept = [], []
    for h in range(heads):
        projected = proj_ref[:, h * PROJ : h * PROJ + CONV]
        taps = taps_ref[:, h * CONV : (h + 1) * CONV]
        *_, queries, keys, values = mixer_inputs(projected, taps)
        q_ref[h], k_ref[h], v_ref[h] = queries, keys, values
        beta, decay, gamma, gamma_row, _ = gates(rates, scales, h, heads)
        spread = decays_of(gamma, gamma_row)
        lower.append(jnp.where(columns < rows, beta * spread * mmt(keys, keys), 0.0))
        kept.append((queries, keys, values, beta, gamma, spread))
    inverses = inverse(lower)
    for h in range(heads):
        queries, keys, values, beta, gamma, spread = kept[h]
        inv_ref[h] = inverses[h]
        growth = jnp.exp(gamma)
        targets = jnp.concatenate([growth * beta * keys.astype(F32), beta * values.astype(F32)], axis=1)
        written = mm(inverses[h], targets, FINE)
        scores = spread * mmt(queries, keys)
        through = mm(scores, written, FINE)
        map_ref[h] = growth * queries.astype(F32) - through[:, :DK]
        out_ref[h] = through[:, DK:]
        final = gamma[size - 1 : size]
        faded = jnp.exp(final - gamma) * keys.astype(F32)
        summary = mtm(faded, written, FINE)
        unit = (iota((DK, DK), 0) == iota((DK, DK), 1)).astype(F32)
        passed = (jnp.exp(final) * unit - summary[:, :DK]).astype(BF16)
        for half in range(HALVES):
            sum_ref[HALVES * h + half, :, :DK] = passed
            sum_ref[HALVES * h + half, :, DK:] = summary[:, (half + 1) * DK : (half + 2) * DK].astype(BF16)


def whole_state(units_ref, head):
    return jnp.concatenate([units_ref[HALVES * head + half] for half in range(HALVES)], axis=1).astype(F32)


def mix_outputs(heads, out_ref, map_ref, state_ref, proj_ref, gain_ref, mixed_ref, gated_ref):
    gain = gain_ref[...]
    for h in range(heads):
        mixer_out = out_ref[h] + mm(map_ref[h], whole_state(state_ref, h), FINE)
        mixed_ref[h] = mixer_out
        gate = proj_ref[HALO:, h * PROJ + CONV : (h + 1) * PROJ]
        scale = lax.rsqrt(jnp.mean(mixer_out * mixer_out, axis=-1, keepdims=True) + 1e-05)
        gated = mixer_out * scale * gain * (gate * jax.nn.sigmoid(gate))
        gated_ref[:, h * DV : (h + 1) * DV] = gated.astype(BF16)


def mix_outputs_back(heads, grad_ref, mixed_ref, map_ref, proj_ref, gain_ref, grad_mixed_ref, grad_gate_ref, grad_gain_ref, carried_ref):
    gain = gain_ref[...]
    total = jnp.zeros_like(gain)
    for h in range(heads):
        grad = grad_ref[:, h * DV : (h + 1) * DV]
        mixer_out = mixed_ref[h]
        z = proj_ref[HALO:, h * PROJ + CONV : (h + 1) * PROJ]
        scale = lax.rsqrt(jnp.mean(mixer_out * mixer_out, axis=-1, keepdims=True) + 1e-05)
        normal = mixer_out * scale
        s = jax.nn.sigmoid(z)
        silu = z * s
        total = total + jnp.sum(grad * normal * silu, axis=0, keepdims=True)
        grad_gate_ref[:, h * DV : (h + 1) * DV] = (grad * normal * gain * s * (1.0 + z * (1.0 - s))).astype(BF16)
        u = grad * gain * silu
        grad_mixed = scale * u - normal * (scale * jnp.mean(u * normal, axis=-1, keepdims=True))
        grad_mixed_ref[h] = grad_mixed
        carried = mtm(map_ref[h], grad_mixed, FINE).astype(BF16)
        for half in range(HALVES):
            carried_ref[HALVES * h + half] = carried[:, half * DK : (half + 1) * DK]
    grad_gain_ref[...] = total


def norm_back(grad, values, scale):
    return scale * grad - values * (scale * scale * scale * jnp.sum(values * grad, axis=-1, keepdims=True))


def local_backward(
    heads, proj_ref, taps_ref, scales_ref, q_ref, k_ref, v_ref, inv_ref, grad_ref, state_ref, leaving_ref, gate_ref,
    out_ref, halo_ref, tail_ref, taps_out_ref, scales_out_ref,
):
    size = proj_ref.shape[0] - HALO
    rows, columns = triangles(size)
    rates = proj_ref[HALO:, heads * PROJ :]
    scales = scales_ref[...]
    lanes = iota((size, LANES), 1)
    grad_rates = jnp.zeros((size, LANES), F32)
    rates_total = jnp.zeros((8, LANES), F32)
    row8, lane8 = iota((8, LANES), 0), iota((8, LANES), 1)
    ones = jnp.ones((size, LANES), F32)
    above = (columns >= rows).astype(F32)
    for h in range(heads):
        queries, keys, values = q_ref[h], k_ref[h], v_ref[h]
        qf, kf, vf = queries.astype(F32), keys.astype(F32), values.astype(F32)
        beta, decay, gamma, gamma_row, pre = gates(rates, scales, h, heads)
        spread = decays_of(gamma, gamma_row)
        strict = columns < rows
        growth = jnp.exp(gamma)
        final = gamma[size - 1 : size]
        fade = jnp.exp(final - gamma)
        state, leaving = whole_state(state_ref, h), whole_state(leaving_ref, h)
        inv, grad = inv_ref[h], grad_ref[h]
        products = mmt(keys, keys)
        scores = spread * mmt(queries, keys)
        lower = jnp.where(strict, beta * spread * products, 0.0)
        residual = vf - growth * mm(kf, state, FINE)
        written = mm(inv, beta * residual, FINE)
        faded = fade * kf
        grad_written = mtm(scores, grad, FINE) + mm(faded, leaving, FINE)
        grad_scores = mmt(grad, written, FINE)
        grad_targets = mtm(inv, grad_written, FINE)
        grad_lower = jnp.where(strict, -mmt(grad_targets, written, FINE), 0.0)
        grad_values = beta * grad_targets
        grad_beta = jnp.sum(grad_targets * residual, axis=-1, keepdims=True)
        grad_beta = grad_beta + jnp.sum(grad_lower * spread * products, axis=-1, keepdims=True)
        q_first = growth * mmt(grad, state, FINE)
        k_first = -growth * mmt(grad_values, state, FINE)
        spread_scores = spread * grad_scores
        spread_lower = grad_lower * beta * spread
        grad_faded = mmt(written, leaving, FINE)
        grad_queries = q_first + mm(spread_scores, kf, FINE)
        grad_keys = (
            k_first
            + mtm(spread_scores, qf, FINE)
            + mm(spread_lower, kf, FINE)
            + mtm(spread_lower, kf, FINE)
            + fade * grad_faded
        )
        energy = grad_scores * scores + grad_lower * lower
        fading = jnp.sum(grad_faded * faded, axis=-1, keepdims=True)
        grad_gamma = jnp.sum(qf * q_first + kf * k_first, axis=-1, keepdims=True) - fading
        grad_gamma = grad_gamma + jnp.sum(energy, axis=-1, keepdims=True)
        at_end = jnp.sum(fading, axis=0, keepdims=True) + jnp.exp(final) * jnp.sum(
            jnp.sum(state * leaving, axis=1, keepdims=True), axis=0, keepdims=True
        )
        grad_gamma = grad_gamma + jnp.where(iota((size, 1), 0) == size - 1, at_end, 0.0)
        wide = jnp.broadcast_to(grad_gamma, (size, LANES)) - mtm(energy, ones, EXACT)
        grad_decay = mm(above, wide, EXACT)[:, 0:1]

        projected = proj_ref[:, h * PROJ : h * PROJ + CONV]
        taps = taps_ref[:, h * CONV : (h + 1) * CONV]
        extended, mixed, gate, (q_raw, q_scale), (k_raw, k_scale), *_ = mixer_inputs(projected, taps)
        grad_active = jnp.concatenate(
            [
                norm_back(grad_queries * DK ** (-0.5), q_raw, q_scale),
                norm_back(grad_keys, k_raw, k_scale),
                grad_values,
            ],
            axis=1,
        )
        grad_mixed = grad_active * gate * (1.0 + mixed * (1.0 - gate))
        padding = jnp.zeros((HALO, CONV), F32)
        full = jnp.concatenate([padding, grad_mixed, padding], axis=0)
        total = None
        for j in range(KW):
            shift = KW - 1 - j
            moved = full if shift == 0 else pltpu.roll(full, size + 2 * HALO - shift, 0)
            term = taps[j : j + 1] * moved[: size + HALO]
            total = term if total is None else total + term
            back = extended if shift == 0 else pltpu.roll(extended, shift, 0)
            taps_out_ref[j : j + 1, h * CONV : (h + 1) * CONV] = jnp.sum(
                grad_mixed * back[HALO:], axis=0, keepdims=True
            )
        halo_ref[:, h * CONV : (h + 1) * CONV] = total[:HALO]
        tail_ref[:, h * CONV : (h + 1) * CONV] = total[size:]
        out_ref[:, h * PROJ : h * PROJ + CONV] = total[HALO:].astype(BF16)
        out_ref[:, h * PROJ + CONV : (h + 1) * PROJ] = gate_ref[:, h * DV : (h + 1) * DV]

        grad_pre = -jnp.exp(column(scales[0:1], h)) * jax.nn.sigmoid(pre) * grad_decay
        grad_strength = grad_beta * beta * (1.0 - beta)
        grad_rates = grad_rates + jnp.where(lanes == h, grad_pre, 0.0)
        grad_rates = grad_rates + jnp.where(lanes == heads + h, grad_strength, 0.0)
        log_total = jnp.sum(grad_decay * decay, axis=0, keepdims=True)
        bias_total = jnp.sum(grad_pre, axis=0, keepdims=True)
        rates_total = rates_total + jnp.where((row8 == 0) & (lane8 == h), log_total, 0.0)
        rates_total = rates_total + jnp.where((row8 == 1) & (lane8 == h), bias_total, 0.0)
    out_ref[:, heads * PROJ :] = grad_rates.astype(BF16)
    scales_out_ref[...] = rates_total


def start_barrier(peers):
    barrier = pltpu.get_barrier_semaphore()
    for peer in peers:
        pl.semaphore_signal(barrier, inc=1, device_id=peer, device_id_type=MESH)
    pl.semaphore_wait(barrier, len(peers))


def send(source, target, sends, receives, slot, peer):
    copy = pltpu.make_async_remote_copy(
        src_ref=source,
        dst_ref=target,
        send_sem=sends.at[slot],
        recv_sem=receives.at[slot],
        device_id=peer,
        device_id_type=MESH,
    )
    copy.start()
    return copy


def twice(left, right):
    high = right.astype(BF16)
    low = (right - high.astype(F32)).astype(BF16)
    return mm(left, high) + mm(left, low)


def scan_places(members, groups):
    seq, head = lax.axis_index("seq"), lax.axis_index("head")
    member, group = seq % members, seq // members
    near = [(member + d) % members for d in range(members)]
    far = [(group + d) % groups for d in range(groups)]
    near_ids = [(group * members + place, head) for place in near]
    far_ids = [(place * members + member, head) for place in far]
    return member, group, near, near_ids, far_ids


def scan_forward(
    groups, pack_ref, out_ref, kept_ref, totals_ref, near_in, before, far_out, far_in, back_out, back_in,
    near_s, near_r, far_s, far_r, back_s, back_r,
):
    members = pack_ref.shape[0]
    member, group, near, near_ids, far_ids = scan_places(members, groups)
    start_barrier(near_ids[1:] + far_ids[1:])
    copies = [
        send(pack_ref.at[near[d]], near_in.at[member], near_s, near_r, d, near_ids[d]) for d in range(1, members)
    ]
    near_in[member] = pack_ref[member]
    for copy in copies:
        copy.wait()
    unit = (iota((DK, DK), 0) == iota((DK, DK), 1)).astype(F32)
    total = jnp.concatenate([unit, jnp.zeros((DK, DK), F32)], axis=1)
    for j in range(members):
        before[j] = total
        kept_ref[j] = near_in[j, :, :DK]
        moved = twice(near_in[j, :, :DK], total)
        total = jnp.concatenate([moved[:, :DK], moved[:, DK:] + near_in[j, :, DK:].astype(F32)], axis=1)
    far_out[...] = total.astype(BF16)
    copies = [send(far_out, far_in.at[group], far_s, far_r, d, far_ids[d]) for d in range(1, groups)]
    far_in[group] = far_out[...]
    for copy in copies:
        copy.wait()
    state = jnp.zeros((DK, DK), F32)
    for j in range(groups):
        totals_ref[j] = far_in[j, :, :DK]
        fresh = twice(far_in[j, :, :DK], state) + far_in[j, :, DK:].astype(F32)
        state = jnp.where(j < group, fresh, state)
    for j in range(members):
        back_out[j] = (mm(before[j, :, :DK], state, FINE) + before[j, :, DK:]).astype(BF16)
    copies = [
        send(back_out.at[near[d]], back_in.at[member], back_s, back_r, d, near_ids[d]) for d in range(1, members)
    ]
    back_in[member] = back_out[member]
    for copy in copies:
        copy.wait()
    out_ref[...] = back_in[...]


def scan_backward(
    groups, pack_ref, kept_ref, totals_ref, out_ref, near_in, turned, before, after, far_out, far_in, back_out, back_in,
    near_s, near_r, far_s, far_r, back_s, back_r,
):
    members = pack_ref.shape[0]
    member, group, near, near_ids, far_ids = scan_places(members, groups)
    start_barrier(near_ids[1:] + far_ids[1:])
    copies = [
        send(pack_ref.at[near[d]], near_in.at[member], near_s, near_r, d, near_ids[d]) for d in range(1, members)
    ]
    near_in[member] = pack_ref[member]
    passed = (iota((DK, DK), 0) == iota((DK, DK), 1)).astype(F32)
    for j in reversed(range(members)):
        turned[j] = kept_ref[j].astype(F32).T.astype(BF16)
        before[j] = passed
        passed = twice(turned[j], passed)
    for copy in copies:
        copy.wait()
    total = jnp.zeros((DK, DK), F32)
    for j in reversed(range(members)):
        after[j] = total
        total = twice(turned[j], total) + near_in[j].astype(F32)
    far_out[...] = total.astype(BF16)
    copies = [send(far_out, far_in.at[group], far_s, far_r, d, far_ids[d]) for d in range(1, groups)]
    far_in[group] = far_out[...]
    turned_totals = [totals_ref[j].astype(F32).T.astype(BF16) for j in range(groups)]
    for copy in copies:
        copy.wait()
    state = jnp.zeros((DK, DK), F32)
    for j in reversed(range(groups)):
        fresh = twice(turned_totals[j], state) + far_in[j].astype(F32)
        state = jnp.where(j > group, fresh, state)
    for j in range(members):
        back_out[j] = (mm(before[j], state, FINE) + after[j]).astype(BF16)
    copies = [
        send(back_out.at[near[d]], back_in.at[member], back_s, back_r, d, near_ids[d]) for d in range(1, members)
    ]
    back_in[member] = back_out[member]
    for copy in copies:
        copy.wait()
    out_ref[...] = back_in[...]


def ring_places(axis):
    seq, head = lax.axis_index("seq"), lax.axis_index("head")
    size = lax.axis_size(axis)
    me = lax.axis_index(axis)
    places = [(me + d) % size for d in range(size)]
    return me, places, [(seq, place) for place in places]


def start_reduce(part_ref, recv, sends, receives, places, ids, rows):
    return [
        send(part_ref.at[pl.ds(pl.multiple_of(places[d] * rows, rows), rows)], recv.at[d - 1], sends, receives, d - 1, ids[d])
        for d in range(1, len(places))
    ]


def end_reduce(copies, part_ref, recv, me, rows):
    for copy in copies:
        copy.wait()
    total = part_ref[pl.ds(pl.multiple_of(me * rows, rows), rows)].astype(F32)
    for d in range(len(copies)):
        total = total + recv[d].astype(F32)
    return total


def start_gather(full_ref, sends, receives, me, ids, rows):
    mine = full_ref.at[pl.ds(pl.multiple_of(me * rows, rows), rows)]
    return [send(mine, mine, sends, receives, d - 1, ids[d]) for d in range(1, len(ids))]


def rms_scale(values):
    return lax.rsqrt(jnp.mean(values * values, axis=-1, keepdims=True) + 1e-05)


def rms_back(grad, values, gain):
    scale = rms_scale(values)
    u = grad * gain
    back = scale * u - values * (scale * scale * scale * jnp.mean(u * values, axis=-1, keepdims=True))
    return back, jnp.sum(grad * values * scale, axis=0, keepdims=True)


def middle_kernel(part_ref, tokens_ref, gain_ref, second_ref, middle_ref, recv, red_s, red_r, gat_s, gat_r):
    me, places, ids = ring_places("head")
    rows = middle_ref.shape[0]
    mine = pl.ds(pl.multiple_of(me * rows, rows), rows)
    start_barrier(ids[1:])
    copies = start_reduce(part_ref, recv, red_s, red_r, places, ids, rows)
    middle = tokens_ref[mine].astype(F32) + end_reduce(copies, part_ref, recv, me, rows)
    second_ref[mine] = (middle * rms_scale(middle) * gain_ref[...]).astype(BF16)
    copies = start_gather(second_ref, gat_s, gat_r, me, ids, rows)
    middle_ref[...] = middle
    for copy in copies:
        copy.wait()


def middle_back_kernel(
    part_ref, middle_ref, cotangent_ref, gain_ref, branch_ref, grad_ref, grad_gain_ref, recv, red_s, red_r, gat_s, gat_r
):
    me, places, ids = ring_places("head")
    rows = middle_ref.shape[0]
    mine = pl.ds(pl.multiple_of(me * rows, rows), rows)
    start_barrier(ids[1:])
    copies = start_reduce(part_ref, recv, red_s, red_r, places, ids, rows)
    grad_second = end_reduce(copies, part_ref, recv, me, rows)
    back, grad_gain = rms_back(grad_second, middle_ref[...], gain_ref[...])
    grad = cotangent_ref[mine].astype(F32) + back
    branch_ref[mine] = grad.astype(BF16)
    copies = start_gather(branch_ref, gat_s, gat_r, me, ids, rows)
    grad_ref[...] = grad
    grad_gain_ref[...] = grad_gain
    for copy in copies:
        copy.wait()


def tokens_back_kernel(
    normed_part_ref, ffn_part_ref, tokens_ref, middle_ref, grad_ref, gain_ref, output_ref, grad_tokens_ref, grad_gain_ref,
    low_ref, recv, recv_2, red_s, red_r, gat_s, gat_r, red_s2, red_r2, gat_s2, gat_r2,
):
    me, places, ids = ring_places("head")
    rows = middle_ref.shape[0]
    mine = pl.ds(pl.multiple_of(me * rows, rows), rows)
    start_barrier(ids[1:])
    copies = start_reduce(normed_part_ref, recv, red_s, red_r, places, ids, rows)
    copies_2 = start_reduce(ffn_part_ref, recv_2, red_s2, red_r2, places, ids, rows)
    grad_normed = end_reduce(copies, normed_part_ref, recv, me, rows)
    back, grad_gain = rms_back(grad_normed, tokens_ref[mine].astype(F32), gain_ref[...])
    low_ref[mine] = (grad_ref[...] + back).astype(BF16)
    copies = start_gather(low_ref, gat_s, gat_r, me, ids, rows)
    grad_gain_ref[...] = grad_gain
    output_ref[mine] = (middle_ref[...] + end_reduce(copies_2, ffn_part_ref, recv_2, me, rows)).astype(BF16)
    copies_2 = start_gather(output_ref, gat_s2, gat_r2, me, ids, rows)
    for copy in copies:
        copy.wait()
    grad_tokens_ref[...] = low_ref[...].astype(F32)
    for copy in copies_2:
        copy.wait()


def call(kernel, outs, *args, name):
    return pl.pallas_call(
        kernel,
        out_shape=[jax.ShapeDtypeStruct(shape, kind) for shape, kind in outs],
        compiler_params=pltpu.CompilerParams(vmem_limit_bytes=VMEM_LIMIT),
        name=name,
    )(*args)


def remote_call(kernel, outs, scratch, identity, *args, name):
    return pl.pallas_call(
        kernel,
        in_specs=[pl.BlockSpec(memory_space=pltpu.VMEM)] * len(args),
        out_specs=[pl.BlockSpec(memory_space=pltpu.VMEM)] * len(outs),
        out_shape=[jax.ShapeDtypeStruct(shape, kind) for shape, kind in outs],
        scratch_shapes=scratch,
        compiler_params=pltpu.CompilerParams(
            vmem_limit_bytes=VMEM_LIMIT, collective_id=identity, has_side_effects=True
        ),
        name=name,
    )(*args)


def pairs(*sizes):
    return [pltpu.SemaphoreType.DMA((size,)) for size in sizes for _ in range(2)]


def shifted(block, axis, distance):
    devices = range(lax.axis_size(axis))
    route = [(i - distance, i) for i in devices if i - distance in devices]
    return lax.ppermute(block, axis, route)


def per_device(
    tokens,
    mixer_gain,
    in_weight,
    rate_weight,
    conv_weight,
    decay_log,
    decay_bias,
    out_gain,
    out_weight,
    ffn_gain,
    gate_up_weight,
    down_weight,
    cotangent,
):
    count, width = tokens.shape
    heads = in_weight.shape[1]
    hidden_units = down_weight.shape[1]
    slab = in_weight.shape[0]
    projections = heads * PROJ + LANES
    units = heads * HALVES
    peers, sharers = lax.axis_size("seq"), lax.axis_size("head")
    groups = peers // units
    rows = count // sharers

    first = jnp.concatenate(
        [
            in_weight.reshape(slab, heads * PROJ),
            rate_weight.reshape(slab, 2 * heads),
            jnp.zeros((slab, LANES - 2 * heads), BF16),
        ],
        axis=1,
    )
    rest = jnp.concatenate(
        [out_weight.reshape(slab, heads * DV), gate_up_weight.reshape(slab, 2 * hidden_units), down_weight], axis=1
    )
    first_full = lax.all_gather(first, "seq", axis=0, tiled=True)
    rest_full = lax.all_gather(rest, "seq", axis=0, tiled=True)
    out_full = rest_full[:, : heads * DV]
    gate_up_full = rest_full[:, heads * DV : heads * DV + 2 * hidden_units]
    down_full = rest_full[:, heads * DV + 2 * hidden_units :]

    behind = shifted(tokens[count - HALO :], "seq", 1)
    source = jnp.concatenate([behind, tokens], axis=0).astype(F32)
    normed_long = (source * rms_scale(source) * mixer_gain).astype(BF16)
    normed = normed_long[HALO:]
    projected = mm(normed_long, first_full)

    taps = conv_weight.reshape(KW, heads * CONV)
    scales = jnp.pad(jnp.stack([decay_log, decay_bias]), ((0, 6), (0, LANES - heads)))
    queries, keys, values, inv, out_local, out_map, summary = call(
        functools.partial(local_forward, heads),
        [
            ((heads, count, DK), BF16),
            ((heads, count, DK), BF16),
            ((heads, count, DV), BF16),
            ((heads, count, count), F32),
            ((heads, count, DV), F32),
            ((heads, count, DK), F32),
            ((units, DK, 2 * DK), BF16),
        ],
        projected,
        taps,
        scales,
        name="local_forward",
    )
    block = (DK, DK)
    double = (DK, 2 * DK)
    entering, kept, totals = remote_call(
        functools.partial(scan_forward, groups),
        [((units, *block), BF16), ((units, *block), BF16), ((groups, *block), BF16)],
        [
            pltpu.VMEM((units, *double), BF16),
            pltpu.VMEM((units, *double), F32),
            pltpu.VMEM(double, BF16),
            pltpu.VMEM((groups, *double), BF16),
            pltpu.VMEM((units, *block), BF16),
            pltpu.VMEM((units, *block), BF16),
            *pairs(units, groups, units),
        ],
        1,
        summary,
        name="scan_forward",
    )
    gain_row = out_gain.reshape(1, DV)
    mixer_out, gated = call(
        functools.partial(mix_outputs, heads),
        [((heads, count, DV), F32), ((count, heads * DV), BF16)],
        out_local,
        out_map,
        entering,
        projected,
        gain_row,
        name="mix_outputs",
    )
    branch = mmt(gated, out_full)
    ring = [pltpu.VMEM((sharers - 1, rows, width), BF16)]
    second, middle = remote_call(
        middle_kernel,
        [((count, width), BF16), ((rows, width), F32)],
        ring + pairs(sharers - 1, sharers - 1),
        2,
        branch.astype(BF16),
        tokens,
        ffn_gain.reshape(1, width),
        name="middle",
    )
    gate_up = mm(second, gate_up_full)
    z, up = gate_up[:, :hidden_units], gate_up[:, hidden_units:]
    s = jax.nn.sigmoid(z)
    hidden = (z * s * up).astype(BF16)
    ffn_part = mmt(hidden, down_full)
    grad_hidden = mm(cotangent, down_full)
    grad_gate_up = jnp.concatenate([grad_hidden * up * s * (1.0 + z * (1.0 - s)), grad_hidden * z * s], axis=1).astype(
        BF16
    )
    second_part = mmt(grad_gate_up, gate_up_full)
    grad_branch, grad_middle, grad_ffn_gain = remote_call(
        middle_back_kernel,
        [((count, width), BF16), ((rows, width), F32), ((1, width), F32)],
        ring + pairs(sharers - 1, sharers - 1),
        3,
        second_part.astype(BF16),
        middle,
        cotangent,
        ffn_gain.reshape(1, width),
        name="middle_back",
    )
    grad_gated = mm(grad_branch, out_full)
    grad_mixed, grad_gate, grad_out_gain, carried = call(
        functools.partial(mix_outputs_back, heads),
        [
            ((heads, count, DV), F32),
            ((count, heads * DV), BF16),
            ((1, DV), F32),
            ((units, DK, DK), BF16),
        ],
        grad_gated,
        mixer_out,
        out_map,
        projected,
        gain_row,
        name="mix_outputs_back",
    )
    leaving = remote_call(
        functools.partial(scan_backward, groups),
        [((units, *block), BF16)],
        [
            pltpu.VMEM((units, *block), BF16),
            pltpu.VMEM((units, *block), BF16),
            pltpu.VMEM((units, *block), F32),
            pltpu.VMEM((units, *block), F32),
            pltpu.VMEM(block, BF16),
            pltpu.VMEM((groups, *block), BF16),
            pltpu.VMEM((units, *block), BF16),
            pltpu.VMEM((units, *block), BF16),
            *pairs(units, groups, units),
        ],
        4,
        carried,
        kept,
        totals,
        name="scan_backward",
    )[0]
    grad_projected, halo, tail, grad_taps, grad_scales = call(
        functools.partial(local_backward, heads),
        [
            ((count, projections), BF16),
            ((HALO, heads * CONV), F32),
            ((HALO, heads * CONV), F32),
            ((KW, heads * CONV), F32),
            ((8, LANES), F32),
        ],
        projected,
        taps,
        scales,
        queries,
        keys,
        values,
        inv,
        grad_mixed,
        entering,
        leaving,
        grad_gate,
        name="local_backward",
    )
    tail = (tail + shifted(halo, "seq", -1)).astype(BF16)
    for h in range(heads):
        grad_projected = lax.dynamic_update_slice(
            grad_projected, tail[:, h * CONV : (h + 1) * CONV], (count - HALO, h * PROJ)
        )
    normed_part = mmt(grad_projected, first_full)
    output, grad_tokens, grad_mixer_gain = remote_call(
        tokens_back_kernel,
        [((count, width), BF16), ((count, width), F32), ((1, width), F32)],
        [pltpu.VMEM((count, width), BF16)] + ring + ring + pairs(*[sharers - 1] * 4),
        5,
        normed_part.astype(BF16),
        ffn_part.astype(BF16),
        tokens,
        middle,
        grad_middle,
        mixer_gain.reshape(1, width),
        name="tokens_back",
    )
    grad_rest = jnp.concatenate(
        [
            mtm(grad_branch, gated).astype(BF16),
            mtm(second, grad_gate_up).astype(BF16),
            mtm(cotangent, hidden).astype(BF16),
        ],
        axis=1,
    )
    grad_first = mtm(normed, grad_projected).astype(BF16)
    grad_rest = lax.psum_scatter(grad_rest, "seq", scatter_dimension=0, tiled=True).astype(F32)
    grad_first = lax.psum_scatter(grad_first, "seq", scatter_dimension=0, tiled=True).astype(F32)
    gains = jnp.concatenate([grad_mixer_gain[0], grad_ffn_gain[0], grad_out_gain[0]])
    gains = lax.psum(gains, ("seq", "head"))
    small = jnp.concatenate([grad_taps.reshape(-1), grad_scales[0, :heads], grad_scales[1, :heads]])
    small = lax.psum(small, "seq")
    at_taps = KW * heads * CONV
    rates_at = heads * PROJ
    gate_at = heads * DV
    down_at = gate_at + 2 * hidden_units
    return (
        output,
        grad_tokens,
        gains[:width],
        grad_first[:, :rates_at].reshape(slab, heads, PROJ),
        grad_first[:, rates_at : rates_at + 2 * heads].reshape(slab, 2, heads),
        small[:at_taps].reshape(KW, heads, CONV),
        small[at_taps : at_taps + heads],
        small[at_taps + heads :],
        gains[2 * width :],
        grad_rest[:, :gate_at].reshape(slab, heads, DV),
        gains[width : 2 * width],
        grad_rest[:, gate_at:down_at].reshape(slab, 2, hidden_units),
        grad_rest[:, down_at:],
    )


def solution(mesh):
    in_specs = (
        P("seq", None),
        P(),
        P("seq", "head", None),
        P("seq", None, "head"),
        P(None, "head", None),
        P("head"),
        P("head"),
        P(),
        P("seq", "head", None),
        P(),
        P("seq", None, "head"),
        P("seq", "head"),
        P("seq", None),
    )
    out_specs = (
        P("seq", None),
        P("seq", None),
        P(),
        P("seq", "head", None),
        P("seq", None, "head"),
        P(None, "head", None),
        P("head"),
        P("head"),
        P(),
        P("seq", "head", None),
        P(),
        P("seq", None, "head"),
        P("seq", "head"),
    )
    return jax.shard_map(
        per_device, mesh=mesh, in_specs=in_specs, out_specs=out_specs, check_vma=False
    )
```

```python
import functools

import jax
import jax.numpy as jnp
from jax import lax
from jax.experimental import pallas as pl
from jax.experimental.pallas import tpu as pltpu
from jax.sharding import PartitionSpec as P

DK = 128
DV = 256
KW = 4
CONV = 512
PROJ = 768
LANES = 128
HALO = 8
HALVES = DV // DK
MESH = pl.DeviceIdType.MESH

F32 = jnp.float32
BF16 = jnp.bfloat16
EXACT = lax.Precision.HIGHEST
FINE = lax.Precision.HIGH
VMEM_LIMIT = 56 * 1024 * 1024


def dot(a, b, dims, precision=None):
    return lax.dot_general(a, b, (dims, ((), ())), precision=precision, preferred_element_type=F32)


def mm(a, b, precision=None):
    return dot(a, b, ((1,), (0,)), precision)


def mmt(a, b, precision=None):
    return dot(a, b, ((1,), (1,)), precision)


def mtm(a, b, precision=None):
    return dot(a, b, ((0,), (0,)), precision)


def iota(shape, dim):
    return lax.broadcasted_iota(jnp.int32, shape, dim)


def softplus(x):
    return jnp.maximum(x, 0.0) + jnp.log1p(jnp.exp(-jnp.abs(x)))


def split_by_core(values, slab):
    width = values.shape[1]
    lanes = iota((values.shape[0], 2 * slab), 1)
    firsts, seconds = [], []
    for at in range(0, width, 4 * slab):
        a, b = values[:, at : at + 2 * slab], values[:, at + 2 * slab : at + 4 * slab]
        firsts.append(jnp.where(lanes < slab, a, pltpu.roll(b, slab, 1)))
        seconds.append(jnp.where(lanes < slab, pltpu.roll(a, slab, 1), b))
    return jnp.concatenate(firsts + seconds, axis=1)


def column(block, index):
    lanes = iota(block.shape, 1)
    return jnp.sum(jnp.where(lanes == index, block, 0.0), axis=1, keepdims=True)


def triangles(size):
    rows, columns = iota((size, size), 0), iota((size, size), 1)
    return rows, columns


def gates(rates, scales, head, heads):
    size = rates.shape[0]
    log_rate = column(scales[0:1], head)
    bias = column(scales[1:2], head)
    pre = column(rates, head) + bias
    beta = jax.nn.sigmoid(column(rates, heads + head))
    decay = -jnp.exp(log_rate) * softplus(pre)
    rows, columns = triangles(size)
    below = (columns <= rows).astype(F32)
    gamma_wide = mm(below, jnp.broadcast_to(decay, (size, LANES)), EXACT)
    gamma = gamma_wide[:, 0:1]
    gamma_row = gamma_wide.T[0:1, :]
    return beta, decay, gamma, gamma_row, pre


def decays_of(gamma, gamma_row):
    size = gamma.shape[0]
    rows, columns = triangles(size)
    inside = columns <= rows
    return jnp.where(inside, jnp.exp(jnp.where(inside, gamma - gamma_row, 0.0)), 0.0)


def inverse(lower):
    size = lower[0].shape[0]
    rows, columns = triangles(size)
    unit = (rows == columns).astype(F32)
    known = [unit - jnp.where(rows // 2 == columns // 2, a, 0.0) for a in lower]
    width = 2
    while width < size:
        fresh = (rows // (2 * width) == columns // (2 * width)) & (rows // width != columns // width)
        parts = [jnp.where(fresh, a, 0.0) for a in lower]
        first = [mm(c, x, FINE) for c, x in zip(parts, known)]
        known = [x - mm(x, y, FINE) for x, y in zip(known, first)]
        width *= 2
    return known


def convolved(extended, taps):
    length = extended.shape[0]
    total = None
    for j in range(KW):
        shift = KW - 1 - j
        moved = extended if shift == 0 else pltpu.roll(extended, shift, 0)
        term = taps[j : j + 1] * moved[HALO:]
        total = term if total is None else total + term
    return total


def unit_rows(values):
    return lax.rsqrt(jnp.sum(values * values, axis=-1, keepdims=True) + 1e-06)


def mixer_inputs(projected, taps):
    extended = projected[:, :CONV].astype(BF16).astype(F32)
    mixed = convolved(extended, taps)
    gate = jax.nn.sigmoid(mixed)
    active = mixed * gate
    q_raw, k_raw = active[:, :DK], active[:, DK : 2 * DK]
    q_scale, k_scale = unit_rows(q_raw), unit_rows(k_raw)
    queries = (q_raw * q_scale * DK ** (-0.5)).astype(BF16)
    keys = (k_raw * k_scale).astype(BF16)
    values = active[:, 2 * DK :].astype(BF16)
    return extended, mixed, gate, (q_raw, q_scale), (k_raw, k_scale), queries, keys, values


def local_forward(
    heads, slab, proj_ref, taps_ref, scales_ref, normed_ref, q_ref, k_ref, v_ref, inv_ref, out_ref, map_ref, sum_ref, split_ref
):
    size = proj_ref.shape[0] - HALO
    split_ref[...] = split_by_core(normed_ref[HALO:].astype(F32), slab).astype(BF16)
    rows, columns = triangles(size)
    rates = proj_ref[HALO:, heads * PROJ :]
    scales = scales_ref[...]
    lower, kept = [], []
    for h in range(heads):
        projected = proj_ref[:, h * PROJ : h * PROJ + CONV]
        taps = taps_ref[:, h * CONV : (h + 1) * CONV]
        *_, queries, keys, values = mixer_inputs(projected, taps)
        q_ref[h], k_ref[h], v_ref[h] = queries, keys, values
        beta, decay, gamma, gamma_row, _ = gates(rates, scales, h, heads)
        spread = decays_of(gamma, gamma_row)
        lower.append(jnp.where(columns < rows, beta * spread * mmt(keys, keys), 0.0))
        kept.append((queries, keys, values, beta, gamma, spread))
    inverses = inverse(lower)
    for h in range(heads):
        queries, keys, values, beta, gamma, spread = kept[h]
        inv_ref[h] = inverses[h]
        growth = jnp.exp(gamma)
        targets = jnp.concatenate([growth * beta * keys.astype(F32), beta * values.astype(F32)], axis=1)
        written = mm(inverses[h], targets, FINE)
        scores = spread * mmt(queries, keys)
        through = mm(scores, written, FINE)
        map_ref[h] = growth * queries.astype(F32) - through[:, :DK]
        out_ref[h] = through[:, DK:]
        final = gamma[size - 1 : size]
        faded = jnp.exp(final - gamma) * keys.astype(F32)
        summary = mtm(faded, written, FINE)
        unit = (iota((DK, DK), 0) == iota((DK, DK), 1)).astype(F32)
        passed = (jnp.exp(final) * unit - summary[:, :DK]).astype(BF16)
        for half in range(HALVES):
            sum_ref[HALVES * h + half, :, :DK] = passed
            sum_ref[HALVES * h + half, :, DK:] = summary[:, (half + 1) * DK : (half + 2) * DK].astype(BF16)


def whole_state(units_ref, head):
    return jnp.concatenate([units_ref[HALVES * head + half] for half in range(HALVES)], axis=1).astype(F32)


def mix_outputs(heads, out_ref, map_ref, state_ref, proj_ref, gain_ref, mixed_ref, gated_ref):
    gain = gain_ref[...]
    for h in range(heads):
        mixer_out = out_ref[h] + mm(map_ref[h], whole_state(state_ref, h), FINE)
        mixed_ref[h] = mixer_out
        gate = proj_ref[HALO:, h * PROJ + CONV : (h + 1) * PROJ]
        scale = lax.rsqrt(jnp.mean(mixer_out * mixer_out, axis=-1, keepdims=True) + 1e-05)
        gated = mixer_out * scale * gain * (gate * jax.nn.sigmoid(gate))
        gated_ref[:, h * DV : (h + 1) * DV] = gated.astype(BF16)


def mix_outputs_back(
    heads, slab, grad_ref, mixed_ref, map_ref, proj_ref, gain_ref, branch_ref,
    grad_mixed_ref, grad_gate_ref, grad_gain_ref, carried_ref, split_ref,
):
    gain = gain_ref[...]
    split_ref[...] = split_by_core(branch_ref[...].astype(F32), slab).astype(BF16)
    total = jnp.zeros_like(gain)
    for h in range(heads):
        grad = grad_ref[:, h * DV : (h + 1) * DV]
        mixer_out = mixed_ref[h]
        z = proj_ref[HALO:, h * PROJ + CONV : (h + 1) * PROJ]
        scale = lax.rsqrt(jnp.mean(mixer_out * mixer_out, axis=-1, keepdims=True) + 1e-05)
        normal = mixer_out * scale
        s = jax.nn.sigmoid(z)
        silu = z * s
        total = total + jnp.sum(grad * normal * silu, axis=0, keepdims=True)
        grad_gate_ref[:, h * DV : (h + 1) * DV] = (grad * normal * gain * s * (1.0 + z * (1.0 - s))).astype(BF16)
        u = grad * gain * silu
        grad_mixed = scale * u - normal * (scale * jnp.mean(u * normal, axis=-1, keepdims=True))
        grad_mixed_ref[h] = grad_mixed
        carried = mtm(map_ref[h], grad_mixed, FINE).astype(BF16)
        for half in range(HALVES):
            carried_ref[HALVES * h + half] = carried[:, half * DK : (half + 1) * DK]
    grad_gain_ref[...] = total


def norm_back(grad, values, scale):
    return scale * grad - values * (scale * scale * scale * jnp.sum(values * grad, axis=-1, keepdims=True))


def local_backward(
    heads, proj_ref, taps_ref, scales_ref, q_ref, k_ref, v_ref, inv_ref, grad_ref, state_ref, leaving_ref, gate_ref,
    out_ref, sibling_ref, taps_out_ref, scales_out_ref, halo_out, halo_in, tails,
    halo_s, halo_r, body_s, body_r, tail_s, tail_r, rate_s, rate_r,
):
    size = proj_ref.shape[0] - HALO
    seq, head_place = lax.axis_index("seq"), lax.axis_index("head")
    peers = lax.axis_size("seq")
    before, after = (lax.rem(seq + peers - 1, peers), head_place), (lax.rem(seq + 1, peers), head_place)
    sibling = (seq + 1 - 2 * (seq % 2), head_place)
    start_barrier([before, after, sibling])
    copies = []
    body = size - 2 * HALO
    rows, columns = triangles(size)
    rates = proj_ref[HALO:, heads * PROJ :]
    scales = scales_ref[...]
    lanes = iota((size, LANES), 1)
    grad_rates = jnp.zeros((size, LANES), F32)
    rates_total = jnp.zeros((8, LANES), F32)
    row8, lane8 = iota((8, LANES), 0), iota((8, LANES), 1)
    ones = jnp.ones((size, LANES), F32)
    above = (columns >= rows).astype(F32)
    for h in range(heads):
        queries, keys, values = q_ref[h], k_ref[h], v_ref[h]
        qf, kf, vf = queries.astype(F32), keys.astype(F32), values.astype(F32)
        beta, decay, gamma, gamma_row, pre = gates(rates, scales, h, heads)
        spread = decays_of(gamma, gamma_row)
        strict = columns < rows
        growth = jnp.exp(gamma)
        final = gamma[size - 1 : size]
        fade = jnp.exp(final - gamma)
        state, leaving = whole_state(state_ref, h), whole_state(leaving_ref, h)
        inv, grad = inv_ref[h], grad_ref[h]
        products = mmt(keys, keys)
        scores = spread * mmt(queries, keys)
        lower = jnp.where(strict, beta * spread * products, 0.0)
        residual = vf - growth * mm(kf, state, FINE)
        written = mm(inv, beta * residual, FINE)
        faded = fade * kf
        grad_written = mtm(scores, grad, FINE) + mm(faded, leaving, FINE)
        grad_scores = mmt(grad, written, FINE)
        grad_targets = mtm(inv, grad_written, FINE)
        grad_lower = jnp.where(strict, -mmt(grad_targets, written, FINE), 0.0)
        grad_values = beta * grad_targets
        grad_beta = jnp.sum(grad_targets * residual, axis=-1, keepdims=True)
        grad_beta = grad_beta + jnp.sum(grad_lower * spread * products, axis=-1, keepdims=True)
        q_first = growth * mmt(grad, state, FINE)
        k_first = -growth * mmt(grad_values, state, FINE)
        spread_scores = spread * grad_scores
        spread_lower = grad_lower * beta * spread
        grad_faded = mmt(written, leaving, FINE)
        grad_queries = q_first + mm(spread_scores, kf, FINE)
        grad_keys = (
            k_first
            + mtm(spread_scores, qf, FINE)
            + mm(spread_lower, kf, FINE)
            + mtm(spread_lower, kf, FINE)
            + fade * grad_faded
        )
        energy = grad_scores * scores + grad_lower * lower
        fading = jnp.sum(grad_faded * faded, axis=-1, keepdims=True)
        grad_gamma = jnp.sum(qf * q_first + kf * k_first, axis=-1, keepdims=True) - fading
        grad_gamma = grad_gamma + jnp.sum(energy, axis=-1, keepdims=True)
        at_end = jnp.sum(fading, axis=0, keepdims=True) + jnp.exp(final) * jnp.sum(
            jnp.sum(state * leaving, axis=1, keepdims=True), axis=0, keepdims=True
        )
        grad_gamma = grad_gamma + jnp.where(iota((size, 1), 0) == size - 1, at_end, 0.0)
        wide = jnp.broadcast_to(grad_gamma, (size, LANES)) - mtm(energy, ones, EXACT)
        grad_decay = mm(above, wide, EXACT)[:, 0:1]

        projected = proj_ref[:, h * PROJ : h * PROJ + CONV]
        taps = taps_ref[:, h * CONV : (h + 1) * CONV]
        extended, mixed, gate, (q_raw, q_scale), (k_raw, k_scale), *_ = mixer_inputs(projected, taps)
        grad_active = jnp.concatenate(
            [
                norm_back(grad_queries * DK ** (-0.5), q_raw, q_scale),
                norm_back(grad_keys, k_raw, k_scale),
                grad_values,
            ],
            axis=1,
        )
        grad_mixed = grad_active * gate * (1.0 + mixed * (1.0 - gate))
        padding = jnp.zeros((HALO, CONV), F32)
        full = jnp.concatenate([padding, grad_mixed, padding], axis=0)
        total = None
        for j in range(KW):
            shift = KW - 1 - j
            moved = full if shift == 0 else pltpu.roll(full, size + 2 * HALO - shift, 0)
            term = taps[j : j + 1] * moved[: size + HALO]
            total = term if total is None else total + term
            back = extended if shift == 0 else pltpu.roll(extended, shift, 0)
            taps_out_ref[j : j + 1, h * CONV : (h + 1) * CONV] = jnp.sum(
                grad_mixed * back[HALO:], axis=0, keepdims=True
            )
        halo_out[h] = total[:HALO]
        tails[h] = total[size - HALO :]
        out_ref[:, h * PROJ : h * PROJ + CONV] = total[HALO:].astype(BF16)
        out_ref[:, h * PROJ + CONV : (h + 1) * PROJ] = gate_ref[:, h * DV : (h + 1) * DV]
        copies.append(send(halo_out.at[h], halo_in.at[h], halo_s, halo_r, h, before))
        upper = (pl.ds(0, body), pl.ds(h * PROJ, PROJ))
        copies.append(send(out_ref.at[upper], sibling_ref.at[upper], body_s, body_r, h, sibling))

        grad_pre = -jnp.exp(column(scales[0:1], h)) * jax.nn.sigmoid(pre) * grad_decay
        grad_strength = grad_beta * beta * (1.0 - beta)
        grad_rates = grad_rates + jnp.where(lanes == h, grad_pre, 0.0)
        grad_rates = grad_rates + jnp.where(lanes == heads + h, grad_strength, 0.0)
        log_total = jnp.sum(grad_decay * decay, axis=0, keepdims=True)
        bias_total = jnp.sum(grad_pre, axis=0, keepdims=True)
        rates_total = rates_total + jnp.where((row8 == 0) & (lane8 == h), log_total, 0.0)
        rates_total = rates_total + jnp.where((row8 == 1) & (lane8 == h), bias_total, 0.0)
    out_ref[:, heads * PROJ :] = grad_rates.astype(BF16)
    scales_out_ref[...] = rates_total
    side = (pl.ds(0, size), pl.ds(heads * PROJ, LANES))
    last = [send(out_ref.at[side], sibling_ref.at[side], rate_s, rate_r, 0, sibling)]
    for copy in copies:
        copy.wait()
    for h in range(heads):
        arrived = jnp.where(seq < peers - 1, halo_in[h], 0.0)
        fixed = tails[h] + jnp.concatenate([jnp.zeros_like(arrived), arrived], axis=0)
        out_ref[body:, h * PROJ : h * PROJ + CONV] = fixed.astype(BF16)
        lower = (pl.ds(body, 2 * HALO), pl.ds(h * PROJ, PROJ))
        last.append(send(out_ref.at[lower], sibling_ref.at[lower], tail_s, tail_r, h, sibling))
    for copy in last:
        copy.wait()


def start_barrier(peers):
    barrier = pltpu.get_barrier_semaphore()
    for peer in peers:
        pl.semaphore_signal(barrier, inc=1, device_id=peer, device_id_type=MESH)
    pl.semaphore_wait(barrier, len(peers))


def send(source, target, sends, receives, slot, peer):
    copy = pltpu.make_async_remote_copy(
        src_ref=source,
        dst_ref=target,
        send_sem=sends.at[slot],
        recv_sem=receives.at[slot],
        device_id=peer,
        device_id_type=MESH,
    )
    copy.start()
    return copy


def twice(left, right):
    high = right.astype(BF16)
    low = (right - high.astype(F32)).astype(BF16)
    return mm(left, high) + mm(left, low)


def scan_places(members, groups):
    seq, head = lax.axis_index("seq"), lax.axis_index("head")
    member, group = seq % members, seq // members
    near = [(member + d) % members for d in range(members)]
    far = [(group + d) % groups for d in range(groups)]
    near_ids = [(group * members + place, head) for place in near]
    far_ids = [(place * members + member, head) for place in far]
    return member, group, near, near_ids, far_ids


def to_sibling(slots, sends, receives):
    seq, head = lax.axis_index("seq"), lax.axis_index("head")
    sibling = seq + 1 - 2 * (seq % 2)
    return [
        send(source, target, sends, receives, index, (sibling, head)) for index, (source, target) in enumerate(slots)
    ]


def other_half(ref):
    half = ref.shape[1] // 2
    at = (1 - lax.axis_index("seq") % 2) * half
    return ref.at[:, pl.ds(pl.multiple_of(at, half), half)]


def scan_forward(
    groups, pack_ref, split_ref, out_ref, sibling_ref, kept_ref, totals_ref, near_in, before, far_out, far_in, back_out, back_in,
    near_s, near_r, far_s, far_r, back_s, back_r, core_s, core_r,
):
    members = pack_ref.shape[0]
    member, group, near, near_ids, far_ids = scan_places(members, groups)
    start_barrier(near_ids[1:] + far_ids[1:])
    copies = [
        send(pack_ref.at[near[d]], near_in.at[member], near_s, near_r, d, near_ids[d]) for d in range(1, members)
    ]
    aside = to_sibling([(other_half(split_ref), sibling_ref)], core_s, core_r)
    near_in[member] = pack_ref[member]
    for copy in copies:
        copy.wait()
    unit = (iota((DK, DK), 0) == iota((DK, DK), 1)).astype(F32)
    total = jnp.concatenate([unit, jnp.zeros((DK, DK), F32)], axis=1)
    for j in range(members):
        before[j] = total
        kept_ref[j] = near_in[j, :, :DK]
        moved = twice(near_in[j, :, :DK], total)
        total = jnp.concatenate([moved[:, :DK], moved[:, DK:] + near_in[j, :, DK:].astype(F32)], axis=1)
    far_out[...] = total.astype(BF16)
    copies = [send(far_out, far_in.at[group], far_s, far_r, d, far_ids[d]) for d in range(1, groups)]
    far_in[group] = far_out[...]
    for copy in copies:
        copy.wait()
    state = jnp.zeros((DK, DK), F32)
    for j in range(groups):
        totals_ref[j] = far_in[j, :, :DK]
        fresh = twice(far_in[j, :, :DK], state) + far_in[j, :, DK:].astype(F32)
        state = jnp.where(j < group, fresh, state)
    for j in range(members):
        back_out[j] = (mm(before[j, :, :DK], state, FINE) + before[j, :, DK:]).astype(BF16)
    copies = [
        send(back_out.at[near[d]], back_in.at[member], back_s, back_r, d, near_ids[d]) for d in range(1, members)
    ]
    back_in[member] = back_out[member]
    for copy in copies:
        copy.wait()
    out_ref[...] = back_in[...]
    for copy in aside:
        copy.wait()


def scan_backward(
    groups, pack_ref, kept_ref, totals_ref, split_ref, gated_ref, out_ref, sibling_ref, sibling_gated_ref, near_in, turned, before, after, far_out, far_in, back_out, back_in,
    near_s, near_r, far_s, far_r, back_s, back_r, core_s, core_r,
):
    members = pack_ref.shape[0]
    member, group, near, near_ids, far_ids = scan_places(members, groups)
    start_barrier(near_ids[1:] + far_ids[1:])
    copies = [
        send(pack_ref.at[near[d]], near_in.at[member], near_s, near_r, d, near_ids[d]) for d in range(1, members)
    ]
    aside = to_sibling([(other_half(split_ref), sibling_ref), (gated_ref, sibling_gated_ref)], core_s, core_r)
    near_in[member] = pack_ref[member]
    passed = (iota((DK, DK), 0) == iota((DK, DK), 1)).astype(F32)
    for j in reversed(range(members)):
        turned[j] = kept_ref[j].astype(F32).T.astype(BF16)
        before[j] = passed
        passed = twice(turned[j], passed)
    for copy in copies:
        copy.wait()
    total = jnp.zeros((DK, DK), F32)
    for j in reversed(range(members)):
        after[j] = total
        total = twice(turned[j], total) + near_in[j].astype(F32)
    far_out[...] = total.astype(BF16)
    copies = [send(far_out, far_in.at[group], far_s, far_r, d, far_ids[d]) for d in range(1, groups)]
    far_in[group] = far_out[...]
    turned_totals = [totals_ref[j].astype(F32).T.astype(BF16) for j in range(groups)]
    for copy in copies:
        copy.wait()
    state = jnp.zeros((DK, DK), F32)
    for j in reversed(range(groups)):
        fresh = twice(turned_totals[j], state) + far_in[j].astype(F32)
        state = jnp.where(j > group, fresh, state)
    for j in range(members):
        back_out[j] = (mm(before[j], state, FINE) + after[j]).astype(BF16)
    copies = [
        send(back_out.at[near[d]], back_in.at[member], back_s, back_r, d, near_ids[d]) for d in range(1, members)
    ]
    back_in[member] = back_out[member]
    for copy in copies:
        copy.wait()
    out_ref[...] = back_in[...]
    for copy in aside:
        copy.wait()


def ring_ids(axis):
    seq, head = lax.axis_index("seq"), lax.axis_index("head")
    size = {"x": lax.axis_size("seq") // 8, "y": lax.axis_size("head"), "z": 4}[axis]
    me = {"x": seq // 8, "y": head, "z": (seq // 2) % 4}[axis]

    def at(place):
        if axis == "y":
            return (seq, place)
        if axis == "x":
            return (place * 8 + seq % 8, head)
        return ((seq // 8) * 8 + place * 2 + seq % 2, head)

    right, left = lax.rem(me + 1, size), lax.rem(me + size - 1, size)
    return me, right, left, lax.rem(me + 2, size), at(right), at(left)


def add_into(target, pieces, rows):
    step = min(rows, 32)

    @pl.loop(0, rows // step)
    def _(k):
        part = pl.ds(pl.multiple_of(k * step, step), step)
        total = pieces[0][part].astype(F32)
        for piece in pieces[1:]:
            total = total + piece[part].astype(F32)
        target[part] = total.astype(target.dtype)


def ring_reduce(ring, blocks, result, landing, sends, receives):
    me, right, left, across, right_id, left_id = ring
    rows = blocks.shape[1]
    half = rows // 2
    upper, lower = pl.ds(0, half), pl.ds(half, half)
    by_right = send(blocks.at[across, upper], landing.at[0], sends, receives, 0, right_id)
    by_left = send(blocks.at[across, lower], landing.at[1], sends, receives, 1, left_id)
    plain_right = send(blocks.at[right, lower], landing.at[2], sends, receives, 2, right_id)
    plain_left = send(blocks.at[left, upper], landing.at[3], sends, receives, 3, left_id)
    yield
    by_right.wait()
    add_into(landing.at[0], [blocks.at[right, upper], landing.at[0]], half)
    summed_right = send(landing.at[0], landing.at[4], sends, receives, 4, right_id)
    by_left.wait()
    add_into(landing.at[1], [blocks.at[left, lower], landing.at[1]], half)
    summed_left = send(landing.at[1], landing.at[5], sends, receives, 5, left_id)
    yield
    plain_right.wait()
    plain_left.wait()
    summed_right.wait()
    summed_left.wait()
    add_into(result.at[upper], [blocks.at[me, upper], landing.at[4], landing.at[3]], half)
    add_into(result.at[lower], [blocks.at[me, lower], landing.at[2], landing.at[5]], half)


def ring_gather(ring, blocks, sends, receives):
    me, right, left, across, right_id, left_id = ring
    rows = blocks.shape[1]
    half = rows // 2
    upper, lower = pl.ds(0, half), pl.ds(half, half)

    def go(place, part, slot, peer):
        return send(blocks.at[place, part], blocks.at[place, part], sends, receives, slot, peer)

    upper_right = go(me, upper, 0, right_id)
    lower_left = go(me, lower, 1, left_id)
    lower_right = go(me, lower, 2, right_id)
    upper_left = go(me, upper, 3, left_id)
    yield
    upper_right.wait()
    far_right = go(left, upper, 4, right_id)
    lower_left.wait()
    far_left = go(right, lower, 5, left_id)
    yield
    for copy in (lower_right, upper_left, far_right, far_left):
        copy.wait()


def finish(*generators):
    active = list(generators)
    while active:
        active = [g for g in active if next(g, active) is not active]


def rms_scale(values):
    return lax.rsqrt(jnp.mean(values * values, axis=-1, keepdims=True) + 1e-05)


def rms_back(grad, values, gain):
    scale = rms_scale(values)
    u = grad * gain
    back = scale * u - values * (scale * scale * scale * jnp.mean(u * values, axis=-1, keepdims=True))
    return back, jnp.sum(grad * values * scale, axis=0, keepdims=True)


def middle_kernel(part_ref, tokens_ref, gain_ref, second_ref, middle_ref, landing, red_s, red_r, gat_s, gat_r):
    ring = ring_ids("y")
    me = ring[0]
    start_barrier(ring[4:])
    finish(ring_reduce(ring, part_ref, middle_ref, landing, red_s, red_r))
    middle = tokens_ref[me].astype(F32) + middle_ref[...]
    second_ref[me] = (middle * rms_scale(middle) * gain_ref[...]).astype(BF16)
    gather = ring_gather(ring, second_ref, gat_s, gat_r)
    next(gather)
    middle_ref[...] = middle
    finish(gather)


def middle_back_kernel(
    part_ref, middle_ref, cotangent_ref, gain_ref, branch_ref, grad_ref, grad_gain_ref, landing, red_s, red_r, gat_s, gat_r
):
    ring = ring_ids("y")
    me = ring[0]
    start_barrier(ring[4:])
    finish(ring_reduce(ring, part_ref, grad_ref, landing, red_s, red_r))
    back, grad_gain = rms_back(grad_ref[...], middle_ref[...], gain_ref[...])
    grad = cotangent_ref[me].astype(F32) + back
    branch_ref[me] = grad.astype(BF16)
    gather = ring_gather(ring, branch_ref, gat_s, gat_r)
    next(gather)
    grad_ref[...] = grad
    grad_gain_ref[...] = grad_gain
    finish(gather)


def swap_add(value, partner, outgoing, incoming, sends, receives, slot, mask=None):
    outgoing[slot] = value
    copy = send(outgoing.at[slot], incoming.at[slot], sends, receives, slot, partner)
    yield
    copy.wait()
    other = incoming[slot]
    return value + (other if mask is None else jnp.where(mask, other, 0.0))


def last_kernel(
    heads, slab, normed_part_ref, ffn_part_ref, tokens_ref, middle_ref, grad_ref, gain_ref, small_ref,
    split_ref, split_sib_ref, proj_ref, proj_sib_ref, branch_ref, branch_sib_ref, gated_ref, gated_sib_ref,
    output_ref, low_ref, small_out_ref, first_a_ref, first_b_ref,
    land_n, land_f, sum_n, sum_f, swap_out, swap_in, part_a, part_b, land_a, land_b, mid_a, mid_b, land_a2, land_b2,
    rn_s, rn_r, gn_s, gn_r, rf_s, rf_r, gf_s, gf_r, sw_s, sw_r, a1_s, a1_r, b1_s, b1_r, a2_s, a2_r, b2_s, b2_r,
):
    seq, head = lax.axis_index("seq"), lax.axis_index("head")
    core = seq % 2
    ring_x, ring_y, ring_z = ring_ids("x"), ring_ids("y"), ring_ids("z")
    sibling = (seq + 1 - 2 * core, head)
    start_barrier(ring_x[4:] + ring_y[4:] + ring_z[4:] + (sibling,))
    me = ring_y[0]
    reduce_n = ring_reduce(ring_y, normed_part_ref, sum_n, land_n, rn_s, rn_r)
    next(reduce_n)

    half = split_ref.shape[1] // 2
    own = core * half
    wide_a, wide_b = part_a.shape[2], part_b.shape[2]
    rest = proj_ref.shape[1] - wide_a
    places = 4
    many = places * slab

    def product(x, x_sib, y, y_sib, block, columns):
        at = pl.ds(pl.multiple_of(own + block * many, many), many)
        here = pl.ds(pl.multiple_of(block * many, many), many)
        return mtm(x[:, at], y[:, columns]) + mtm(x_sib[:, here], y_sib[:, columns])

    @pl.loop(0, places)
    def _(block):
        rows = pl.ds(pl.multiple_of(block * slab, slab), slab)
        in_part = product(split_ref, split_sib_ref, proj_ref, proj_sib_ref, block, pl.ds(wide_a, rest)).astype(BF16)
        out_part = product(branch_ref, branch_sib_ref, gated_ref, gated_sib_ref, block, pl.ds(0, wide_b - rest)).astype(BF16)
        for place in range(places):
            part_b[place, rows, :rest] = in_part[place * slab : (place + 1) * slab]
            part_b[place, rows, rest:] = out_part[place * slab : (place + 1) * slab]

    reduce_b = ring_reduce(ring_z, part_b, mid_b, land_b, b1_s, b1_r)
    next(reduce_b)

    @pl.loop(0, places)
    def _(block):
        part_a[block] = product(split_ref, split_sib_ref, proj_ref, proj_sib_ref, block, pl.ds(0, wide_a)).astype(BF16)

    reduce_a = ring_reduce(ring_x, part_a, mid_a, land_a, a1_s, a1_r)
    next(reduce_a)

    next(reduce_n)
    finish(reduce_n)
    back, grad_gain = rms_back(sum_n[...], tokens_ref[me].astype(F32), gain_ref[...])
    low_ref[me] = (grad_ref[...] + back).astype(BF16)
    gather_n = ring_gather(ring_y, low_ref, gn_s, gn_r)
    next(gather_n)
    reduce_f = ring_reduce(ring_y, ffn_part_ref, sum_f, land_f, rf_s, rf_r)
    next(reduce_f)
    next(reduce_b)
    next(reduce_a)
    next(gather_n)

    def all_small():
        rows8, lanes = iota(small_ref.shape, 0), iota(small_ref.shape, 1)
        value = small_ref[...] + jnp.where(rows8 == 0, grad_gain, 0.0)
        shared = (rows8 < 2) | ((rows8 == 2) & (lanes < DV))
        slot = 0
        for ring, mask in ((ring_y, shared), (ring_x, None), (ring_z, None)):
            place, right_id, left_id = ring[0], ring[4], ring[5]
            even = lax.rem(place, 2) == 0
            for flip in (False, True):
                ids = tuple(
                    jnp.where(jnp.logical_xor(even, flip), r, l) for r, l in zip(right_id, left_id)
                )
                value = yield from swap_add(value, ids, swap_out, swap_in, sw_s, sw_r, slot, mask)
                slot += 1
        value = yield from swap_add(value, sibling, swap_out, swap_in, sw_s, sw_r, slot)
        small_out_ref[...] = value

    small = all_small()
    next(small)
    next(reduce_f)
    next(small)
    next(small)
    finish(reduce_b)
    reduce_b2 = ring_reduce(ring_x, mid_b.reshape(places, slab, wide_b), first_b_ref, land_b2, b2_s, b2_r)
    next(reduce_b2)
    finish(reduce_a)
    reduce_a2 = ring_reduce(ring_z, mid_a.reshape(places, slab, wide_a), first_a_ref, land_a2, a2_s, a2_r)
    next(reduce_a2)
    finish(reduce_f)
    output_ref[me] = (middle_ref[...] + sum_f[...]).astype(BF16)
    gather_f = ring_gather(ring_y, output_ref, gf_s, gf_r)
    next(gather_f)
    next(reduce_b2)
    next(reduce_a2)
    finish(small, gather_n, gather_f, reduce_b2, reduce_a2)


def mlp_grads(second_ref, cotangent_ref, gate_up_ref, hidden_ref, out_ref):
    wide = gate_up_ref.shape[1]
    out_ref[:, :wide] = mtm(second_ref[...], gate_up_ref[...]).astype(BF16)
    out_ref[:, wide:] = mtm(cotangent_ref[...], hidden_ref[...]).astype(BF16)


def finish_kernel(heads, first_a_ref, first_b_ref, mlp_ref, low_ref, in_ref, rate_ref, out_ref, gate_up_ref, down_ref, tokens_ref):
    wide = first_a_ref.shape[1]
    rates = heads * PROJ
    both = jnp.concatenate([first_a_ref[...], first_b_ref[...]], axis=1)
    for h in range(heads):
        in_ref[:, h] = both[:, h * PROJ : (h + 1) * PROJ]
        out_ref[:, h] = both[:, rates + LANES + h * DV : rates + LANES + (h + 1) * DV]
    for g in range(2):
        rate_ref[:, g] = both[:, rates + g * heads : rates + (g + 1) * heads]
    units = down_ref.shape[1]
    for g in range(2):
        gate_up_ref[:, g] = mlp_ref[:, g * units : (g + 1) * units].astype(F32)
    down_ref[...] = mlp_ref[:, 2 * units :].astype(F32)
    tokens_ref[...] = low_ref[...].astype(F32)


def call(kernel, outs, *args, name):
    return pl.pallas_call(
        kernel,
        in_specs=[pl.BlockSpec(memory_space=pltpu.VMEM)] * len(args),
        out_specs=[pl.BlockSpec(memory_space=pltpu.VMEM)] * len(outs),
        out_shape=[jax.ShapeDtypeStruct(shape, kind) for shape, kind in outs],
        compiler_params=pltpu.CompilerParams(vmem_limit_bytes=VMEM_LIMIT),
        name=name,
    )(*args)


def remote_call(kernel, outs, scratch, identity, *args, name):
    return pl.pallas_call(
        kernel,
        in_specs=[pl.BlockSpec(memory_space=pltpu.VMEM)] * len(args),
        out_specs=[pl.BlockSpec(memory_space=pltpu.VMEM)] * len(outs),
        out_shape=[jax.ShapeDtypeStruct(shape, kind) for shape, kind in outs],
        scratch_shapes=scratch,
        compiler_params=pltpu.CompilerParams(
            vmem_limit_bytes=VMEM_LIMIT, collective_id=identity, has_side_effects=True
        ),
        name=name,
    )(*args)


def pairs(*sizes):
    return [pltpu.SemaphoreType.DMA((size,)) for size in sizes for _ in range(2)]


def shifted(block, axis, distance):
    devices = range(lax.axis_size(axis))
    route = [(i - distance, i) for i in devices if i - distance in devices]
    return lax.ppermute(block, axis, route)


def per_device(
    tokens,
    mixer_gain,
    in_weight,
    rate_weight,
    conv_weight,
    decay_log,
    decay_bias,
    out_gain,
    out_weight,
    ffn_gain,
    gate_up_weight,
    down_weight,
    cotangent,
):
    count, width = tokens.shape
    heads = in_weight.shape[1]
    hidden_units = down_weight.shape[1]
    slab = in_weight.shape[0]
    projections = heads * PROJ + LANES
    units = heads * HALVES
    peers, sharers = lax.axis_size("seq"), lax.axis_size("head")
    groups = peers // units
    rows = count // sharers

    first = jnp.concatenate(
        [
            in_weight.reshape(slab, heads * PROJ),
            rate_weight.reshape(slab, 2 * heads),
            jnp.zeros((slab, LANES - 2 * heads), BF16),
        ],
        axis=1,
    )
    rest = jnp.concatenate(
        [out_weight.reshape(slab, heads * DV), gate_up_weight.reshape(slab, 2 * hidden_units), down_weight], axis=1
    )
    first_full = lax.all_gather(first, "seq", axis=0, tiled=True)
    rest_full = lax.all_gather(rest, "seq", axis=0, tiled=True)
    out_full = rest_full[:, : heads * DV]
    gate_up_full = rest_full[:, heads * DV : heads * DV + 2 * hidden_units]
    down_full = rest_full[:, heads * DV + 2 * hidden_units :]

    behind = shifted(tokens[count - HALO :], "seq", 1)
    source = jnp.concatenate([behind, tokens], axis=0).astype(F32)
    normed_long = (source * rms_scale(source) * mixer_gain).astype(BF16)
    projected = mm(normed_long, first_full)

    taps = conv_weight.reshape(KW, heads * CONV)
    scales = jnp.pad(jnp.stack([decay_log, decay_bias]), ((0, 6), (0, LANES - heads)))
    queries, keys, values, inv, out_local, out_map, summary, normed_split = call(
        functools.partial(local_forward, heads, slab),
        [
            ((heads, count, DK), BF16),
            ((heads, count, DK), BF16),
            ((heads, count, DV), BF16),
            ((heads, count, count), F32),
            ((heads, count, DV), F32),
            ((heads, count, DK), F32),
            ((units, DK, 2 * DK), BF16),
            ((count, width), BF16),
        ],
        projected,
        taps,
        scales,
        normed_long,
        name="local_forward",
    )
    block = (DK, DK)
    double = (DK, 2 * DK)
    entering, normed_sibling, kept, totals = remote_call(
        functools.partial(scan_forward, groups),
        [((units, *block), BF16), ((count, width // 2), BF16), ((units, *block), BF16), ((groups, *block), BF16)],
        [
            pltpu.VMEM((units, *double), BF16),
            pltpu.VMEM((units, *double), F32),
            pltpu.VMEM(double, BF16),
            pltpu.VMEM((groups, *double), BF16),
            pltpu.VMEM((units, *block), BF16),
            pltpu.VMEM((units, *block), BF16),
            *pairs(units, groups, units, 1),
        ],
        1,
        summary,
        normed_split,
        name="scan_forward",
    )
    gain_row = out_gain.reshape(1, DV)
    mixer_out, gated = call(
        functools.partial(mix_outputs, heads),
        [((heads, count, DV), F32), ((count, heads * DV), BF16)],
        out_local,
        out_map,
        entering,
        projected,
        gain_row,
        name="mix_outputs",
    )
    branch = mmt(gated, out_full)
    def landing(*shape):
        return pltpu.VMEM((6, *shape), BF16)

    blocked = (sharers, rows, width)
    ring = [landing(rows // 2, width)]
    second, middle = remote_call(
        middle_kernel,
        [(blocked, BF16), ((rows, width), F32)],
        ring + pairs(6, 6),
        2,
        branch.astype(BF16).reshape(blocked),
        tokens.reshape(blocked),
        ffn_gain.reshape(1, width),
        name="middle",
    )
    second = second.reshape(count, width)
    gate_up = mm(second, gate_up_full)
    z, up = gate_up[:, :hidden_units], gate_up[:, hidden_units:]
    s = jax.nn.sigmoid(z)
    hidden = (z * s * up).astype(BF16)
    ffn_part = mmt(hidden, down_full)
    grad_hidden = mm(cotangent, down_full)
    grad_gate_up = jnp.concatenate([grad_hidden * up * s * (1.0 + z * (1.0 - s)), grad_hidden * z * s], axis=1).astype(
        BF16
    )
    second_part = mmt(grad_gate_up, gate_up_full)
    grad_mlp = pl.pallas_call(
        mlp_grads,
        grid=(width // 256,),
        in_specs=[
            pl.BlockSpec((count, 256), lambda i: (0, i)),
            pl.BlockSpec((count, 256), lambda i: (0, i)),
            pl.BlockSpec((count, 2 * hidden_units), lambda i: (0, 0)),
            pl.BlockSpec((count, hidden_units), lambda i: (0, 0)),
        ],
        out_specs=pl.BlockSpec((256, 3 * hidden_units), lambda i: (i, 0)),
        out_shape=jax.ShapeDtypeStruct((width, 3 * hidden_units), BF16),
        compiler_params=pltpu.CompilerParams(vmem_limit_bytes=VMEM_LIMIT),
        name="mlp_grads",
    )(second, cotangent, grad_gate_up, hidden)
    second_part, grad_mlp = lax.optimization_barrier((second_part.astype(BF16), grad_mlp))
    grad_mlp = lax.psum_scatter(grad_mlp, "seq", scatter_dimension=0, tiled=True)
    grad_branch, grad_middle, grad_ffn_gain = remote_call(
        middle_back_kernel,
        [(blocked, BF16), ((rows, width), F32), ((1, width), F32)],
        ring + pairs(6, 6),
        3,
        second_part.reshape(blocked),
        middle,
        cotangent.reshape(blocked),
        ffn_gain.reshape(1, width),
        name="middle_back",
    )
    grad_branch = grad_branch.reshape(count, width)
    grad_gated = mm(grad_branch, out_full)
    grad_mixed, grad_gate, grad_out_gain, carried, branch_split = call(
        functools.partial(mix_outputs_back, heads, slab),
        [
            ((heads, count, DV), F32),
            ((count, heads * DV), BF16),
            ((1, DV), F32),
            ((units, DK, DK), BF16),
            ((count, width), BF16),
        ],
        grad_gated,
        mixer_out,
        out_map,
        projected,
        gain_row,
        grad_branch,
        name="mix_outputs_back",
    )
    leaving, branch_sibling, gated_sibling = remote_call(
        functools.partial(scan_backward, groups),
        [((units, *block), BF16), ((count, width // 2), BF16), ((count, heads * DV), BF16)],
        [
            pltpu.VMEM((units, *block), BF16),
            pltpu.VMEM((units, *block), BF16),
            pltpu.VMEM((units, *block), F32),
            pltpu.VMEM((units, *block), F32),
            pltpu.VMEM(block, BF16),
            pltpu.VMEM((groups, *block), BF16),
            pltpu.VMEM((units, *block), BF16),
            pltpu.VMEM((units, *block), BF16),
            *pairs(units, groups, units, 2),
        ],
        4,
        carried,
        kept,
        totals,
        branch_split,
        gated,
        name="scan_backward",
    )
    grad_projected, grad_sibling, grad_taps, grad_scales = remote_call(
        functools.partial(local_backward, heads),
        [
            ((count, projections), BF16),
            ((count, projections), BF16),
            ((KW, heads * CONV), F32),
            ((8, LANES), F32),
        ],
        [
            pltpu.VMEM((heads, HALO, CONV), F32),
            pltpu.VMEM((heads, HALO, CONV), F32),
            pltpu.VMEM((heads, 2 * HALO, CONV), F32),
            *pairs(heads, heads, heads, 1),
        ],
        6,
        projected,
        taps,
        scales,
        queries,
        keys,
        values,
        inv,
        grad_mixed,
        entering,
        leaving,
        grad_gate,
        name="local_backward",
    )
    normed_part = mmt(grad_projected, first_full)
    small = jnp.concatenate(
        [
            jnp.zeros((1, width), F32),
            grad_ffn_gain,
            jnp.concatenate(
                [
                    grad_out_gain,
                    grad_scales[0:1],
                    grad_scales[1:2],
                    jnp.zeros((1, width - DV - 2 * LANES), F32),
                ],
                axis=1,
            ),
            grad_taps,
            jnp.zeros((1, width), F32),
        ],
        axis=0,
    )
    wide_a = -(-(projections + heads * DV) // (2 * LANES)) * LANES
    wide_b = projections + heads * DV - wide_a
    many = 4 * slab
    output, low, small, first_a, first_b = remote_call(
        functools.partial(last_kernel, heads, slab),
        [
            (blocked, BF16),
            (blocked, BF16),
            ((8, width), F32),
            ((slab, wide_a), F32),
            ((slab, wide_b), F32),
        ],
        [
            landing(rows // 2, width),
            landing(rows // 2, width),
            pltpu.VMEM((rows, width), F32),
            pltpu.VMEM((rows, width), F32),
            pltpu.VMEM((7, 8, width), F32),
            pltpu.VMEM((7, 8, width), F32),
            pltpu.VMEM((4, many, wide_a), BF16),
            pltpu.VMEM((4, many, wide_b), BF16),
            landing(many // 2, wide_a),
            landing(many // 2, wide_b),
            pltpu.VMEM((many, wide_a), BF16),
            pltpu.VMEM((many, wide_b), BF16),
            landing(slab // 2, wide_a),
            landing(slab // 2, wide_b),
            *pairs(6, 6, 6, 6, 7, 6, 6, 6, 6),
        ],
        5,
        normed_part.astype(BF16).reshape(blocked),
        ffn_part.astype(BF16).reshape(blocked),
        tokens.reshape(blocked),
        middle,
        grad_middle,
        mixer_gain.reshape(1, width),
        small,
        normed_split,
        normed_sibling,
        grad_projected,
        grad_sibling,
        branch_split,
        branch_sibling,
        gated,
        gated_sibling,
        name="last",
    )
    grad_in, grad_rate, grad_out, grad_gate_up_weight, grad_down, grad_tokens = call(
        functools.partial(finish_kernel, heads),
        [
            ((slab, heads, PROJ), F32),
            ((slab, 2, heads), F32),
            ((slab, heads, DV), F32),
            ((slab, 2, hidden_units), F32),
            ((slab, hidden_units), F32),
            ((count, width), F32),
        ],
        first_a,
        first_b,
        grad_mlp,
        low.reshape(count, width),
        name="finish",
    )
    return (
        output.reshape(count, width),
        grad_tokens,
        small[0],
        grad_in,
        grad_rate,
        small[3 : 3 + KW].reshape(KW, heads, CONV),
        small[2, DV : DV + heads],
        small[2, DV + LANES : DV + LANES + heads],
        small[2, :DV],
        grad_out,
        small[1],
        grad_gate_up_weight,
        grad_down,
    )


def solution(mesh):
    in_specs = (
        P("seq", None),
        P(),
        P("seq", "head", None),
        P("seq", None, "head"),
        P(None, "head", None),
        P("head"),
        P("head"),
        P(),
        P("seq", "head", None),
        P(),
        P("seq", None, "head"),
        P("seq", "head"),
        P("seq", None),
    )
    out_specs = (
        P("seq", None),
        P("seq", None),
        P(),
        P("seq", "head", None),
        P("seq", None, "head"),
        P(None, "head", None),
        P("head"),
        P("head"),
        P(),
        P("seq", "head", None),
        P(),
        P("seq", None, "head"),
        P("seq", "head"),
    )
    return jax.shard_map(
        per_device, mesh=mesh, in_specs=in_specs, out_specs=out_specs, check_vma=False
    )
```

```python
import functools

import jax
import jax.numpy as jnp
from jax import lax
from jax.experimental import pallas as pl
from jax.experimental.pallas import tpu as pltpu
from jax.sharding import PartitionSpec as P

DK = 128
DV = 256
KW = 4
CONV = 512
PROJ = 768
LANES = 128
HALO = 8
HALVES = DV // DK
MESH = pl.DeviceIdType.MESH

F32 = jnp.float32
BF16 = jnp.bfloat16
EXACT = lax.Precision.HIGHEST
FINE = lax.Precision.HIGH
VMEM_LIMIT = 56 * 1024 * 1024


def dot(a, b, dims, precision=None):
    return lax.dot_general(a, b, (dims, ((), ())), precision=precision, preferred_element_type=F32)


def mm(a, b, precision=None):
    return dot(a, b, ((1,), (0,)), precision)


def mmt(a, b, precision=None):
    return dot(a, b, ((1,), (1,)), precision)


def mtm(a, b, precision=None):
    return dot(a, b, ((0,), (0,)), precision)


def iota(shape, dim):
    return lax.broadcasted_iota(jnp.int32, shape, dim)


def softplus(x):
    return jnp.maximum(x, 0.0) + jnp.log1p(jnp.exp(-jnp.abs(x)))


def split_by_core(values, slab):
    width = values.shape[1]
    lanes = iota((values.shape[0], 2 * slab), 1)
    firsts, seconds = [], []
    for at in range(0, width, 4 * slab):
        a, b = values[:, at : at + 2 * slab], values[:, at + 2 * slab : at + 4 * slab]
        firsts.append(jnp.where(lanes < slab, a, pltpu.roll(b, slab, 1)))
        seconds.append(jnp.where(lanes < slab, pltpu.roll(a, slab, 1), b))
    return jnp.concatenate(firsts + seconds, axis=1)


def column(block, index):
    lanes = iota(block.shape, 1)
    return jnp.sum(jnp.where(lanes == index, block, 0.0), axis=1, keepdims=True)


def triangles(size):
    rows, columns = iota((size, size), 0), iota((size, size), 1)
    return rows, columns


def gates(rates, scales, head, heads):
    size = rates.shape[0]
    log_rate = column(scales[0:1], head)
    bias = column(scales[1:2], head)
    pre = column(rates, head) + bias
    beta = jax.nn.sigmoid(column(rates, heads + head))
    decay = -jnp.exp(log_rate) * softplus(pre)
    rows, columns = triangles(size)
    below = (columns <= rows).astype(F32)
    gamma_wide = mm(below, jnp.broadcast_to(decay, (size, LANES)), EXACT)
    gamma = gamma_wide[:, 0:1]
    gamma_row = gamma_wide.T[0:1, :]
    return beta, decay, gamma, gamma_row, pre


def decays_of(gamma, gamma_row):
    size = gamma.shape[0]
    rows, columns = triangles(size)
    inside = columns <= rows
    return jnp.where(inside, jnp.exp(jnp.where(inside, gamma - gamma_row, 0.0)), 0.0)


def inverse(lower):
    size = lower[0].shape[0]
    rows, columns = triangles(size)
    unit = (rows == columns).astype(F32)
    known = [unit - jnp.where(rows // 2 == columns // 2, a, 0.0) for a in lower]
    width = 2
    while width < size:
        fresh = (rows // (2 * width) == columns // (2 * width)) & (rows // width != columns // width)
        parts = [jnp.where(fresh, a, 0.0) for a in lower]
        first = [mm(c, x, FINE) for c, x in zip(parts, known)]
        known = [x - mm(x, y, FINE) for x, y in zip(known, first)]
        width *= 2
    return known


def convolved(extended, taps):
    length = extended.shape[0]
    total = None
    for j in range(KW):
        shift = KW - 1 - j
        moved = extended if shift == 0 else pltpu.roll(extended, shift, 0)
        term = taps[j : j + 1] * moved[HALO:]
        total = term if total is None else total + term
    return total


def unit_rows(values):
    return lax.rsqrt(jnp.sum(values * values, axis=-1, keepdims=True) + 1e-06)


def mixer_inputs(projected, taps):
    extended = projected[:, :CONV].astype(BF16).astype(F32)
    mixed = convolved(extended, taps)
    gate = jax.nn.sigmoid(mixed)
    active = mixed * gate
    q_raw, k_raw = active[:, :DK], active[:, DK : 2 * DK]
    q_scale, k_scale = unit_rows(q_raw), unit_rows(k_raw)
    queries = (q_raw * q_scale * DK ** (-0.5)).astype(BF16)
    keys = (k_raw * k_scale).astype(BF16)
    values = active[:, 2 * DK :].astype(BF16)
    return extended, mixed, gate, (q_raw, q_scale), (k_raw, k_scale), queries, keys, values


def local_forward(
    heads, slab, proj_ref, taps_ref, scales_ref, normed_ref, q_ref, k_ref, v_ref, inv_ref, out_ref, map_ref, sum_ref, split_ref
):
    size = proj_ref.shape[0] - HALO
    split_ref[...] = split_by_core(normed_ref[HALO:].astype(F32), slab).astype(BF16)
    rows, columns = triangles(size)
    rates = proj_ref[HALO:, heads * CONV : heads * CONV + LANES]
    scales = scales_ref[...]
    lower, kept = [], []
    for h in range(heads):
        projected = proj_ref[:, h * CONV : (h + 1) * CONV]
        taps = taps_ref[:, h * CONV : (h + 1) * CONV]
        *_, queries, keys, values = mixer_inputs(projected, taps)
        q_ref[h], k_ref[h], v_ref[h] = queries, keys, values
        beta, decay, gamma, gamma_row, _ = gates(rates, scales, h, heads)
        spread = decays_of(gamma, gamma_row)
        lower.append(jnp.where(columns < rows, beta * spread * mmt(keys, keys), 0.0))
        kept.append((queries, keys, values, beta, gamma, spread))
    inverses = inverse(lower)
    for h in range(heads):
        queries, keys, values, beta, gamma, spread = kept[h]
        inv_ref[h] = inverses[h]
        growth = jnp.exp(gamma)
        targets = jnp.concatenate([growth * beta * keys.astype(F32), beta * values.astype(F32)], axis=1)
        written = mm(inverses[h], targets, FINE)
        scores = spread * mmt(queries, keys)
        through = mm(scores, written, FINE)
        map_ref[h] = growth * queries.astype(F32) - through[:, :DK]
        out_ref[h] = through[:, DK:]
        final = gamma[size - 1 : size]
        faded = jnp.exp(final - gamma) * keys.astype(F32)
        summary = mtm(faded, written, FINE)
        unit = (iota((DK, DK), 0) == iota((DK, DK), 1)).astype(F32)
        passed = (jnp.exp(final) * unit - summary[:, :DK]).astype(BF16)
        for half in range(HALVES):
            sum_ref[HALVES * h + half, :, :DK] = passed
            sum_ref[HALVES * h + half, :, DK:] = summary[:, (half + 1) * DK : (half + 2) * DK].astype(BF16)


def gate_columns(heads, head):
    at = heads * CONV + LANES + head * DV
    return pl.ds(at, DV)


def whole_state(units_ref, head):
    return jnp.concatenate([units_ref[HALVES * head + half] for half in range(HALVES)], axis=1).astype(F32)


def mix_outputs(heads, out_ref, map_ref, state_ref, proj_ref, gain_ref, mixed_ref, gated_ref):
    gain = gain_ref[...]
    for h in range(heads):
        mixer_out = out_ref[h] + mm(map_ref[h], whole_state(state_ref, h), FINE)
        mixed_ref[h] = mixer_out
        gate = proj_ref[HALO:, gate_columns(heads, h)]
        scale = lax.rsqrt(jnp.mean(mixer_out * mixer_out, axis=-1, keepdims=True) + 1e-05)
        gated = mixer_out * scale * gain * (gate * jax.nn.sigmoid(gate))
        gated_ref[:, h * DV : (h + 1) * DV] = gated.astype(BF16)


def mix_outputs_back(
    heads, slab, grad_ref, mixed_ref, map_ref, proj_ref, gain_ref, branch_ref,
    grad_mixed_ref, grad_gate_ref, grad_gain_ref, carried_ref, split_ref,
):
    gain = gain_ref[...]
    split_ref[...] = split_by_core(branch_ref[...].astype(F32), slab).astype(BF16)
    total = jnp.zeros_like(gain)
    for h in range(heads):
        grad = grad_ref[:, h * DV : (h + 1) * DV]
        mixer_out = mixed_ref[h]
        z = proj_ref[HALO:, gate_columns(heads, h)]
        scale = lax.rsqrt(jnp.mean(mixer_out * mixer_out, axis=-1, keepdims=True) + 1e-05)
        normal = mixer_out * scale
        s = jax.nn.sigmoid(z)
        silu = z * s
        total = total + jnp.sum(grad * normal * silu, axis=0, keepdims=True)
        grad_gate_ref[:, h * DV : (h + 1) * DV] = (grad * normal * gain * s * (1.0 + z * (1.0 - s))).astype(BF16)
        u = grad * gain * silu
        grad_mixed = scale * u - normal * (scale * jnp.mean(u * normal, axis=-1, keepdims=True))
        grad_mixed_ref[h] = grad_mixed
        carried = mtm(map_ref[h], grad_mixed, FINE).astype(BF16)
        for half in range(HALVES):
            carried_ref[HALVES * h + half] = carried[:, half * DK : (half + 1) * DK]
    grad_gain_ref[...] = total


def weight_blocks(x, x_sib, y, y_sib, columns, target, slab, z_first):
    places = target.shape[0]
    many = places * slab
    own = lax.axis_index("seq") % 2 * (x.shape[1] // 2)

    @pl.loop(0, places)
    def _(block):
        at = pl.ds(pl.multiple_of(own + block * many, many), many)
        here = pl.ds(pl.multiple_of(block * many, many), many)
        part = (mtm(x[:, at], y[:, columns]) + mtm(x_sib[:, here], y_sib[:, columns])).astype(BF16)
        if z_first:
            rows = pl.ds(pl.multiple_of(block * slab, slab), slab)
            for place in range(places):
                target[place, rows] = part[place * slab : (place + 1) * slab]
        else:
            target[block] = part


def sum_both(first, second, part, middle, result, landing, landing_2, semaphores):
    places, many, wide = part.shape
    yield from ring_reduce(first, part, middle, landing, semaphores[0], semaphores[1])
    blocks = middle.reshape(places, many // places, wide)
    yield from ring_reduce(second, blocks, result, landing_2, semaphores[2], semaphores[3])


def norm_back(grad, values, scale):
    return scale * grad - values * (scale * scale * scale * jnp.sum(values * grad, axis=-1, keepdims=True))


def local_backward(
    heads, slab, proj_ref, taps_ref, scales_ref, q_ref, k_ref, v_ref, inv_ref, grad_ref, state_ref, leaving_ref,
    gate_ref, gate_sib_ref, gated_ref, gated_sib_ref, split_ref, split_sib_ref, branch_ref, branch_sib_ref,
    ffn_part_ref, middle_ref,
    out_ref, sibling_ref, taps_out_ref, scales_out_ref, first_out_ref, first_gate_ref, output_ref,
    halo_out, halo_in, tails, part_o, part_g, land_o, land_g, mid_o, mid_g, land_o2, land_g2, land_f, sum_f,
    halo_s, halo_r, body_s, body_r, tail_s, tail_r, rate_s, rate_r,
    o1_s, o1_r, g1_s, g1_r, o2_s, o2_r, g2_s, g2_r, rf_s, rf_r, gf_s, gf_r,
):
    size = proj_ref.shape[0] - HALO
    seq, head_place = lax.axis_index("seq"), lax.axis_index("head")
    peers = lax.axis_size("seq")
    before, after = (lax.rem(seq + peers - 1, peers), head_place), (lax.rem(seq + 1, peers), head_place)
    sibling = (seq + 1 - 2 * (seq % 2), head_place)
    ring_x, ring_y, ring_z = ring_ids("x"), ring_ids("y"), ring_ids("z")
    start_barrier([before, after, sibling, *ring_x[4:], *ring_y[4:], *ring_z[4:]])
    copies = []

    def output_sum():
        yield from ring_reduce(ring_y, ffn_part_ref, sum_f, land_f, rf_s, rf_r)
        output_ref[ring_y[0]] = (middle_ref[...] + sum_f[...]).astype(BF16)
        yield from ring_gather(ring_y, output_ref, gf_s, gf_r)

    weight_blocks(branch_ref, branch_sib_ref, gated_ref, gated_sib_ref, pl.ds(0, part_o.shape[2]), part_o, slab, False)
    beside = [
        output_sum(),
        sum_both(ring_x, ring_z, part_o, mid_o, first_out_ref, land_o, land_o2, (o1_s, o1_r, o2_s, o2_r)),
        sum_both(ring_z, ring_x, part_g, mid_g, first_gate_ref, land_g, land_g2, (g1_s, g1_r, g2_s, g2_r)),
    ]
    next(beside[0])
    next(beside[1])
    weight_blocks(split_ref, split_sib_ref, gate_ref, gate_sib_ref, pl.ds(0, part_g.shape[2]), part_g, slab, True)
    next(beside[2])
    body = size - 2 * HALO
    rows, columns = triangles(size)
    rates = proj_ref[HALO:, heads * CONV : heads * CONV + LANES]
    scales = scales_ref[...]
    lanes = iota((size, LANES), 1)
    grad_rates = jnp.zeros((size, LANES), F32)
    rates_total = jnp.zeros((8, LANES), F32)
    row8, lane8 = iota((8, LANES), 0), iota((8, LANES), 1)
    ones = jnp.ones((size, LANES), F32)
    above = (columns >= rows).astype(F32)
    for h in range(heads):
        queries, keys, values = q_ref[h], k_ref[h], v_ref[h]
        qf, kf, vf = queries.astype(F32), keys.astype(F32), values.astype(F32)
        beta, decay, gamma, gamma_row, pre = gates(rates, scales, h, heads)
        spread = decays_of(gamma, gamma_row)
        strict = columns < rows
        growth = jnp.exp(gamma)
        final = gamma[size - 1 : size]
        fade = jnp.exp(final - gamma)
        state, leaving = whole_state(state_ref, h), whole_state(leaving_ref, h)
        inv, grad = inv_ref[h], grad_ref[h]
        products = mmt(keys, keys)
        scores = spread * mmt(queries, keys)
        lower = jnp.where(strict, beta * spread * products, 0.0)
        residual = vf - growth * mm(kf, state, FINE)
        written = mm(inv, beta * residual, FINE)
        faded = fade * kf
        grad_written = mtm(scores, grad, FINE) + mm(faded, leaving, FINE)
        grad_scores = mmt(grad, written, FINE)
        grad_targets = mtm(inv, grad_written, FINE)
        grad_lower = jnp.where(strict, -mmt(grad_targets, written, FINE), 0.0)
        grad_values = beta * grad_targets
        grad_beta = jnp.sum(grad_targets * residual, axis=-1, keepdims=True)
        grad_beta = grad_beta + jnp.sum(grad_lower * spread * products, axis=-1, keepdims=True)
        q_first = growth * mmt(grad, state, FINE)
        k_first = -growth * mmt(grad_values, state, FINE)
        spread_scores = spread * grad_scores
        spread_lower = grad_lower * beta * spread
        grad_faded = mmt(written, leaving, FINE)
        grad_queries = q_first + mm(spread_scores, kf, FINE)
        grad_keys = (
            k_first
            + mtm(spread_scores, qf, FINE)
            + mm(spread_lower, kf, FINE)
            + mtm(spread_lower, kf, FINE)
            + fade * grad_faded
        )
        energy = grad_scores * scores + grad_lower * lower
        fading = jnp.sum(grad_faded * faded, axis=-1, keepdims=True)
        grad_gamma = jnp.sum(qf * q_first + kf * k_first, axis=-1, keepdims=True) - fading
        grad_gamma = grad_gamma + jnp.sum(energy, axis=-1, keepdims=True)
        at_end = jnp.sum(fading, axis=0, keepdims=True) + jnp.exp(final) * jnp.sum(
            jnp.sum(state * leaving, axis=1, keepdims=True), axis=0, keepdims=True
        )
        grad_gamma = grad_gamma + jnp.where(iota((size, 1), 0) == size - 1, at_end, 0.0)
        wide = jnp.broadcast_to(grad_gamma, (size, LANES)) - mtm(energy, ones, EXACT)
        grad_decay = mm(above, wide, EXACT)[:, 0:1]

        projected = proj_ref[:, h * CONV : (h + 1) * CONV]
        taps = taps_ref[:, h * CONV : (h + 1) * CONV]
        extended, mixed, gate, (q_raw, q_scale), (k_raw, k_scale), *_ = mixer_inputs(projected, taps)
        grad_active = jnp.concatenate(
            [
                norm_back(grad_queries * DK ** (-0.5), q_raw, q_scale),
                norm_back(grad_keys, k_raw, k_scale),
                grad_values,
            ],
            axis=1,
        )
        grad_mixed = grad_active * gate * (1.0 + mixed * (1.0 - gate))
        padding = jnp.zeros((HALO, CONV), F32)
        full = jnp.concatenate([padding, grad_mixed, padding], axis=0)
        total = None
        for j in range(KW):
            shift = KW - 1 - j
            moved = full if shift == 0 else pltpu.roll(full, size + 2 * HALO - shift, 0)
            term = taps[j : j + 1] * moved[: size + HALO]
            total = term if total is None else total + term
            back = extended if shift == 0 else pltpu.roll(extended, shift, 0)
            taps_out_ref[j : j + 1, h * CONV : (h + 1) * CONV] = jnp.sum(
                grad_mixed * back[HALO:], axis=0, keepdims=True
            )
        halo_out[h] = total[:HALO]
        tails[h] = total[size - HALO :]
        out_ref[:, h * CONV : (h + 1) * CONV] = total[HALO:].astype(BF16)
        copies.append(send(halo_out.at[h], halo_in.at[h], halo_s, halo_r, h, before))
        upper = (pl.ds(0, body), pl.ds(h * CONV, CONV))
        copies.append(send(out_ref.at[upper], sibling_ref.at[upper], body_s, body_r, h, sibling))
        if h > 0:
            for stage in beside:
                next(stage)

        grad_pre = -jnp.exp(column(scales[0:1], h)) * jax.nn.sigmoid(pre) * grad_decay
        grad_strength = grad_beta * beta * (1.0 - beta)
        grad_rates = grad_rates + jnp.where(lanes == h, grad_pre, 0.0)
        grad_rates = grad_rates + jnp.where(lanes == heads + h, grad_strength, 0.0)
        log_total = jnp.sum(grad_decay * decay, axis=0, keepdims=True)
        bias_total = jnp.sum(grad_pre, axis=0, keepdims=True)
        rates_total = rates_total + jnp.where((row8 == 0) & (lane8 == h), log_total, 0.0)
        rates_total = rates_total + jnp.where((row8 == 1) & (lane8 == h), bias_total, 0.0)
    out_ref[:, heads * CONV :] = grad_rates.astype(BF16)
    scales_out_ref[...] = rates_total
    side = (pl.ds(0, size), pl.ds(heads * CONV, LANES))
    last = [send(out_ref.at[side], sibling_ref.at[side], rate_s, rate_r, 0, sibling)]
    for copy in copies:
        copy.wait()
    for h in range(heads):
        arrived = jnp.where(seq < peers - 1, halo_in[h], 0.0)
        fixed = tails[h] + jnp.concatenate([jnp.zeros_like(arrived), arrived], axis=0)
        out_ref[body:, h * CONV : (h + 1) * CONV] = fixed.astype(BF16)
        lower = (pl.ds(body, 2 * HALO), pl.ds(h * CONV, CONV))
        last.append(send(out_ref.at[lower], sibling_ref.at[lower], tail_s, tail_r, h, sibling))
    for copy in last:
        copy.wait()
    finish(*beside)


def say_here(peers):
    barrier = pltpu.get_barrier_semaphore()
    for peer in peers:
        pl.semaphore_signal(barrier, inc=1, device_id=peer, device_id_type=MESH)

    def all_here():
        pl.semaphore_wait(barrier, len(peers))

    return all_here


def start_barrier(peers):
    say_here(peers)()


def send(source, target, sends, receives, slot, peer):
    copy = pltpu.make_async_remote_copy(
        src_ref=source,
        dst_ref=target,
        send_sem=sends.at[slot],
        recv_sem=receives.at[slot],
        device_id=peer,
        device_id_type=MESH,
    )
    copy.start()
    return copy


def twice(left, right):
    high = right.astype(BF16)
    low = (right - high.astype(F32)).astype(BF16)
    return mm(left, high) + mm(left, low)


def scan_places(members, groups):
    seq, head = lax.axis_index("seq"), lax.axis_index("head")
    member, group = seq % members, seq // members
    near = [(member + d) % members for d in range(members)]
    far = [(group + d) % groups for d in range(groups)]
    near_ids = [(group * members + place, head) for place in near]
    far_ids = [(place * members + member, head) for place in far]
    return member, group, near, near_ids, far_ids


def to_sibling(slots, sends, receives):
    seq, head = lax.axis_index("seq"), lax.axis_index("head")
    sibling = seq + 1 - 2 * (seq % 2)
    return [
        send(source, target, sends, receives, index, (sibling, head)) for index, (source, target) in enumerate(slots)
    ]


def other_half(ref):
    half = ref.shape[1] // 2
    at = (1 - lax.axis_index("seq") % 2) * half
    return ref.at[:, pl.ds(pl.multiple_of(at, half), half)]


def scan_forward(
    groups, pack_ref, split_ref, out_ref, sibling_ref, kept_ref, totals_ref, near_in, before, far_out, far_in, back_out, back_in,
    near_s, near_r, far_s, far_r, back_s, back_r, core_s, core_r,
):
    members = pack_ref.shape[0]
    member, group, near, near_ids, far_ids = scan_places(members, groups)
    start_barrier(near_ids[1:] + far_ids[1:])
    copies = [
        send(pack_ref.at[near[d]], near_in.at[member], near_s, near_r, d, near_ids[d]) for d in range(1, members)
    ]
    aside = to_sibling([(other_half(split_ref), sibling_ref)], core_s, core_r)
    near_in[member] = pack_ref[member]
    for copy in copies:
        copy.wait()
    unit = (iota((DK, DK), 0) == iota((DK, DK), 1)).astype(F32)
    total = jnp.concatenate([unit, jnp.zeros((DK, DK), F32)], axis=1)
    for j in range(members):
        before[j] = total
        kept_ref[j] = near_in[j, :, :DK]
        moved = twice(near_in[j, :, :DK], total)
        total = jnp.concatenate([moved[:, :DK], moved[:, DK:] + near_in[j, :, DK:].astype(F32)], axis=1)
    far_out[...] = total.astype(BF16)
    copies = [send(far_out, far_in.at[group], far_s, far_r, d, far_ids[d]) for d in range(1, groups)]
    far_in[group] = far_out[...]
    for copy in copies:
        copy.wait()
    state = jnp.zeros((DK, DK), F32)
    for j in range(groups):
        totals_ref[j] = far_in[j, :, :DK]
        fresh = twice(far_in[j, :, :DK], state) + far_in[j, :, DK:].astype(F32)
        state = jnp.where(j < group, fresh, state)
    for j in range(members):
        back_out[j] = (mm(before[j, :, :DK], state, FINE) + before[j, :, DK:]).astype(BF16)
    copies = [
        send(back_out.at[near[d]], back_in.at[member], back_s, back_r, d, near_ids[d]) for d in range(1, members)
    ]
    back_in[member] = back_out[member]
    for copy in copies:
        copy.wait()
    out_ref[...] = back_in[...]
    for copy in aside:
        copy.wait()


def scan_backward(
    groups, pack_ref, kept_ref, totals_ref, split_ref, gated_ref, gate_ref,
    out_ref, sibling_ref, sibling_gated_ref, sibling_gate_ref, near_in, turned, before, after, far_out, far_in, back_out, back_in,
    near_s, near_r, far_s, far_r, back_s, back_r, core_s, core_r,
):
    members = pack_ref.shape[0]
    member, group, near, near_ids, far_ids = scan_places(members, groups)
    start_barrier(near_ids[1:] + far_ids[1:])
    copies = [
        send(pack_ref.at[near[d]], near_in.at[member], near_s, near_r, d, near_ids[d]) for d in range(1, members)
    ]
    aside = to_sibling(
        [(other_half(split_ref), sibling_ref), (gated_ref, sibling_gated_ref), (gate_ref, sibling_gate_ref)], core_s, core_r
    )
    near_in[member] = pack_ref[member]
    passed = (iota((DK, DK), 0) == iota((DK, DK), 1)).astype(F32)
    for j in reversed(range(members)):
        turned[j] = kept_ref[j].astype(F32).T.astype(BF16)
        before[j] = passed
        passed = twice(turned[j], passed)
    for copy in copies:
        copy.wait()
    total = jnp.zeros((DK, DK), F32)
    for j in reversed(range(members)):
        after[j] = total
        total = twice(turned[j], total) + near_in[j].astype(F32)
    far_out[...] = total.astype(BF16)
    copies = [send(far_out, far_in.at[group], far_s, far_r, d, far_ids[d]) for d in range(1, groups)]
    far_in[group] = far_out[...]
    turned_totals = [totals_ref[j].astype(F32).T.astype(BF16) for j in range(groups)]
    for copy in copies:
        copy.wait()
    state = jnp.zeros((DK, DK), F32)
    for j in reversed(range(groups)):
        fresh = twice(turned_totals[j], state) + far_in[j].astype(F32)
        state = jnp.where(j > group, fresh, state)
    for j in range(members):
        back_out[j] = (mm(before[j], state, FINE) + after[j]).astype(BF16)
    copies = [
        send(back_out.at[near[d]], back_in.at[member], back_s, back_r, d, near_ids[d]) for d in range(1, members)
    ]
    back_in[member] = back_out[member]
    for copy in copies:
        copy.wait()
    out_ref[...] = back_in[...]
    for copy in aside:
        copy.wait()


def ring_ids(axis):
    seq, head = lax.axis_index("seq"), lax.axis_index("head")
    size = {"x": lax.axis_size("seq") // 8, "y": lax.axis_size("head"), "z": 4}[axis]
    me = {"x": seq // 8, "y": head, "z": (seq // 2) % 4}[axis]

    def at(place):
        if axis == "y":
            return (seq, place)
        if axis == "x":
            return (place * 8 + seq % 8, head)
        return ((seq // 8) * 8 + place * 2 + seq % 2, head)

    right, left = lax.rem(me + 1, size), lax.rem(me + size - 1, size)
    return me, right, left, lax.rem(me + 2, size), at(right), at(left)


def add_into(target, pieces, rows):
    step = min(rows, 32)

    @pl.loop(0, rows // step)
    def _(k):
        part = pl.ds(pl.multiple_of(k * step, step), step)
        total = pieces[0][part].astype(F32)
        for piece in pieces[1:]:
            total = total + piece[part].astype(F32)
        target[part] = total.astype(target.dtype)


def ring_reduce(ring, blocks, result, landing, sends, receives):
    me, right, left, across, right_id, left_id = ring
    rows = blocks.shape[1]
    half = rows // 2
    upper, lower = pl.ds(0, half), pl.ds(half, half)
    by_right = send(blocks.at[across, upper], landing.at[0], sends, receives, 0, right_id)
    by_left = send(blocks.at[across, lower], landing.at[1], sends, receives, 1, left_id)
    plain_right = send(blocks.at[right, lower], landing.at[2], sends, receives, 2, right_id)
    plain_left = send(blocks.at[left, upper], landing.at[3], sends, receives, 3, left_id)
    yield
    by_right.wait()
    add_into(landing.at[0], [blocks.at[right, upper], landing.at[0]], half)
    summed_right = send(landing.at[0], landing.at[4], sends, receives, 4, right_id)
    by_left.wait()
    add_into(landing.at[1], [blocks.at[left, lower], landing.at[1]], half)
    summed_left = send(landing.at[1], landing.at[5], sends, receives, 5, left_id)
    yield
    plain_right.wait()
    plain_left.wait()
    summed_right.wait()
    summed_left.wait()
    add_into(result.at[upper], [blocks.at[me, upper], landing.at[4], landing.at[3]], half)
    add_into(result.at[lower], [blocks.at[me, lower], landing.at[2], landing.at[5]], half)


def ring_gather(ring, blocks, sends, receives):
    me, right, left, across, right_id, left_id = ring
    rows = blocks.shape[1]
    half = rows // 2
    upper, lower = pl.ds(0, half), pl.ds(half, half)

    def go(place, part, slot, peer):
        return send(blocks.at[place, part], blocks.at[place, part], sends, receives, slot, peer)

    upper_right = go(me, upper, 0, right_id)
    lower_left = go(me, lower, 1, left_id)
    lower_right = go(me, lower, 2, right_id)
    upper_left = go(me, upper, 3, left_id)
    yield
    upper_right.wait()
    far_right = go(left, upper, 4, right_id)
    lower_left.wait()
    far_left = go(right, lower, 5, left_id)
    yield
    for copy in (lower_right, upper_left, far_right, far_left):
        copy.wait()


def finish(*generators):
    active = list(generators)
    while active:
        active = [g for g in active if next(g, active) is not active]


def rms_scale(values):
    return lax.rsqrt(jnp.mean(values * values, axis=-1, keepdims=True) + 1e-05)


def rms_back(grad, values, gain):
    scale = rms_scale(values)
    u = grad * gain
    back = scale * u - values * (scale * scale * scale * jnp.mean(u * values, axis=-1, keepdims=True))
    return back, jnp.sum(grad * values * scale, axis=0, keepdims=True)


def middle_kernel(part_ref, tokens_ref, gain_ref, second_ref, middle_ref, landing, red_s, red_r, gat_s, gat_r):
    ring = ring_ids("y")
    me = ring[0]
    start_barrier(ring[4:])
    finish(ring_reduce(ring, part_ref, middle_ref, landing, red_s, red_r))
    middle = tokens_ref[me].astype(F32) + middle_ref[...]
    second_ref[me] = (middle * rms_scale(middle) * gain_ref[...]).astype(BF16)
    gather = ring_gather(ring, second_ref, gat_s, gat_r)
    next(gather)
    middle_ref[...] = middle
    finish(gather)


def chunks_of(units):
    return [(at, min(2 * LANES, units - at)) for at in range(0, units, 2 * LANES)]


def ffn_kernel(
    slab, second_ref, cotangent_ref, middle_ref, gain_ref, weights_ref,
    branch_ref, grad_ref, grad_gain_ref, ffn_ref, gate_up_ref, down_a_ref, down_b_ref,
    weights, hidden, grad_hidden, second_split, cotangent_split, second_sib, cotangent_sib, hidden_sib, grad_sib,
    total, part, landing, gate_up_part, part_a, part_b, land_a, land_b, mid_a, mid_b, land_a2, land_b2,
    load_s, store_s, half_s, half_r, hid_s, hid_r, gra_s, gra_r, red_s, red_r, gat_s, gat_r,
    a1_s, a1_r, b1_s, b1_r, a2_s, a2_r, b2_s, b2_r,
):
    seq, head = lax.axis_index("seq"), lax.axis_index("head")
    ring_x, ring_y, ring_z = ring_ids("x"), ring_ids("y"), ring_ids("z")
    sibling = (seq + 1 - 2 * (seq % 2), head)
    all_here = say_here(ring_x[4:] + ring_y[4:] + ring_z[4:] + (sibling,))
    count, width = second_ref.shape
    chunks = chunks_of(hidden.shape[1])
    loads = []
    for i, (at, length) in enumerate(chunks):
        columns = pl.ds(3 * at, 3 * length)
        loads.append(pltpu.make_async_copy(weights_ref.at[:, columns], weights.at[:, columns], load_s.at[i]))
        loads[-1].start()
    second_split[...] = split_by_core(second_ref[...].astype(F32), slab).astype(BF16)
    cotangent_split[...] = split_by_core(cotangent_ref[...].astype(F32), slab).astype(BF16)
    all_here()
    aside = [
        send(other_half(second_split), second_sib, half_s, half_r, 0, sibling),
        send(other_half(cotangent_split), cotangent_sib, half_s, half_r, 1, sibling),
    ]
    step = 256
    for i, (at, length) in enumerate(chunks):
        loads[i].wait()
        gate, up, down = (pl.ds(3 * at + k * length, length) for k in range(3))
        z = mm(second_ref[...], weights[:, gate])
        u = mm(second_ref[...], weights[:, up])
        g = mm(cotangent_ref[...], weights[:, down])
        s = jax.nn.sigmoid(z)
        silu = z * s
        here, both = pl.ds(at, length), pl.ds(2 * at, 2 * length)
        hidden[:, here] = (silu * u).astype(BF16)
        grad_hidden[:, pl.ds(2 * at, length)] = (g * u * s * (1.0 + z * (1.0 - s))).astype(BF16)
        grad_hidden[:, pl.ds(2 * at + length, length)] = (g * silu).astype(BF16)
        aside.append(send(hidden.at[:, here], hidden_sib.at[:, here], hid_s, hid_r, i, sibling))
        aside.append(send(grad_hidden.at[:, both], grad_sib.at[:, both], gra_s, gra_r, i, sibling))

        @pl.loop(0, width // step)
        def _(k, at=at, length=length, both=both, i=i):
            rows = pl.ds(pl.multiple_of(k * step, step), step)
            product = mmt(grad_hidden[:, both], weights[rows, pl.ds(3 * at, 2 * length)])
            if i == 0:
                total[:, rows] = product
            elif i < len(chunks) - 1:
                total[:, rows] += product
            else:
                full = total[:, rows] + product
                for p in range(part.shape[0]):
                    n = part.shape[1]
                    part[p, :, rows] = full[p * n : (p + 1) * n].astype(BF16)

    reduce = ring_reduce(ring_y, part, grad_ref, landing, red_s, red_r)
    next(reduce)
    for copy in aside:
        copy.wait()
    wide_a, wide_b = part_a.shape[2], part_b.shape[2]
    weight_blocks(cotangent_split, cotangent_sib, hidden, hidden_sib, pl.ds(0, wide_a), part_a, slab, False)
    sum_a = sum_both(ring_x, ring_z, part_a, mid_a, down_a_ref, land_a, land_a2, (a1_s, a1_r, a2_s, a2_r))
    next(sum_a)
    weight_blocks(cotangent_split, cotangent_sib, hidden, hidden_sib, pl.ds(wide_a, wide_b), part_b, slab, True)
    sum_b = sum_both(ring_z, ring_x, part_b, mid_b, down_b_ref, land_b, land_b2, (b1_s, b1_r, b2_s, b2_r))
    next(sum_b)
    next(reduce)

    @pl.loop(0, width // step)
    def _(k):
        rows = pl.ds(pl.multiple_of(k * step, step), step)
        product = None
        for at, length in chunks:
            term = mmt(hidden[:, pl.ds(at, length)], weights[rows, pl.ds(3 * at + 2 * length, length)])
            product = term if product is None else product + term
        for p in range(ffn_ref.shape[0]):
            n = ffn_ref.shape[1]
            ffn_ref[p, :, rows] = product[p * n : (p + 1) * n].astype(BF16)

    finish(reduce)
    back, grad_gain = rms_back(grad_ref[...], middle_ref[...], gain_ref[...])
    grad = cotangent_ref[pl.ds(pl.multiple_of(ring_y[0] * slab, slab), slab)].astype(F32) + back
    branch_ref[ring_y[0]] = grad.astype(BF16)
    gather = ring_gather(ring_y, branch_ref, gat_s, gat_r)
    next(gather)
    grad_ref[...] = grad
    grad_gain_ref[...] = grad_gain
    next(sum_a)
    next(sum_b)
    weight_blocks(
        second_split, second_sib, grad_hidden, grad_sib, pl.ds(0, grad_hidden.shape[1]), gate_up_part, slab, False
    )
    store = pltpu.make_async_copy(gate_up_part, gate_up_ref, store_s)
    store.start()
    next(gather)
    next(sum_a)
    next(sum_b)
    finish(gather, sum_a, sum_b)
    store.wait()


def swap_add(value, partner, outgoing, incoming, sends, receives, slot, mask=None):
    outgoing[slot] = value
    copy = send(outgoing.at[slot], incoming.at[slot], sends, receives, slot, partner)
    yield
    copy.wait()
    other = incoming[slot]
    return value + (other if mask is None else jnp.where(mask, other, 0.0))


def last_kernel(
    slab, gate_ref, tokens_ref, middle_grad_ref, gain_ref, ffn_gain_ref, out_gain_ref, scales_ref, taps_ref,
    split_ref, split_sib_ref, proj_ref, proj_sib_ref, weights_ref,
    low_ref, small_out_ref, first_a_ref, first_b_ref,
    weights, small_ref, part_n, land_n, sum_n, swap_out, swap_in, part_a, part_b, land_a, land_b, mid_a, mid_b, land_a2, land_b2,
    load_s, rn_s, rn_r, gn_s, gn_r, sw_s, sw_r, a1_s, a1_r, b1_s, b1_r, a2_s, a2_r, b2_s, b2_r,
):
    seq, head = lax.axis_index("seq"), lax.axis_index("head")
    ring_x, ring_y, ring_z = ring_ids("x"), ring_ids("y"), ring_ids("z")
    sibling = (seq + 1 - 2 * (seq % 2), head)
    all_here = say_here(ring_x[4:] + ring_y[4:] + ring_z[4:] + (sibling,))
    width, wide = weights.shape
    step = 256

    def load(k):
        rows = pl.ds(pl.multiple_of(k * step, step), step)
        return pltpu.make_async_copy(weights_ref.at[rows, pl.ds(0, wide)], weights.at[rows], load_s.at[k])

    for k in range(width // step):
        load(k).start()
    small_ref[...] = jnp.zeros_like(small_ref)
    small_ref[1:2] = ffn_gain_ref[...]
    small_ref[2:3, :DV] = out_gain_ref[...]
    small_ref[2:3, DV : DV + LANES] = scales_ref[0:1]
    small_ref[2:3, DV + LANES : DV + 2 * LANES] = scales_ref[1:2]
    small_ref[3 : 3 + KW] = taps_ref[...]
    me = ring_y[0]
    wide_a, wide_b = part_a.shape[2], part_b.shape[2]
    weight_blocks(split_ref, split_sib_ref, proj_ref, proj_sib_ref, pl.ds(0, wide_a), part_a, slab, False)
    all_here()
    sum_a = sum_both(ring_x, ring_z, part_a, mid_a, first_a_ref, land_a, land_a2, (a1_s, a1_r, a2_s, a2_r))
    next(sum_a)
    weight_blocks(split_ref, split_sib_ref, proj_ref, proj_sib_ref, pl.ds(wide_a, wide_b), part_b, slab, True)
    sum_b = sum_both(ring_z, ring_x, part_b, mid_b, first_b_ref, land_b, land_b2, (b1_s, b1_r, b2_s, b2_r))
    next(sum_b)
    narrow = proj_ref.shape[1]

    @pl.loop(0, width // step)
    def _(k):
        load(k).wait()
        rows = pl.ds(pl.multiple_of(k * step, step), step)
        product = mmt(proj_ref[...], weights[rows, :narrow]) + mmt(gate_ref[...], weights[rows, narrow:])
        for p in range(part_n.shape[0]):
            n = part_n.shape[1]
            part_n[p, :, rows] = product[p * n : (p + 1) * n].astype(BF16)

    reduce_n = ring_reduce(ring_y, part_n, sum_n, land_n, rn_s, rn_r)
    next(reduce_n)
    next(sum_a)
    next(sum_b)
    next(reduce_n)
    finish(reduce_n)
    back, grad_gain = rms_back(sum_n[...], tokens_ref[me].astype(F32), gain_ref[...])
    low_ref[me] = (middle_grad_ref[...] + back).astype(BF16)
    gather_n = ring_gather(ring_y, low_ref, gn_s, gn_r)
    next(gather_n)

    def all_small():
        rows8, lanes = iota(small_ref.shape, 0), iota(small_ref.shape, 1)
        value = small_ref[...] + jnp.where(rows8 == 0, grad_gain, 0.0)
        shared = (rows8 < 2) | ((rows8 == 2) & (lanes < DV))
        slot = 0
        for ring, mask in ((ring_y, shared), (ring_x, None), (ring_z, None)):
            place, right_id, left_id = ring[0], ring[4], ring[5]
            even = lax.rem(place, 2) == 0
            for flip in (False, True):
                ids = tuple(jnp.where(jnp.logical_xor(even, flip), r, l) for r, l in zip(right_id, left_id))
                value = yield from swap_add(value, ids, swap_out, swap_in, sw_s, sw_r, slot, mask)
                slot += 1
        value = yield from swap_add(value, sibling, swap_out, swap_in, sw_s, sw_r, slot)
        small_out_ref[...] = value

    small = all_small()
    next(small)
    next(sum_a)
    next(sum_b)
    next(small)
    next(gather_n)
    next(small)
    next(sum_a)
    next(sum_b)
    finish(small, gather_n, sum_a, sum_b)


def finish_kernel(
    heads, first_a_ref, first_b_ref, first_out_ref, first_gate_ref, gate_up_in_ref, down_a_ref, down_b_ref, low_ref, small_ref,
    in_ref, rate_ref, out_ref, gate_up_ref, down_ref, tokens_ref, taps_ref, mixer_gain_ref, ffn_gain_ref, out_gain_ref,
):
    both = jnp.concatenate([first_a_ref[...], first_b_ref[...]], axis=1)
    for h in range(heads):
        in_ref[:, h, :CONV] = both[:, h * CONV : (h + 1) * CONV]
        in_ref[:, h, CONV:] = first_gate_ref[:, h * DV : (h + 1) * DV]
        out_ref[:, h] = first_out_ref[:, h * DV : (h + 1) * DV]
        taps_ref[:, h] = small_ref[3 : 3 + KW, h * CONV : (h + 1) * CONV]
    rates = heads * CONV
    for g in range(2):
        rate_ref[:, g] = both[:, rates + g * heads : rates + (g + 1) * heads]
    for at, length in chunks_of(down_ref.shape[1]):
        for g in range(2):
            gate_up_ref[:, g, at : at + length] = gate_up_in_ref[:, pl.ds(2 * at + g * length, length)].astype(F32)
    down_ref[:, : down_a_ref.shape[1]] = down_a_ref[...]
    down_ref[:, down_a_ref.shape[1] :] = down_b_ref[...]
    tokens_ref[...] = low_ref[...].astype(F32)
    mixer_gain_ref[...] = small_ref[0]
    ffn_gain_ref[...] = small_ref[1]
    out_gain_ref[...] = small_ref[2, :DV]


def gather_weights(slab_ref, full_ref, own_s, core_s, core_r, ring_s, ring_r):
    seq, head = lax.axis_index("seq"), lax.axis_index("head")
    core = seq % 2
    sibling = (seq + 1 - 2 * core, head)
    ring_x, ring_z = ring_ids("x"), ring_ids("z")
    x, z = ring_x[0], ring_z[0]
    rows, wide = slab_ref.shape
    cut = -(-wide // (2 * LANES)) * LANES
    start_barrier(ring_x[4:] + ring_z[4:] + (sibling,))
    own = pltpu.make_async_copy(slab_ref, full_ref.at[x, z, core], own_s)
    own.start()
    counts = {"core": 0, "ring": 0}
    waiting = []

    def slot(kind):
        counts[kind] += 1
        return counts[kind] - 1

    def across(source, target):
        waiting.append(send(source, target, core_s, core_r, slot("core"), sibling))

    across(slab_ref, full_ref.at[x, z, core])
    half = rows // 2
    upper, lower = pl.ds(0, half), pl.ds(half, half)

    def round_ring(ring, at, source, arrived):
        me, right, left, opposite, right_id, left_id = ring

        def go(place, part, peer):
            index = slot("ring")
            origin = source(part) if place is me else at(place, part)
            return send(origin, at(place, part), ring_s, ring_r, index, peer)

        upper_right = go(me, upper, right_id)
        lower_left = go(me, lower, left_id)
        lower_right = go(me, lower, right_id)
        upper_left = go(me, upper, left_id)
        yield
        upper_right.wait()
        far_right = go(left, upper, right_id)
        lower_left.wait()
        far_left = go(right, lower, left_id)
        lower_right.wait()
        arrived(left)
        upper_left.wait()
        arrived(right)
        yield
        far_right.wait()
        far_left.wait()
        arrived(opposite)

    active = []
    for ring_1, ring_2, columns, x_first in (
        (ring_x, ring_z, pl.ds(0, cut), True),
        (ring_z, ring_x, pl.ds(cut, wide - cut), False),
    ):
        def place_of(first, second, part, columns=columns, x_first=x_first):
            where = (first, second) if x_first else (second, first)
            return full_ref.at[where[0], where[1], core, part, columns]

        everything = pl.ds(0, rows)

        def start_second(first, source=None, ring_1=ring_1, ring_2=ring_2, place_of=place_of):
            def at(place, part):
                return place_of(first, place, part)

            def arrived(place):
                across(place_of(first, place, everything), place_of(first, place, everything))

            active.append(round_ring(ring_2, at, source or (lambda part: at(ring_2[0], part)), arrived))

        def at_first(place, part, ring_2=ring_2, place_of=place_of):
            return place_of(place, ring_2[0], part)

        def arrived_first(place, at_first=at_first, start_second=start_second):
            across(at_first(place, everything), at_first(place, everything))
            start_second(place)

        def mine(part, columns=columns):
            return slab_ref.at[part, columns]

        active.append(round_ring(ring_1, at_first, mine, arrived_first))
        start_second(ring_1[0], mine)
    while active:
        ended = []
        for stage in list(active):
            if next(stage, active) is active:
                ended.append(stage)
        active[:] = [stage for stage in active if stage not in ended]
    own.wait()
    for copy in waiting:
        copy.wait()


def call(kernel, outs, *args, name):
    return pl.pallas_call(
        kernel,
        in_specs=[pl.BlockSpec(memory_space=pltpu.VMEM)] * len(args),
        out_specs=[pl.BlockSpec(memory_space=pltpu.VMEM)] * len(outs),
        out_shape=[jax.ShapeDtypeStruct(shape, kind) for shape, kind in outs],
        compiler_params=pltpu.CompilerParams(vmem_limit_bytes=VMEM_LIMIT),
        name=name,
    )(*args)


def remote_call(kernel, outs, scratch, identity, *args, name):
    return pl.pallas_call(
        kernel,
        in_specs=[pl.BlockSpec(memory_space=pltpu.VMEM)] * len(args),
        out_specs=[pl.BlockSpec(memory_space=pltpu.VMEM)] * len(outs),
        out_shape=[jax.ShapeDtypeStruct(shape, kind) for shape, kind in outs],
        scratch_shapes=scratch,
        compiler_params=pltpu.CompilerParams(
            vmem_limit_bytes=VMEM_LIMIT, collective_id=identity, has_side_effects=True
        ),
        name=name,
    )(*args)


def pairs(*sizes):
    return [pltpu.SemaphoreType.DMA((size,)) for size in sizes for _ in range(2)]


def shifted(block, axis, distance):
    devices = range(lax.axis_size(axis))
    route = [(i - distance, i) for i in devices if i - distance in devices]
    return lax.ppermute(block, axis, route)


def per_device(
    tokens,
    mixer_gain,
    in_weight,
    rate_weight,
    conv_weight,
    decay_log,
    decay_bias,
    out_gain,
    out_weight,
    ffn_gain,
    gate_up_weight,
    down_weight,
    cotangent,
):
    count, width = tokens.shape
    heads = in_weight.shape[1]
    hidden_units = down_weight.shape[1]
    slab = in_weight.shape[0]
    projections = heads * PROJ + LANES
    units = heads * HALVES
    peers, sharers = lax.axis_size("seq"), lax.axis_size("head")
    groups = peers // units
    rows = count // sharers

    convolved_wide = heads * CONV + LANES
    first = jnp.concatenate(
        [
            in_weight[:, :, :CONV].reshape(slab, heads * CONV),
            rate_weight.reshape(slab, 2 * heads),
            jnp.zeros((slab, LANES - 2 * heads), BF16),
            in_weight[:, :, CONV:].reshape(slab, heads * DV),
            out_weight.reshape(slab, heads * DV),
        ],
        axis=1,
    )
    anywhere = pl.BlockSpec(memory_space=pl.ANY)
    first_full = pl.pallas_call(
        gather_weights,
        in_specs=[anywhere],
        out_specs=anywhere,
        out_shape=jax.ShapeDtypeStruct((4, 4, 2, slab, projections + heads * DV), BF16),
        scratch_shapes=[pltpu.SemaphoreType.DMA, *pairs(31, 60)],
        compiler_params=pltpu.CompilerParams(vmem_limit_bytes=VMEM_LIMIT, collective_id=7, has_side_effects=True),
        name="gather_weights",
    )(first)
    pieces = []
    for at, length in chunks_of(hidden_units):
        part = slice(at, at + length)
        pieces += [gate_up_weight[:, 0, part], gate_up_weight[:, 1, part], down_weight[:, part]]
    first_full, rest = lax.optimization_barrier((first_full, jnp.concatenate(pieces, axis=1)))
    first_full = first_full.reshape(width, projections + heads * DV)
    rest_full = lax.all_gather(rest, "seq", axis=0, tiled=True)
    out_full = first_full[:, projections:]
    behind = shifted(tokens[count - HALO :], "seq", 1)
    source = jnp.concatenate([behind, tokens], axis=0).astype(F32)
    normed_long = (source * rms_scale(source) * mixer_gain).astype(BF16)
    projected = mm(normed_long, first_full[:, :projections])

    taps = conv_weight.reshape(KW, heads * CONV)
    scales = jnp.pad(jnp.stack([decay_log, decay_bias]), ((0, 6), (0, LANES - heads)))
    queries, keys, values, inv, out_local, out_map, summary, normed_split = call(
        functools.partial(local_forward, heads, slab),
        [
            ((heads, count, DK), BF16),
            ((heads, count, DK), BF16),
            ((heads, count, DV), BF16),
            ((heads, count, count), F32),
            ((heads, count, DV), F32),
            ((heads, count, DK), F32),
            ((units, DK, 2 * DK), BF16),
            ((count, width), BF16),
        ],
        projected,
        taps,
        scales,
        normed_long,
        name="local_forward",
    )
    block = (DK, DK)
    double = (DK, 2 * DK)
    entering, normed_sibling, kept, totals = remote_call(
        functools.partial(scan_forward, groups),
        [((units, *block), BF16), ((count, width // 2), BF16), ((units, *block), BF16), ((groups, *block), BF16)],
        [
            pltpu.VMEM((units, *double), BF16),
            pltpu.VMEM((units, *double), F32),
            pltpu.VMEM(double, BF16),
            pltpu.VMEM((groups, *double), BF16),
            pltpu.VMEM((units, *block), BF16),
            pltpu.VMEM((units, *block), BF16),
            *pairs(units, groups, units, 1),
        ],
        1,
        summary,
        normed_split,
        name="scan_forward",
    )
    gain_row = out_gain.reshape(1, DV)
    mixer_out, gated = call(
        functools.partial(mix_outputs, heads),
        [((heads, count, DV), F32), ((count, heads * DV), BF16)],
        out_local,
        out_map,
        entering,
        projected,
        gain_row,
        name="mix_outputs",
    )
    branch = mmt(gated, out_full)
    def landing(*shape):
        return pltpu.VMEM((6, *shape), BF16)

    blocked = (sharers, rows, width)
    ring = [landing(rows // 2, width)]
    second, middle = remote_call(
        middle_kernel,
        [(blocked, BF16), ((rows, width), F32)],
        ring + pairs(6, 6),
        2,
        branch.astype(BF16).reshape(blocked),
        tokens.reshape(blocked),
        ffn_gain.reshape(1, width),
        name="middle",
    )
    second = second.reshape(count, width)
    gate_wide = heads * DV
    many = 4 * slab

    def sums_scratch(wide_1, wide_2):
        return [
            pltpu.VMEM((4, many, wide_1), BF16),
            pltpu.VMEM((4, many, wide_2), BF16),
            landing(many // 2, wide_1),
            landing(many // 2, wide_2),
            pltpu.VMEM((many, wide_1), BF16),
            pltpu.VMEM((many, wide_2), BF16),
            landing(slab // 2, wide_1),
            landing(slab // 2, wide_2),
        ]

    down_a = -(-hidden_units // (2 * LANES)) * LANES
    down_b = hidden_units - down_a
    chunk_count = len(chunks_of(hidden_units))
    in_vmem = pl.BlockSpec(memory_space=pltpu.VMEM)
    grad_branch, grad_middle, grad_ffn_gain, ffn_part, gate_up_part, grad_down_a, grad_down_b = pl.pallas_call(
        functools.partial(ffn_kernel, slab),
        in_specs=[in_vmem] * 4 + [anywhere],
        out_specs=[in_vmem] * 4 + [anywhere] + [in_vmem] * 2,
        out_shape=[
            jax.ShapeDtypeStruct(blocked, BF16),
            jax.ShapeDtypeStruct((rows, width), F32),
            jax.ShapeDtypeStruct((1, width), F32),
            jax.ShapeDtypeStruct(blocked, BF16),
            jax.ShapeDtypeStruct((4, many, 2 * hidden_units), BF16),
            jax.ShapeDtypeStruct((slab, down_a), F32),
            jax.ShapeDtypeStruct((slab, down_b), F32),
        ],
        scratch_shapes=[
            pltpu.VMEM((width, 3 * hidden_units), BF16),
            pltpu.VMEM((count, hidden_units), BF16),
            pltpu.VMEM((count, 2 * hidden_units), BF16),
            pltpu.VMEM((count, width), BF16),
            pltpu.VMEM((count, width), BF16),
            pltpu.VMEM((count, width // 2), BF16),
            pltpu.VMEM((count, width // 2), BF16),
            pltpu.VMEM((count, hidden_units), BF16),
            pltpu.VMEM((count, 2 * hidden_units), BF16),
            pltpu.VMEM((count, width), F32),
            pltpu.VMEM(blocked, BF16),
            *ring,
            pltpu.VMEM((4, many, 2 * hidden_units), BF16),
            *sums_scratch(down_a, down_b),
            pltpu.SemaphoreType.DMA((chunk_count,)),
            pltpu.SemaphoreType.DMA,
            *pairs(2, chunk_count, chunk_count, 6, 6, 6, 6, 6, 6),
        ],
        compiler_params=pltpu.CompilerParams(vmem_limit_bytes=VMEM_LIMIT, collective_id=3, has_side_effects=True),
        name="ffn",
    )(second, cotangent, middle, ffn_gain.reshape(1, width), rest_full)
    same_core = [[device for device in range(peers) if device % 2 == core] for core in range(2)]
    grad_gate_up_part = lax.psum_scatter(
        gate_up_part.reshape(width // 2, 2 * hidden_units), "seq", scatter_dimension=0, axis_index_groups=same_core, tiled=True
    )
    grad_branch = grad_branch.reshape(count, width)
    grad_gated = mm(grad_branch, out_full)
    grad_mixed, grad_gate, grad_out_gain, carried, branch_split = call(
        functools.partial(mix_outputs_back, heads, slab),
        [
            ((heads, count, DV), F32),
            ((count, heads * DV), BF16),
            ((1, DV), F32),
            ((units, DK, DK), BF16),
            ((count, width), BF16),
        ],
        grad_gated,
        mixer_out,
        out_map,
        projected,
        gain_row,
        grad_branch,
        name="mix_outputs_back",
    )
    leaving, branch_sibling, gated_sibling, gate_sibling = remote_call(
        functools.partial(scan_backward, groups),
        [
            ((units, *block), BF16),
            ((count, width // 2), BF16),
            ((count, heads * DV), BF16),
            ((count, heads * DV), BF16),
        ],
        [
            pltpu.VMEM((units, *block), BF16),
            pltpu.VMEM((units, *block), BF16),
            pltpu.VMEM((units, *block), F32),
            pltpu.VMEM((units, *block), F32),
            pltpu.VMEM(block, BF16),
            pltpu.VMEM((groups, *block), BF16),
            pltpu.VMEM((units, *block), BF16),
            pltpu.VMEM((units, *block), BF16),
            *pairs(units, groups, units, 3),
        ],
        4,
        carried,
        kept,
        totals,
        branch_split,
        gated,
        grad_gate,
        name="scan_backward",
    )
    grad_projected, grad_sibling, grad_taps, grad_scales, first_out, first_gate, output = remote_call(
        functools.partial(local_backward, heads, slab),
        [
            ((count, convolved_wide), BF16),
            ((count, convolved_wide), BF16),
            ((KW, heads * CONV), F32),
            ((8, LANES), F32),
            ((slab, gate_wide), F32),
            ((slab, gate_wide), F32),
            (blocked, BF16),
        ],
        [
            pltpu.VMEM((heads, HALO, CONV), F32),
            pltpu.VMEM((heads, HALO, CONV), F32),
            pltpu.VMEM((heads, 2 * HALO, CONV), F32),
            *sums_scratch(gate_wide, gate_wide),
            landing(rows // 2, width),
            pltpu.VMEM((rows, width), F32),
            *pairs(heads, heads, heads, 1, 6, 6, 6, 6, 6, 6),
        ],
        6,
        projected,
        taps,
        scales,
        queries,
        keys,
        values,
        inv,
        grad_mixed,
        entering,
        leaving,
        grad_gate,
        gate_sibling,
        gated,
        gated_sibling,
        normed_split,
        normed_sibling,
        branch_split,
        branch_sibling,
        ffn_part,
        middle,
        name="local_backward",
    )
    wide_a = -(-convolved_wide // (2 * LANES)) * LANES
    wide_b = convolved_wide - wide_a
    low, small, first_a, first_b = pl.pallas_call(
        functools.partial(last_kernel, slab),
        in_specs=[in_vmem] * 12 + [anywhere],
        out_specs=[in_vmem] * 4,
        out_shape=[
            jax.ShapeDtypeStruct(blocked, BF16),
            jax.ShapeDtypeStruct((8, width), F32),
            jax.ShapeDtypeStruct((slab, wide_a), F32),
            jax.ShapeDtypeStruct((slab, wide_b), F32),
        ],
        scratch_shapes=[
            pltpu.VMEM((width, projections), BF16),
            pltpu.VMEM((8, width), F32),
            pltpu.VMEM(blocked, BF16),
            landing(rows // 2, width),
            pltpu.VMEM((rows, width), F32),
            pltpu.VMEM((7, 8, width), F32),
            pltpu.VMEM((7, 8, width), F32),
            *sums_scratch(wide_a, wide_b),
            pltpu.SemaphoreType.DMA((width // 256,)),
            *pairs(6, 6, 7, 6, 6, 6, 6),
        ],
        compiler_params=pltpu.CompilerParams(vmem_limit_bytes=VMEM_LIMIT, collective_id=5, has_side_effects=True),
        name="last",
    )(
        grad_gate,
        tokens.reshape(blocked),
        grad_middle,
        mixer_gain.reshape(1, width),
        grad_ffn_gain,
        grad_out_gain,
        grad_scales,
        grad_taps,
        normed_split,
        normed_sibling,
        grad_projected,
        grad_sibling,
        first_full,
    )
    grad_in, grad_rate, grad_out, grad_gate_up_weight, grad_down, grad_tokens, grad_conv, *gains = call(
        functools.partial(finish_kernel, heads),
        [
            ((slab, heads, PROJ), F32),
            ((slab, 2, heads), F32),
            ((slab, heads, DV), F32),
            ((slab, 2, hidden_units), F32),
            ((slab, hidden_units), F32),
            ((count, width), F32),
            ((KW, heads, CONV), F32),
            ((width,), F32),
            ((width,), F32),
            ((DV,), F32),
        ],
        first_a,
        first_b,
        first_out,
        first_gate,
        grad_gate_up_part,
        grad_down_a,
        grad_down_b,
        low.reshape(count, width),
        small,
        name="finish",
    )
    return (
        output.reshape(count, width),
        grad_tokens,
        gains[0],
        grad_in,
        grad_rate,
        grad_conv,
        small[2, DV : DV + heads],
        small[2, DV + LANES : DV + LANES + heads],
        gains[2],
        grad_out,
        gains[1],
        grad_gate_up_weight,
        grad_down,
    )


def solution(mesh):
    in_specs = (
        P("seq", None),
        P(),
        P("seq", "head", None),
        P("seq", None, "head"),
        P(None, "head", None),
        P("head"),
        P("head"),
        P(),
        P("seq", "head", None),
        P(),
        P("seq", None, "head"),
        P("seq", "head"),
        P("seq", None),
    )
    out_specs = (
        P("seq", None),
        P("seq", None),
        P(),
        P("seq", "head", None),
        P("seq", None, "head"),
        P(None, "head", None),
        P("head"),
        P("head"),
        P(),
        P("seq", "head", None),
        P(),
        P("seq", None, "head"),
        P("seq", "head"),
    )
    return jax.shard_map(
        per_device, mesh=mesh, in_specs=in_specs, out_specs=out_specs, check_vma=False
    )
```

```python
import functools

import jax
import jax.numpy as jnp
from jax import lax
from jax.experimental import pallas as pl
from jax.experimental.pallas import tpu as pltpu
from jax.sharding import PartitionSpec as P

DK = 128
DV = 256
KW = 4
CONV = 512
PROJ = 768
LANES = 128
HALO = 16
HALVES = DV // DK
MESH = pl.DeviceIdType.MESH

F32 = jnp.float32
BF16 = jnp.bfloat16
EXACT = lax.Precision.HIGHEST
FINE = lax.Precision.HIGH
VMEM_LIMIT = 56 * 1024 * 1024


def dot(a, b, dims, precision=None):
    return lax.dot_general(a, b, (dims, ((), ())), precision=precision, preferred_element_type=F32)


def mm(a, b, precision=None):
    return dot(a, b, ((1,), (0,)), precision)


def mmt(a, b, precision=None):
    return dot(a, b, ((1,), (1,)), precision)


def mtm(a, b, precision=None):
    return dot(a, b, ((0,), (0,)), precision)


def iota(shape, dim):
    return lax.broadcasted_iota(jnp.int32, shape, dim)


def softplus(x):
    return jnp.maximum(x, 0.0) + jnp.log1p(jnp.exp(-jnp.abs(x)))


def split_by_core(values, slab):
    width = values.shape[1]
    lanes = iota((values.shape[0], 2 * slab), 1)
    firsts, seconds = [], []
    for at in range(0, width, 4 * slab):
        a, b = values[:, at : at + 2 * slab], values[:, at + 2 * slab : at + 4 * slab]
        firsts.append(jnp.where(lanes < slab, a, pltpu.roll(b, slab, 1)))
        seconds.append(jnp.where(lanes < slab, pltpu.roll(a, slab, 1), b))
    return jnp.concatenate(firsts + seconds, axis=1)


def column(block, index):
    lanes = iota(block.shape, 1)
    return jnp.sum(jnp.where(lanes == index, block, 0.0), axis=1, keepdims=True)


def triangles(size):
    rows, columns = iota((size, size), 0), iota((size, size), 1)
    return rows, columns


def gates(rates, scales, head, heads):
    size = rates.shape[0]
    log_rate, bias = scales[0][head], scales[1][head]
    pre = column(rates, head) + bias
    beta = jax.nn.sigmoid(column(rates, heads + head))
    decay = -jnp.exp(jnp.full((1, 1), log_rate, F32)) * softplus(pre)
    rows, columns = triangles(size)
    below = (columns <= rows).astype(F32)
    gamma_wide = mm(below, jnp.broadcast_to(decay, (size, LANES)), EXACT)
    gamma = gamma_wide[:, 0:1]
    gamma_row = gamma_wide.T[0:1, :]
    return beta, decay, gamma, gamma_row, pre


def decays_of(gamma, gamma_row):
    size = gamma.shape[0]
    rows, columns = triangles(size)
    inside = columns <= rows
    return jnp.where(inside, jnp.exp(jnp.where(inside, gamma - gamma_row, 0.0)), 0.0)


def inverse(lower, between):
    size = lower[0].shape[0]
    rows, columns = triangles(size)
    unit = (rows == columns).astype(F32)
    known = [unit - jnp.where(rows // 2 == columns // 2, a, 0.0) for a in lower]
    width = 2
    while width < size:
        fresh = (rows // (2 * width) == columns // (2 * width)) & (rows // width != columns // width)
        parts = [jnp.where(fresh, a, 0.0) for a in lower]
        first = [mm(c, x, FINE) for c, x in zip(parts, known)]
        known = [x - mm(x, y, FINE) for x, y in zip(known, first)]
        width *= 2
        between(width)
    return known


def convolved(extended, taps):
    total = None
    for j in range(KW):
        shift = KW - 1 - j
        moved = extended if shift == 0 else pltpu.roll(extended, shift, 0)
        term = taps[j : j + 1] * moved[HALO:]
        total = term if total is None else total + term
    return total


def unit_rows(values):
    return lax.rsqrt(jnp.sum(values * values, axis=-1, keepdims=True) + 1e-06)


def mixer_inputs(projected, taps):
    extended = projected[:, :CONV].astype(BF16).astype(F32)
    mixed = convolved(extended, taps)
    gate = jax.nn.sigmoid(mixed)
    active = mixed * gate
    q_raw, k_raw = active[:, :DK], active[:, DK : 2 * DK]
    q_scale, k_scale = unit_rows(q_raw), unit_rows(k_raw)
    queries = (q_raw * q_scale * DK ** (-0.5)).astype(BF16)
    keys = (k_raw * k_scale).astype(BF16)
    values = active[:, 2 * DK :].astype(BF16)
    return extended, mixed, gate, (q_raw, q_scale), (k_raw, k_scale), queries, keys, values


def gate_columns(heads, head):
    at = heads * CONV + LANES + head * DV
    return pl.ds(at, DV)


def whole_state(units_ref, head):
    return jnp.concatenate([units_ref[HALVES * head + half] for half in range(HALVES)], axis=1).astype(F32)


def weight_blocks(x, x_sib, y, y_sib, columns, target, slab, z_first):
    places = target.shape[0]
    many = places * slab
    own = lax.axis_index("seq") % 2 * (x.shape[1] // 2)

    @pl.loop(0, places)
    def _(block):
        at = pl.ds(pl.multiple_of(own + block * many, many), many)
        here = pl.ds(pl.multiple_of(block * many, many), many)
        part = (mtm(x[:, at], y[:, columns]) + mtm(x_sib[:, here], y_sib[:, columns])).astype(BF16)
        if z_first:
            rows = pl.ds(pl.multiple_of(block * slab, slab), slab)
            for place in range(places):
                target[place, rows] = part[place * slab : (place + 1) * slab]
        else:
            target[block] = part


def sum_both(first, second, part, middle, result, landing, landing_2, semaphores):
    places, many, wide = part.shape
    yield from ring_reduce(first, part, middle, landing, semaphores[0], semaphores[1])
    blocks = middle.reshape(places, many // places, wide)
    yield from ring_reduce(second, blocks, result, landing_2, semaphores[2], semaphores[3])


def norm_back(grad, values, scale):
    return scale * grad - values * (scale * scale * scale * jnp.sum(values * grad, axis=-1, keepdims=True))


def say_here(peers):
    barrier = pltpu.get_barrier_semaphore()
    for peer in peers:
        pl.semaphore_signal(barrier, inc=1, device_id=peer, device_id_type=MESH)

    def all_here():
        pl.semaphore_wait(barrier, len(peers))

    return all_here


def start_barrier(peers):
    say_here(peers)()


def send(source, target, sends, receives, slot, peer):
    copy = pltpu.make_async_remote_copy(
        src_ref=source,
        dst_ref=target,
        send_sem=sends.at[slot],
        recv_sem=receives.at[slot],
        device_id=peer,
        device_id_type=MESH,
    )
    copy.start()
    return copy


def twice(left, right):
    high = right.astype(BF16)
    low = (right - high.astype(F32)).astype(BF16)
    return mm(left, high) + mm(left, low)


def scan_places(members, groups):
    seq, head = lax.axis_index("seq"), lax.axis_index("head")
    member, group = seq % members, seq // members
    near = [(member + d) % members for d in range(members)]
    far = [(group + d) % groups for d in range(groups)]
    near_ids = [(group * members + place, head) for place in near]
    far_ids = [(place * members + member, head) for place in far]
    return member, group, near, near_ids, far_ids


def other_half(ref):
    half = ref.shape[1] // 2
    at = (1 - lax.axis_index("seq") % 2) * half
    return ref.at[:, pl.ds(pl.multiple_of(at, half), half)]


def ring_ids(axis):
    seq, head = lax.axis_index("seq"), lax.axis_index("head")
    size = {"x": lax.axis_size("seq") // 8, "y": lax.axis_size("head"), "z": 4}[axis]
    me = {"x": seq // 8, "y": head, "z": (seq // 2) % 4}[axis]

    def at(place):
        if axis == "y":
            return (seq, place)
        if axis == "x":
            return (place * 8 + seq % 8, head)
        return ((seq // 8) * 8 + place * 2 + seq % 2, head)

    right, left = lax.rem(me + 1, size), lax.rem(me + size - 1, size)
    return me, right, left, lax.rem(me + 2, size), at(right), at(left)


def add_into(target, pieces, rows):
    step = min(rows, 32)

    @pl.loop(0, rows // step)
    def _(k):
        part = pl.ds(pl.multiple_of(k * step, step), step)
        total = pieces[0][part].astype(F32)
        for piece in pieces[1:]:
            total = total + piece[part].astype(F32)
        target[part] = total.astype(target.dtype)


def ring_reduce(ring, blocks, result, landing, sends, receives):
    me, right, left, across, right_id, left_id = ring
    rows = blocks.shape[1]
    half = rows // 2
    upper, lower = pl.ds(0, half), pl.ds(half, half)
    by_right = send(blocks.at[across, upper], landing.at[0], sends, receives, 0, right_id)
    by_left = send(blocks.at[across, lower], landing.at[1], sends, receives, 1, left_id)
    plain_right = send(blocks.at[right, lower], landing.at[2], sends, receives, 2, right_id)
    plain_left = send(blocks.at[left, upper], landing.at[3], sends, receives, 3, left_id)
    yield
    by_right.wait()
    add_into(landing.at[0], [blocks.at[right, upper], landing.at[0]], half)
    summed_right = send(landing.at[0], landing.at[4], sends, receives, 4, right_id)
    by_left.wait()
    add_into(landing.at[1], [blocks.at[left, lower], landing.at[1]], half)
    summed_left = send(landing.at[1], landing.at[5], sends, receives, 5, left_id)
    yield
    plain_right.wait()
    plain_left.wait()
    summed_right.wait()
    summed_left.wait()
    add_into(result.at[upper], [blocks.at[me, upper], landing.at[4], landing.at[3]], half)
    add_into(result.at[lower], [blocks.at[me, lower], landing.at[2], landing.at[5]], half)


def ring_gather(ring, blocks, sends, receives):
    me, right, left, across, right_id, left_id = ring
    rows = blocks.shape[1]
    half = rows // 2
    upper, lower = pl.ds(0, half), pl.ds(half, half)

    def go(place, part, slot, peer):
        return send(blocks.at[place, part], blocks.at[place, part], sends, receives, slot, peer)

    upper_right = go(me, upper, 0, right_id)
    lower_left = go(me, lower, 1, left_id)
    lower_right = go(me, lower, 2, right_id)
    upper_left = go(me, upper, 3, left_id)
    yield
    upper_right.wait()
    far_right = go(left, upper, 4, right_id)
    lower_left.wait()
    far_left = go(right, lower, 5, left_id)
    yield
    for copy in (lower_right, upper_left, far_right, far_left):
        copy.wait()


def finish(*generators):
    active = list(generators)
    while active:
        active = [g for g in active if next(g, active) is not active]


def rms_scale(values):
    return lax.rsqrt(jnp.mean(values * values, axis=-1, keepdims=True) + 1e-05)


def rms_back(grad, values, gain):
    scale = rms_scale(values)
    u = grad * gain
    back = scale * u - values * (scale * scale * scale * jnp.mean(u * values, axis=-1, keepdims=True))
    return back, jnp.sum(grad * values * scale, axis=0, keepdims=True)


def backward_kernel(
    heads, slab, groups, branch_ref, out_weight_ref, mixed_ref, map_ref, proj_ref, gain_ref, gated_ref, taps_ref, log_ref, bias_ref,
    normed_split_ref, normed_sib_ref, kept_ref, totals_ref, state_ref, q_ref, k_ref, v_ref, inv_ref, ffn_part_ref, middle_ref,
    out_ref, sibling_ref, gate_ref, gain_out_ref, taps_out_ref, scales_out_ref, first_out_ref, first_gate_ref, output_ref,
    out_weight, branch_split, branch_sib, gated_sib, gate_sib, grad_outs, pack, near_in, turned, before, after, far_out, far_in,
    back_out, back_in, spreads, residuals, writtens, grad_scores_all, partial, halo_out, halo_in, tails,
    part_o, part_g, land_o, land_g, mid_o, mid_g, land_o2, land_g2, land_f, sum_f,
    load_s, core_s, core_r, near_s, near_r, far_s, far_r, back_s, back_r, halo_s, halo_r, body_s, body_r, tail_s, tail_r,
    rate_s, rate_r, o1_s, o1_r, g1_s, g1_r, o2_s, o2_r, g2_s, g2_r, rf_s, rf_r, gf_s, gf_r,
):
    size = proj_ref.shape[0] - HALO
    seq, head_place = lax.axis_index("seq"), lax.axis_index("head")
    peers = lax.axis_size("seq")
    members = pack.shape[0]
    member, group, near, near_ids, far_ids = scan_places(members, groups)
    ring_x, ring_y, ring_z = ring_ids("x"), ring_ids("y"), ring_ids("z")
    previous, following = (lax.rem(seq + peers - 1, peers), head_place), (lax.rem(seq + 1, peers), head_place)
    sibling = (seq + 1 - 2 * (seq % 2), head_place)
    all_here = say_here([*near_ids[1:], *far_ids[1:], *ring_y[4:], previous, following])
    load = pltpu.make_async_copy(out_weight_ref, out_weight, load_s)
    load.start()
    branch_split[...] = split_by_core(branch_ref[...].astype(F32), slab).astype(BF16)
    all_here()
    first_aside = [
        send(other_half(branch_split), branch_sib, core_s, core_r, 0, sibling),
        send(gated_ref, gated_sib, core_s, core_r, 1, sibling),
    ]

    def output_sum():
        yield from ring_reduce(ring_y, ffn_part_ref, sum_f, land_f, rf_s, rf_r)
        output_ref[ring_y[0]] = (middle_ref[...] + sum_f[...]).astype(BF16)
        yield from ring_gather(ring_y, output_ref, gf_s, gf_r)

    output = output_sum()
    next(output)
    gain = gain_ref[...]
    gain_total = jnp.zeros_like(gain)
    load.wait()
    for h in range(heads):
        columns = slice(h * DV, (h + 1) * DV)
        grad = mm(branch_ref[...], out_weight[:, columns])
        mixer_out = mixed_ref[h]
        z = proj_ref[HALO:, gate_columns(heads, h)]
        scale = lax.rsqrt(jnp.mean(mixer_out * mixer_out, axis=-1, keepdims=True) + 1e-05)
        normal = mixer_out * scale
        s = jax.nn.sigmoid(z)
        silu = z * s
        gain_total = gain_total + jnp.sum(grad * normal * silu, axis=0, keepdims=True)
        gate_ref[:, columns] = (grad * normal * gain * s * (1.0 + z * (1.0 - s))).astype(BF16)
        u = grad * gain * silu
        grad_outs[h] = scale * u - normal * (scale * jnp.mean(u * normal, axis=-1, keepdims=True))
        carried = mtm(map_ref[h], grad_outs[h], FINE).astype(BF16)
        for half in range(HALVES):
            pack[HALVES * h + half] = carried[:, half * DK : (half + 1) * DK]
    gain_out_ref[...] = gain_total
    copies = [send(pack.at[near[d]], near_in.at[member], near_s, near_r, d, near_ids[d]) for d in range(1, members)]
    gate_aside = send(gate_ref, gate_sib, core_s, core_r, 2, sibling)
    near_in[member] = pack[member]
    for copy in first_aside:
        copy.wait()
    weight_blocks(branch_split, branch_sib, gated_ref, gated_sib, pl.ds(0, part_o.shape[2]), part_o, slab, False)
    sum_o = sum_both(ring_x, ring_z, part_o, mid_o, first_out_ref, land_o, land_o2, (o1_s, o1_r, o2_s, o2_r))
    next(sum_o)
    passed = (iota((DK, DK), 0) == iota((DK, DK), 1)).astype(F32)
    for j in reversed(range(members)):
        turned[j] = kept_ref[j].astype(F32).T.astype(BF16)
        before[j] = passed
        passed = twice(turned[j], passed)
    for copy in copies:
        copy.wait()
    total = jnp.zeros((DK, DK), F32)
    for j in reversed(range(members)):
        after[j] = total
        total = twice(turned[j], total) + near_in[j].astype(F32)
    far_out[...] = total.astype(BF16)
    copies = [send(far_out, far_in.at[group], far_s, far_r, d, far_ids[d]) for d in range(1, groups)]
    far_in[group] = far_out[...]

    rows, columns = triangles(size)
    strict = columns < rows
    rates = proj_ref[HALO:, heads * CONV : heads * CONV + LANES]
    scales = (log_ref, bias_ref)

    def without_leaving(h):
        kf = k_ref[h].astype(F32)
        beta, _, gamma, gamma_row, _ = gates(rates, scales, h, heads)
        spread = decays_of(gamma, gamma_row)
        spreads[h] = spread
        residual = v_ref[h].astype(F32) - jnp.exp(gamma) * mm(kf, whole_state(state_ref, h), FINE)
        residuals[h] = residual
        written = mm(inv_ref[h], beta * residual, FINE)
        writtens[h] = written
        grad_scores_all[h] = mmt(grad_outs[h], written, FINE)
        partial[h] = mtm(spread * mmt(q_ref[h], k_ref[h]), grad_outs[h], FINE)

    without_leaving(0)
    gate_aside.wait()
    weight_blocks(normed_split_ref, normed_sib_ref, gate_ref, gate_sib, pl.ds(0, part_g.shape[2]), part_g, slab, True)
    sum_g = sum_both(ring_z, ring_x, part_g, mid_g, first_gate_ref, land_g, land_g2, (g1_s, g1_r, g2_s, g2_r))
    next(sum_g)
    turned_totals = [totals_ref[j].astype(F32).T.astype(BF16) for j in range(groups)]
    for copy in copies:
        copy.wait()
    state = jnp.zeros((DK, DK), F32)
    for j in reversed(range(groups)):
        fresh = twice(turned_totals[j], state) + far_in[j].astype(F32)
        state = jnp.where(j > group, fresh, state)
    for j in range(members):
        back_out[j] = (mm(before[j], state, FINE) + after[j]).astype(BF16)
    copies = [send(back_out.at[near[d]], back_in.at[member], back_s, back_r, d, near_ids[d]) for d in range(1, members)]
    back_in[member] = back_out[member]
    next(output)
    without_leaving(1)
    next(sum_o)
    without_leaving(2)
    next(output)
    without_leaving(3)
    next(sum_g)
    for copy in copies:
        copy.wait()

    lanes = iota((size, LANES), 1)
    grad_rates = jnp.zeros((size, LANES), F32)
    rates_total = jnp.zeros((8, LANES), F32)
    row8, lane8 = iota((8, LANES), 0), iota((8, LANES), 1)
    ones = jnp.ones((size, LANES), F32)
    above = (columns >= rows).astype(F32)
    body = size - HALO
    copies = []
    beside = {0: [sum_o], 1: [sum_g, output], 2: [sum_o], 3: [sum_g]}
    for h in range(heads):
        queries, keys = q_ref[h], k_ref[h]
        qf, kf = queries.astype(F32), keys.astype(F32)
        beta, decay, gamma, _, pre = gates(rates, scales, h, heads)
        spread, residual, written, grad_scores = spreads[h], residuals[h], writtens[h], grad_scores_all[h]
        growth = jnp.exp(gamma)
        final = gamma[size - 1 : size]
        fade = jnp.exp(final - gamma)
        state, leaving = whole_state(state_ref, h), whole_state(back_in, h)
        inv, grad = inv_ref[h], grad_outs[h]
        products = mmt(keys, keys)
        scores = spread * mmt(queries, keys)
        lower = jnp.where(strict, beta * spread * products, 0.0)
        faded = fade * kf
        grad_written = partial[h] + mm(faded, leaving, FINE)
        grad_targets = mtm(inv, grad_written, FINE)
        grad_lower = jnp.where(strict, -mmt(grad_targets, written, FINE), 0.0)
        grad_values = beta * grad_targets
        grad_beta = jnp.sum(grad_targets * residual, axis=-1, keepdims=True)
        grad_beta = grad_beta + jnp.sum(grad_lower * spread * products, axis=-1, keepdims=True)
        q_first = growth * mmt(grad, state, FINE)
        k_first = -growth * mmt(grad_values, state, FINE)
        spread_scores = spread * grad_scores
        spread_lower = grad_lower * beta * spread
        grad_faded = mmt(written, leaving, FINE)
        grad_queries = q_first + mm(spread_scores, kf, FINE)
        grad_keys = (
            k_first
            + mtm(spread_scores, qf, FINE)
            + mm(spread_lower, kf, FINE)
            + mtm(spread_lower, kf, FINE)
            + fade * grad_faded
        )
        energy = grad_scores * scores + grad_lower * lower
        fading = jnp.sum(grad_faded * faded, axis=-1, keepdims=True)
        grad_gamma = jnp.sum(qf * q_first + kf * k_first, axis=-1, keepdims=True) - fading
        grad_gamma = grad_gamma + jnp.sum(energy, axis=-1, keepdims=True)
        at_end = jnp.sum(fading, axis=0, keepdims=True) + jnp.exp(final) * jnp.sum(
            jnp.sum(state * leaving, axis=1, keepdims=True), axis=0, keepdims=True
        )
        grad_gamma = grad_gamma + jnp.where(iota((size, 1), 0) == size - 1, at_end, 0.0)
        wide = jnp.broadcast_to(grad_gamma, (size, LANES)) - mtm(energy, ones, EXACT)
        grad_decay = mm(above, wide, EXACT)[:, 0:1]

        projected = proj_ref[:, h * CONV : (h + 1) * CONV]
        taps = taps_ref[:, h]
        extended, mixed, gate, (q_raw, q_scale), (k_raw, k_scale), *_ = mixer_inputs(projected, taps)
        grad_active = jnp.concatenate(
            [
                norm_back(grad_queries * DK ** (-0.5), q_raw, q_scale),
                norm_back(grad_keys, k_raw, k_scale),
                grad_values,
            ],
            axis=1,
        )
        grad_mixed = grad_active * gate * (1.0 + mixed * (1.0 - gate))
        padding = jnp.zeros((HALO, CONV), F32)
        full = jnp.concatenate([padding, grad_mixed, padding], axis=0)
        total = None
        for j in range(KW):
            shift = KW - 1 - j
            moved = full if shift == 0 else pltpu.roll(full, size + 2 * HALO - shift, 0)
            term = taps[j : j + 1] * moved[: size + HALO]
            total = term if total is None else total + term
            back = extended if shift == 0 else pltpu.roll(extended, shift, 0)
            taps_out_ref[j : j + 1, h * CONV : (h + 1) * CONV] = jnp.sum(
                grad_mixed * back[HALO:], axis=0, keepdims=True
            )
        halo_out[h] = total[:HALO]
        tails[h] = total[size:]
        out_ref[:, h * CONV : (h + 1) * CONV] = total[HALO:].astype(BF16)
        copies.append(send(halo_out.at[h], halo_in.at[h], halo_s, halo_r, h, previous))
        upper = (pl.ds(0, body), pl.ds(h * CONV, CONV))
        copies.append(send(out_ref.at[upper], sibling_ref.at[upper], body_s, body_r, h, sibling))
        for stage in beside[h]:
            next(stage)

        grad_pre = -jnp.exp(jnp.full((1, 1), log_ref[h], F32)) * jax.nn.sigmoid(pre) * grad_decay
        grad_strength = grad_beta * beta * (1.0 - beta)
        grad_rates = grad_rates + jnp.where(lanes == h, grad_pre, 0.0)
        grad_rates = grad_rates + jnp.where(lanes == heads + h, grad_strength, 0.0)
        log_total = jnp.sum(grad_decay * decay, axis=0, keepdims=True)
        bias_total = jnp.sum(grad_pre, axis=0, keepdims=True)
        rates_total = rates_total + jnp.where((row8 == 0) & (lane8 == h), log_total, 0.0)
        rates_total = rates_total + jnp.where((row8 == 1) & (lane8 == h), bias_total, 0.0)
    out_ref[:, heads * CONV :] = grad_rates.astype(BF16)
    scales_out_ref[...] = rates_total
    side = (pl.ds(0, size), pl.ds(heads * CONV, LANES))
    last = [send(out_ref.at[side], sibling_ref.at[side], rate_s, rate_r, 0, sibling)]
    for copy in copies:
        copy.wait()
    for h in range(heads):
        arrived = jnp.where(seq < peers - 1, halo_in[h], 0.0)
        fixed = tails[h] + arrived
        out_ref[body:, h * CONV : (h + 1) * CONV] = fixed.astype(BF16)
        lower = (pl.ds(body, HALO), pl.ds(h * CONV, CONV))
        last.append(send(out_ref.at[lower], sibling_ref.at[lower], tail_s, tail_r, h, sibling))
    for copy in last:
        copy.wait()
    finish(output, sum_o, sum_g)


def chunks_of(units):
    return [(at, min(2 * LANES, units - at)) for at in range(0, units, 2 * LANES)]


def ffn_kernel(
    slab, second_ref, cotangent_ref, middle_ref, gain_ref, weights_ref,
    branch_ref, grad_ref, grad_gain_ref, ffn_ref, gate_up_ref, down_a_ref, down_b_ref,
    weights, hidden, grad_hidden, second_split, cotangent_split, second_sib, cotangent_sib, hidden_sib, grad_sib,
    total, part, landing, gate_up_part, part_a, part_b, land_a, land_b, mid_a, mid_b, land_a2, land_b2,
    load_s, store_s, half_s, half_r, hid_s, hid_r, gra_s, gra_r, red_s, red_r, gat_s, gat_r,
    a1_s, a1_r, b1_s, b1_r, a2_s, a2_r, b2_s, b2_r,
):
    seq, head = lax.axis_index("seq"), lax.axis_index("head")
    ring_x, ring_y, ring_z = ring_ids("x"), ring_ids("y"), ring_ids("z")
    sibling = (seq + 1 - 2 * (seq % 2), head)
    all_here = say_here(ring_x[4:] + ring_y[4:] + ring_z[4:] + (sibling,))
    count, width = second_ref.shape
    chunks = chunks_of(hidden.shape[1])
    loads = []
    for i, (at, length) in enumerate(chunks):
        columns = pl.ds(3 * at, 3 * length)
        loads.append(pltpu.make_async_copy(weights_ref.at[:, columns], weights.at[:, columns], load_s.at[i]))
        loads[-1].start()
    second_split[...] = split_by_core(second_ref[...].astype(F32), slab).astype(BF16)
    cotangent_split[...] = split_by_core(cotangent_ref[...].astype(F32), slab).astype(BF16)
    all_here()
    aside = [
        send(other_half(second_split), second_sib, half_s, half_r, 0, sibling),
        send(other_half(cotangent_split), cotangent_sib, half_s, half_r, 1, sibling),
    ]
    step = 256
    for i, (at, length) in enumerate(chunks):
        loads[i].wait()
        gate, up, down = (pl.ds(3 * at + k * length, length) for k in range(3))
        z = mm(second_ref[...], weights[:, gate])
        u = mm(second_ref[...], weights[:, up])
        g = mm(cotangent_ref[...], weights[:, down])
        s = jax.nn.sigmoid(z)
        silu = z * s
        here, both = pl.ds(at, length), pl.ds(2 * at, 2 * length)
        hidden[:, here] = (silu * u).astype(BF16)
        grad_hidden[:, pl.ds(2 * at, length)] = (g * u * s * (1.0 + z * (1.0 - s))).astype(BF16)
        grad_hidden[:, pl.ds(2 * at + length, length)] = (g * silu).astype(BF16)
        aside.append(send(hidden.at[:, here], hidden_sib.at[:, here], hid_s, hid_r, i, sibling))
        aside.append(send(grad_hidden.at[:, both], grad_sib.at[:, both], gra_s, gra_r, i, sibling))

        @pl.loop(0, width // step)
        def _(k, at=at, length=length, both=both, i=i):
            rows = pl.ds(pl.multiple_of(k * step, step), step)
            product = mmt(grad_hidden[:, both], weights[rows, pl.ds(3 * at, 2 * length)])
            if i == 0:
                total[:, rows] = product
            elif i < len(chunks) - 1:
                total[:, rows] += product
            else:
                full = total[:, rows] + product
                for p in range(part.shape[0]):
                    n = part.shape[1]
                    part[p, :, rows] = full[p * n : (p + 1) * n].astype(BF16)

    reduce = ring_reduce(ring_y, part, grad_ref, landing, red_s, red_r)
    next(reduce)
    for copy in aside:
        copy.wait()
    wide_a, wide_b = part_a.shape[2], part_b.shape[2]
    weight_blocks(cotangent_split, cotangent_sib, hidden, hidden_sib, pl.ds(0, wide_a), part_a, slab, False)
    sum_a = sum_both(ring_x, ring_z, part_a, mid_a, down_a_ref, land_a, land_a2, (a1_s, a1_r, a2_s, a2_r))
    next(sum_a)
    weight_blocks(cotangent_split, cotangent_sib, hidden, hidden_sib, pl.ds(wide_a, wide_b), part_b, slab, True)
    sum_b = sum_both(ring_z, ring_x, part_b, mid_b, down_b_ref, land_b, land_b2, (b1_s, b1_r, b2_s, b2_r))
    next(sum_b)
    next(reduce)

    @pl.loop(0, width // step)
    def _(k):
        rows = pl.ds(pl.multiple_of(k * step, step), step)
        product = None
        for at, length in chunks:
            term = mmt(hidden[:, pl.ds(at, length)], weights[rows, pl.ds(3 * at + 2 * length, length)])
            product = term if product is None else product + term
        for p in range(ffn_ref.shape[0]):
            n = ffn_ref.shape[1]
            ffn_ref[p, :, rows] = product[p * n : (p + 1) * n].astype(BF16)

    finish(reduce)
    back, grad_gain = rms_back(grad_ref[...], middle_ref[...], gain_ref[...])
    grad = cotangent_ref[pl.ds(pl.multiple_of(ring_y[0] * slab, slab), slab)].astype(F32) + back
    branch_ref[ring_y[0]] = grad.astype(BF16)
    gather = ring_gather(ring_y, branch_ref, gat_s, gat_r)
    next(gather)
    grad_ref[...] = grad
    grad_gain_ref[...] = grad_gain
    next(sum_a)
    next(sum_b)
    weight_blocks(
        second_split, second_sib, grad_hidden, grad_sib, pl.ds(0, grad_hidden.shape[1]), gate_up_part, slab, False
    )
    store = pltpu.make_async_copy(gate_up_part, gate_up_ref, store_s)
    store.start()
    next(gather)
    next(sum_a)
    next(sum_b)
    finish(gather, sum_a, sum_b)
    store.wait()


def swap_add(value, partner, outgoing, incoming, sends, receives, slot, mask=None):
    outgoing[slot] = value
    copy = send(outgoing.at[slot], incoming.at[slot], sends, receives, slot, partner)
    yield
    copy.wait()
    other = incoming[slot]
    return value + (other if mask is None else jnp.where(mask, other, 0.0))


def last_kernel(
    slab, gate_ref, tokens_ref, middle_grad_ref, gain_ref, ffn_gain_ref, out_gain_ref, scales_ref, taps_ref,
    split_ref, split_sib_ref, proj_ref, proj_sib_ref, weights_ref,
    low_ref, small_out_ref, late_out_ref, first_a_ref, first_b_ref,
    weights, small_ref, late_ref, part_n, land_n, sum_n, swap_out, swap_in, late_out, late_in, part_a, part_b, land_a, land_b, mid_a, mid_b, land_a2, land_b2,
    load_s, rn_s, rn_r, gn_s, gn_r, sw_s, sw_r, la_s, la_r, a1_s, a1_r, b1_s, b1_r, a2_s, a2_r, b2_s, b2_r,
):
    seq, head = lax.axis_index("seq"), lax.axis_index("head")
    ring_x, ring_y, ring_z = ring_ids("x"), ring_ids("y"), ring_ids("z")
    sibling = (seq + 1 - 2 * (seq % 2), head)
    all_here = say_here(ring_x[4:] + ring_y[4:] + ring_z[4:] + (sibling,))
    width, wide = weights.shape
    step = 256

    def load(k):
        rows = pl.ds(pl.multiple_of(k * step, step), step)
        return pltpu.make_async_copy(weights_ref.at[rows, pl.ds(0, wide)], weights.at[rows], load_s.at[k])

    for k in range(width // step):
        load(k).start()
    small_ref[...] = jnp.zeros_like(small_ref)
    small_ref[1:2] = ffn_gain_ref[...]
    small_ref[2:3, :DV] = out_gain_ref[...]
    small_ref[2:3, DV : DV + LANES] = scales_ref[0:1]
    small_ref[2:3, DV + LANES : DV + 2 * LANES] = scales_ref[1:2]
    small_ref[3 : 3 + KW] = taps_ref[...]
    me = ring_y[0]
    wide_a, wide_b = part_a.shape[2], part_b.shape[2]
    narrow = proj_ref.shape[1]
    all_here()

    def all_small(value, mask, outgoing, incoming, sends, receives, result):
        slot = 0
        for ring, only in ((ring_y, mask), (ring_x, None), (ring_z, None)):
            place, right_id, left_id = ring[0], ring[4], ring[5]
            even = lax.rem(place, 2) == 0
            for flip in (False, True):
                ids = tuple(jnp.where(jnp.logical_xor(even, flip), r, l) for r, l in zip(right_id, left_id))
                value = yield from swap_add(value, ids, outgoing, incoming, sends, receives, slot, only)
                slot += 1
        value = yield from swap_add(value, sibling, outgoing, incoming, sends, receives, slot)
        result[...] = value

    rows8, lanes = iota(small_ref.shape, 0), iota(small_ref.shape, 1)
    shared = (rows8 < 2) | ((rows8 == 2) & (lanes < DV))
    small = all_small(small_ref[...], shared, swap_out, swap_in, sw_s, sw_r, small_out_ref)
    next(small)

    @pl.loop(0, width // step)
    def _(k):
        load(k).wait()
        rows = pl.ds(pl.multiple_of(k * step, step), step)
        product = mmt(proj_ref[...], weights[rows, :narrow]) + mmt(gate_ref[...], weights[rows, narrow:])
        for p in range(part_n.shape[0]):
            n = part_n.shape[1]
            part_n[p, :, rows] = product[p * n : (p + 1) * n].astype(BF16)

    reduce_n = ring_reduce(ring_y, part_n, sum_n, land_n, rn_s, rn_r)
    next(reduce_n)
    weight_blocks(split_ref, split_sib_ref, proj_ref, proj_sib_ref, pl.ds(0, wide_a), part_a, slab, False)
    sum_a = sum_both(ring_x, ring_z, part_a, mid_a, first_a_ref, land_a, land_a2, (a1_s, a1_r, a2_s, a2_r))
    next(sum_a)
    next(small)
    weight_blocks(split_ref, split_sib_ref, proj_ref, proj_sib_ref, pl.ds(wide_a, wide_b), part_b, slab, True)
    sum_b = sum_both(ring_z, ring_x, part_b, mid_b, first_b_ref, land_b, land_b2, (b1_s, b1_r, b2_s, b2_r))
    next(sum_b)
    next(reduce_n)
    next(small)
    finish(reduce_n)
    back, grad_gain = rms_back(sum_n[...], tokens_ref[me].astype(F32), gain_ref[...])
    low_ref[me] = (middle_grad_ref[...] + back).astype(BF16)
    gather_n = ring_gather(ring_y, low_ref, gn_s, gn_r)
    next(gather_n)
    wide_late = late_ref.shape[1]
    for r in range(late_ref.shape[0]):
        late_ref[r : r + 1] = grad_gain[:, r * wide_late : (r + 1) * wide_late]
    late = all_small(late_ref[...], None, late_out, late_in, la_s, la_r, late_out_ref)
    next(late)
    next(sum_a)
    next(sum_b)
    next(small)
    next(late)
    next(gather_n)
    next(late)
    next(small)
    next(sum_a)
    next(sum_b)
    next(late)
    next(small)
    next(late)
    next(sum_a)
    next(sum_b)
    finish(late, small, gather_n, sum_a, sum_b)


def finish_kernel(
    heads, first_a_ref, first_b_ref, first_out_ref, first_gate_ref, gate_up_in_ref, down_a_ref, down_b_ref, low_ref, small_ref, late_ref,
    in_ref, rate_ref, out_ref, gate_up_ref, down_ref, tokens_ref, taps_ref, mixer_gain_ref, ffn_gain_ref, out_gain_ref,
):
    both = jnp.concatenate([first_a_ref[...], first_b_ref[...]], axis=1)
    for h in range(heads):
        in_ref[:, h, :CONV] = both[:, h * CONV : (h + 1) * CONV]
        in_ref[:, h, CONV:] = first_gate_ref[:, h * DV : (h + 1) * DV]
        out_ref[:, h] = first_out_ref[:, h * DV : (h + 1) * DV]
        taps_ref[:, h] = small_ref[3 : 3 + KW, h * CONV : (h + 1) * CONV]
    rates = heads * CONV
    for g in range(2):
        rate_ref[:, g] = both[:, rates + g * heads : rates + (g + 1) * heads]
    for at, length in chunks_of(down_ref.shape[1]):
        for g in range(2):
            gate_up_ref[:, g, at : at + length] = gate_up_in_ref[:, pl.ds(2 * at + g * length, length)].astype(F32)
    down_ref[:, : down_a_ref.shape[1]] = down_a_ref[...]
    down_ref[:, down_a_ref.shape[1] :] = down_b_ref[...]
    tokens_ref[...] = low_ref[...].astype(F32)
    for r in range(late_ref.shape[0]):
        mixer_gain_ref[pl.ds(r * late_ref.shape[1], late_ref.shape[1])] = late_ref[r]
    ffn_gain_ref[...] = small_ref[1]
    out_gain_ref[...] = small_ref[2, :DV]


def gather_rings(slab_ref, full_ref, core_s, core_r, ring_s, ring_r, done):
    seq, head = lax.axis_index("seq"), lax.axis_index("head")
    core = seq % 2
    sibling = (seq + 1 - 2 * core, head)
    ring_x, ring_z = ring_ids("x"), ring_ids("z")
    x, z = ring_x[0], ring_z[0]
    rows, wide = slab_ref.shape
    cut = -(-wide // (2 * LANES)) * LANES
    counts = {"core": 0, "ring": 0}

    def slot(kind):
        counts[kind] += 1
        return counts[kind] - 1

    def across(source, target):
        return send(source, target, core_s, core_r, slot("core"), sibling)

    own_across = across(slab_ref, full_ref.at[x, z, core])
    half = rows // 2
    upper, lower, everything = pl.ds(0, half), pl.ds(half, half), pl.ds(0, rows)

    def round_ring(ring, at, source, arrived, ended):
        me, right, left, opposite, right_id, left_id = ring

        def go(place, part, peer):
            origin = source(part) if place is me else at(place, part)
            return send(origin, at(place, part), ring_s, ring_r, slot("ring"), peer)

        upper_right = go(me, upper, right_id)
        lower_left = go(me, lower, left_id)
        lower_right = go(me, lower, right_id)
        upper_left = go(me, upper, left_id)
        yield
        upper_right.wait()
        far_right = go(left, upper, right_id)
        lower_left.wait()
        far_left = go(right, lower, left_id)
        lower_right.wait()
        arrived(left)
        upper_left.wait()
        arrived(right)
        yield
        far_right.wait()
        far_left.wait()
        arrived(opposite)
        ended()

    active = []
    for ring_1, ring_2, columns, x_first in (
        (ring_x, ring_z, pl.ds(0, cut), True),
        (ring_z, ring_x, pl.ds(cut, wide - cut), False),
    ):
        def place_of(first, second, part, columns=columns, x_first=x_first):
            where = (first, second) if x_first else (second, first)
            return full_ref.at[where[0], where[1], core, part, columns]

        def start_second(first, copies, source=None, ring_2=ring_2, place_of=place_of, x_first=x_first, columns=columns):
            def at(place, part):
                return place_of(first, place, part)

            def arrived(place):
                copies.append(across(at(place, everything), at(place, everything)))

            def ended():
                done(x_first, first, columns, copies)

            active.append(round_ring(ring_2, at, source or (lambda part: at(ring_2[0], part)), arrived, ended))

        def at_first(place, part, ring_2=ring_2, place_of=place_of):
            return place_of(place, ring_2[0], part)

        def arrived_first(place, at_first=at_first, start_second=start_second):
            start_second(place, [across(at_first(place, everything), at_first(place, everything))])

        def mine(part, columns=columns):
            return slab_ref.at[part, columns]

        active.append(round_ring(ring_1, at_first, mine, arrived_first, lambda: None))
        start_second(ring_1[0], [own_across] if x_first else [], mine)
    while active:
        ended = []
        for stage in list(active):
            if next(stage, active) is active:
                ended.append(stage)
        active[:] = [stage for stage in active if stage not in ended]
        yield


def project_kernel(
    heads, in_ref, rate_ref, out_weight_ref, gate_up_ref, down_ref, tokens_ref, gain_ref,
    full_ref, proj_ref, split_ref, split_sib_ref, out_slab_ref, rest_ref,
    slab_ref, weights, normed, halo_in, own_s, store_s, halo_s, halo_r, half_s, half_r, core_s, core_r, ring_s, ring_r,
):
    seq, head = lax.axis_index("seq"), lax.axis_index("head")
    peers = lax.axis_size("seq")
    core = seq % 2
    sibling = (seq + 1 - 2 * core, head)
    before, after = (lax.rem(seq + peers - 1, peers), head), (lax.rem(seq + 1, peers), head)
    ring_x, ring_z = ring_ids("x"), ring_ids("z")
    rows, wide = slab_ref.shape
    count, width = tokens_ref.shape
    all_here = say_here(ring_x[4:] + ring_z[4:] + (sibling, before, after))
    gate_at = heads * CONV + LANES
    mixer = in_ref[...].astype(F32)
    rates = rate_ref[...].astype(F32)
    slab_ref[:, heads * CONV : gate_at] = jnp.concatenate(
        [rates[:, 0], rates[:, 1], jnp.zeros((rows, LANES - 2 * heads), F32)], axis=1
    ).astype(BF16)
    for h in range(heads):
        slab_ref[:, h * CONV : (h + 1) * CONV] = mixer[:, h, :CONV].astype(BF16)
        slab_ref[:, gate_at + h * DV : gate_at + (h + 1) * DV] = mixer[:, h, CONV:].astype(BF16)
    own = pltpu.make_async_copy(slab_ref, weights.at[ring_x[0], ring_z[0], core], own_s)
    own.start()
    all_here()
    ready = []
    gather = gather_rings(slab_ref, weights, core_s, core_r, ring_s, ring_r, lambda *group: ready.append(group))
    next(gather)
    halo = send(tokens_ref.at[pl.ds(count - HALO, HALO)], halo_in, halo_s, halo_r, 0, after)

    def norm(values):
        return values * rms_scale(values) * gain_ref[...]

    fresh = norm(tokens_ref[...].astype(F32))
    normed[HALO:] = fresh.astype(BF16)
    split_ref[...] = split_by_core(normed[HALO:].astype(F32), rows).astype(BF16)
    half = send(other_half(split_ref), split_sib_ref, half_s, half_r, 0, sibling)
    out_weight = out_weight_ref[...].astype(F32)
    for h in range(heads):
        out_slab_ref[:, h * DV : (h + 1) * DV] = out_weight[:, h].astype(BF16)
    gate_up = gate_up_ref[...].astype(F32)
    for at, length in chunks_of(down_ref.shape[1]):
        here = slice(at, at + length)
        for g in range(2):
            rest_ref[:, 3 * at + g * length : 3 * at + (g + 1) * length] = gate_up[:, g, here].astype(BF16)
        rest_ref[:, 3 * at + 2 * length : 3 * at + 3 * length] = down_ref[:, here]
    halo.wait()
    normed[:HALO] = jnp.where(seq > 0, norm(halo_in[...].astype(F32)), 0.0).astype(BF16)
    own.wait()
    stores, started = [], set()
    slabs = 2 * rows
    chip_rows = 4 * slabs

    def use(group):
        x_first, place, columns, copies = group
        for copy in copies:
            copy.wait()
        if x_first:
            left = normed[:, pl.ds(pl.multiple_of(place * chip_rows, chip_rows), chip_rows)]
            source, target = weights.at[place], full_ref.at[place]
        else:
            left = jnp.concatenate(
                [
                    normed[:, pl.ds(pl.multiple_of(k * chip_rows + place * slabs, slabs), slabs)]
                    for k in range(width // chip_rows)
                ],
                axis=1,
            )
            source, target = weights.at[:, place], full_ref.at[:, place]
        region = (slice(None), slice(None), slice(None), columns)
        store = pltpu.make_async_copy(source.at[region], target.at[region], store_s.at[len(stores)])
        store.start()
        stores.append(store)
        at, end = columns.start, columns.start + columns.size
        first_use = x_first not in started
        started.add(x_first)
        while at < end:
            length = min(4 * LANES, end - at)
            here = pl.ds(at, length)
            right = source[:, :, :, here].reshape(chip_rows, length)
            product = mm(left, right)
            if first_use:
                proj_ref[:, here] = product
            else:
                proj_ref[:, here] += product
            at += length

    running = True
    while running or ready:
        if running:
            running = next(gather, gather) is not gather
        if ready:
            use(ready.pop(0))
    half.wait()
    for store in stores:
        store.wait()


def forward_kernel(
    heads, slab, groups, proj_ref, taps_ref, log_ref, bias_ref, out_gain_ref, slab_ref, tokens_ref, ffn_gain_ref,
    q_ref, k_ref, v_ref, inv_ref, map_ref, mixed_ref, gated_ref, entering_ref, kept_ref, totals_ref,
    out_full_ref, second_ref, middle_ref,
    weights, out_local, pack, near_in, before, far_out, far_in, back_out, back_in, part, landing,
    own_s, store_s, core_s, core_r, ring_s, ring_r,
    near_s, near_r, far_s, far_r, back_s, back_r, red_s, red_r, gat_s, gat_r,
):
    size = proj_ref.shape[0] - HALO
    members = pack.shape[0]
    member, group, near, near_ids, far_ids = scan_places(members, groups)
    ring_y = ring_ids("y")
    all_here = say_here([*near_ids[1:], *far_ids[1:], *ring_y[4:]])
    own = pltpu.make_async_copy(
        slab_ref, weights.at[lax.axis_index("seq") // 8, (lax.axis_index("seq") // 2) % 4, lax.axis_index("seq") % 2], own_s
    )
    own.start()
    rows, columns = triangles(size)
    rates = proj_ref[HALO:, heads * CONV : heads * CONV + LANES]
    scales = (log_ref, bias_ref)
    arrived = []
    gather = gather_rings(slab_ref, weights, core_s, core_r, ring_s, ring_r, lambda *group: arrived.extend(group[3]))
    lower, kept = [], []
    for h in range(heads):
        projected = proj_ref[:, h * CONV : (h + 1) * CONV]
        taps = taps_ref[:, h]
        *_, queries, keys, values = mixer_inputs(projected, taps)
        q_ref[h], k_ref[h], v_ref[h] = queries, keys, values
        beta, decay, gamma, gamma_row, _ = gates(rates, scales, h, heads)
        spread = decays_of(gamma, gamma_row)
        lower.append(jnp.where(columns < rows, beta * spread * mmt(keys, keys), 0.0))
        kept.append((queries, keys, values, beta, gamma, spread))
        if h == 0:
            all_here()
            next(gather)

    def between(width):
        if width in (32, 128):
            next(gather, None)

    inverses = inverse(lower, between)
    written = []
    for h in range(heads):
        queries, keys, values, beta, gamma, spread = kept[h]
        inv_ref[h] = inverses[h]
        growth = jnp.exp(gamma)
        targets = jnp.concatenate([growth * beta * keys.astype(F32), beta * values.astype(F32)], axis=1)
        written.append(mm(inverses[h], targets, FINE))
        final = gamma[size - 1 : size]
        faded = jnp.exp(final - gamma) * keys.astype(F32)
        summary = mtm(faded, written[h], FINE)
        unit = (iota((DK, DK), 0) == iota((DK, DK), 1)).astype(F32)
        passed = (jnp.exp(final) * unit - summary[:, :DK]).astype(BF16)
        for half in range(HALVES):
            pack[HALVES * h + half, :, :DK] = passed
            pack[HALVES * h + half, :, DK:] = summary[:, (half + 1) * DK : (half + 2) * DK].astype(BF16)
    copies = [send(pack.at[near[d]], near_in.at[member], near_s, near_r, d, near_ids[d]) for d in range(1, members)]
    near_in[member] = pack[member]
    next(gather, None)
    for h in range(heads):
        queries, keys, values, beta, gamma, spread = kept[h]
        through = mm(spread * mmt(queries, keys), written[h], FINE)
        map_ref[h] = jnp.exp(gamma) * queries.astype(F32) - through[:, :DK]
        out_local[h] = through[:, DK:]
    for copy in copies:
        copy.wait()
    unit = (iota((DK, DK), 0) == iota((DK, DK), 1)).astype(F32)
    total = jnp.concatenate([unit, jnp.zeros((DK, DK), F32)], axis=1)
    for j in range(members):
        before[j] = total
        kept_ref[j] = near_in[j, :, :DK]
        moved = twice(near_in[j, :, :DK], total)
        total = jnp.concatenate([moved[:, :DK], moved[:, DK:] + near_in[j, :, DK:].astype(F32)], axis=1)
    far_out[...] = total.astype(BF16)
    copies = [send(far_out, far_in.at[group], far_s, far_r, d, far_ids[d]) for d in range(1, groups)]
    far_in[group] = far_out[...]
    next(gather, None)
    for copy in copies:
        copy.wait()
    state = jnp.zeros((DK, DK), F32)
    for j in range(groups):
        totals_ref[j] = far_in[j, :, :DK]
        fresh = twice(far_in[j, :, :DK], state) + far_in[j, :, DK:].astype(F32)
        state = jnp.where(j < group, fresh, state)
    for j in range(members):
        back_out[j] = (mm(before[j, :, :DK], state, FINE) + before[j, :, DK:]).astype(BF16)
    copies = [send(back_out.at[near[d]], back_in.at[member], back_s, back_r, d, near_ids[d]) for d in range(1, members)]
    back_in[member] = back_out[member]
    finish(gather)
    for copy in arrived:
        copy.wait()
    own.wait()
    store = pltpu.make_async_copy(weights, out_full_ref, store_s)
    store.start()
    for copy in copies:
        copy.wait()
    entering_ref[...] = back_in[...]
    gain = out_gain_ref[...]
    for h in range(heads):
        mixer_out = out_local[h] + mm(map_ref[h], whole_state(back_in, h), FINE)
        mixed_ref[h] = mixer_out
        gate = proj_ref[HALO:, gate_columns(heads, h)]
        scale = lax.rsqrt(jnp.mean(mixer_out * mixer_out, axis=-1, keepdims=True) + 1e-05)
        gated = mixer_out * scale * gain * (gate * jax.nn.sigmoid(gate))
        gated_ref[:, h * DV : (h + 1) * DV] = gated.astype(BF16)
    slabs = 2 * slab
    pairs_of = 2

    @pl.loop(0, 4)
    def _(x):
        for z in range(0, 4, pairs_of):
            right = weights[x, z : z + pairs_of].reshape(pairs_of * slabs, heads * DV)
            product = mmt(gated_ref[...], right)
            at = pl.ds(pl.multiple_of(x * 4 * slabs + z * slabs, pairs_of * slabs), pairs_of * slabs)
            for p in range(part.shape[0]):
                n = part.shape[1]
                part[p, :, at] = product[p * n : (p + 1) * n].astype(BF16)

    me = ring_y[0]
    finish(ring_reduce(ring_y, part, middle_ref, landing, red_s, red_r))
    middle = tokens_ref[me].astype(F32) + middle_ref[...]
    second_ref[me] = (middle * rms_scale(middle) * ffn_gain_ref[...]).astype(BF16)
    gather_y = ring_gather(ring_y, second_ref, gat_s, gat_r)
    next(gather_y)
    middle_ref[...] = middle
    finish(gather_y)
    store.wait()


def call(kernel, outs, *args, name):
    return pl.pallas_call(
        kernel,
        in_specs=[pl.BlockSpec(memory_space=pltpu.VMEM)] * len(args),
        out_specs=[pl.BlockSpec(memory_space=pltpu.VMEM)] * len(outs),
        out_shape=[jax.ShapeDtypeStruct(shape, kind) for shape, kind in outs],
        compiler_params=pltpu.CompilerParams(vmem_limit_bytes=VMEM_LIMIT),
        name=name,
    )(*args)


def pairs(*sizes):
    return [pltpu.SemaphoreType.DMA((size,)) for size in sizes for _ in range(2)]


def per_device(
    tokens,
    mixer_gain,
    in_weight,
    rate_weight,
    conv_weight,
    decay_log,
    decay_bias,
    out_gain,
    out_weight,
    ffn_gain,
    gate_up_weight,
    down_weight,
    cotangent,
):
    count, width = tokens.shape
    heads = in_weight.shape[1]
    hidden_units = down_weight.shape[1]
    slab = in_weight.shape[0]
    projections = heads * PROJ + LANES
    units = heads * HALVES
    peers, sharers = lax.axis_size("seq"), lax.axis_size("head")
    groups = peers // units
    rows = count // sharers

    convolved_wide = heads * CONV + LANES
    out_wide = heads * DV
    anywhere = pl.BlockSpec(memory_space=pl.ANY)
    in_vmem = pl.BlockSpec(memory_space=pltpu.VMEM)

    def landing(*shape):
        return pltpu.VMEM((6, *shape), BF16)

    blocked = (sharers, rows, width)
    stacked = (4, 4, 2, slab)
    first_full, projected, normed_split, normed_sibling, out_slab, rest = pl.pallas_call(
        functools.partial(project_kernel, heads),
        in_specs=[in_vmem] * 7,
        out_specs=[anywhere] + [in_vmem] * 5,
        out_shape=[
            jax.ShapeDtypeStruct((*stacked, projections), BF16),
            jax.ShapeDtypeStruct((HALO + count, projections), F32),
            jax.ShapeDtypeStruct((count, width), BF16),
            jax.ShapeDtypeStruct((count, width // 2), BF16),
            jax.ShapeDtypeStruct((slab, out_wide), BF16),
            jax.ShapeDtypeStruct((slab, 3 * hidden_units), BF16),
        ],
        scratch_shapes=[
            pltpu.VMEM((slab, projections), BF16),
            pltpu.VMEM((*stacked, projections), BF16),
            pltpu.VMEM((HALO + count, width), BF16),
            pltpu.VMEM((HALO, width), BF16),
            pltpu.SemaphoreType.DMA,
            pltpu.SemaphoreType.DMA((8,)),
            *pairs(1, 1, 31, 60),
        ],
        compiler_params=pltpu.CompilerParams(vmem_limit_bytes=VMEM_LIMIT, collective_id=7, has_side_effects=True),
        name="project",
    )(in_weight, rate_weight, out_weight, gate_up_weight, down_weight, tokens, mixer_gain.reshape(1, width))
    rest_full = lax.all_gather(rest, "seq", axis=0, tiled=True)
    first_full = first_full.reshape(width, projections)

    in_smem = pl.BlockSpec(memory_space=pltpu.SMEM)
    gain_row = out_gain.reshape(1, DV)
    block = (DK, DK)
    double = (DK, 2 * DK)
    (
        queries, keys, values, inv, out_map, mixer_out, gated, entering, kept, totals, out_full, second, middle,
    ) = pl.pallas_call(
        functools.partial(forward_kernel, heads, slab, groups),
        in_specs=[in_vmem] * 2 + [in_smem] * 2 + [in_vmem] * 4,
        out_specs=[in_vmem] * 10 + [anywhere] + [in_vmem] * 2,
        out_shape=[
            jax.ShapeDtypeStruct((heads, count, DK), BF16),
            jax.ShapeDtypeStruct((heads, count, DK), BF16),
            jax.ShapeDtypeStruct((heads, count, DV), BF16),
            jax.ShapeDtypeStruct((heads, count, count), F32),
            jax.ShapeDtypeStruct((heads, count, DK), F32),
            jax.ShapeDtypeStruct((heads, count, DV), F32),
            jax.ShapeDtypeStruct((count, out_wide), BF16),
            jax.ShapeDtypeStruct((units, *block), BF16),
            jax.ShapeDtypeStruct((units, *block), BF16),
            jax.ShapeDtypeStruct((groups, *block), BF16),
            jax.ShapeDtypeStruct((*stacked, out_wide), BF16),
            jax.ShapeDtypeStruct(blocked, BF16),
            jax.ShapeDtypeStruct((rows, width), F32),
        ],
        scratch_shapes=[
            pltpu.VMEM((*stacked, out_wide), BF16),
            pltpu.VMEM((heads, count, DV), F32),
            pltpu.VMEM((units, *double), BF16),
            pltpu.VMEM((units, *double), BF16),
            pltpu.VMEM((units, *double), F32),
            pltpu.VMEM(double, BF16),
            pltpu.VMEM((groups, *double), BF16),
            pltpu.VMEM((units, *block), BF16),
            pltpu.VMEM((units, *block), BF16),
            pltpu.VMEM(blocked, BF16),
            landing(rows // 2, width),
            pltpu.SemaphoreType.DMA,
            pltpu.SemaphoreType.DMA,
            *pairs(31, 60, units, groups, units, 6, 6),
        ],
        compiler_params=pltpu.CompilerParams(vmem_limit_bytes=VMEM_LIMIT, collective_id=1, has_side_effects=True),
        name="forward",
    )(
        projected,
        conv_weight,
        decay_log,
        decay_bias,
        gain_row,
        out_slab,
        tokens.reshape(blocked),
        ffn_gain.reshape(1, width),
    )
    out_full = out_full.reshape(width, out_wide)
    ring = [landing(rows // 2, width)]
    second = second.reshape(count, width)
    gate_wide = heads * DV
    many = 4 * slab

    def sums_scratch(wide_1, wide_2):
        return [
            pltpu.VMEM((4, many, wide_1), BF16),
            pltpu.VMEM((4, many, wide_2), BF16),
            landing(many // 2, wide_1),
            landing(many // 2, wide_2),
            pltpu.VMEM((many, wide_1), BF16),
            pltpu.VMEM((many, wide_2), BF16),
            landing(slab // 2, wide_1),
            landing(slab // 2, wide_2),
        ]

    down_a = -(-hidden_units // (2 * LANES)) * LANES
    down_b = hidden_units - down_a
    chunk_count = len(chunks_of(hidden_units))
    grad_branch, grad_middle, grad_ffn_gain, ffn_part, gate_up_part, grad_down_a, grad_down_b = pl.pallas_call(
        functools.partial(ffn_kernel, slab),
        in_specs=[in_vmem] * 4 + [anywhere],
        out_specs=[in_vmem] * 4 + [anywhere] + [in_vmem] * 2,
        out_shape=[
            jax.ShapeDtypeStruct(blocked, BF16),
            jax.ShapeDtypeStruct((rows, width), F32),
            jax.ShapeDtypeStruct((1, width), F32),
            jax.ShapeDtypeStruct(blocked, BF16),
            jax.ShapeDtypeStruct((4, many, 2 * hidden_units), BF16),
            jax.ShapeDtypeStruct((slab, down_a), F32),
            jax.ShapeDtypeStruct((slab, down_b), F32),
        ],
        scratch_shapes=[
            pltpu.VMEM((width, 3 * hidden_units), BF16),
            pltpu.VMEM((count, hidden_units), BF16),
            pltpu.VMEM((count, 2 * hidden_units), BF16),
            pltpu.VMEM((count, width), BF16),
            pltpu.VMEM((count, width), BF16),
            pltpu.VMEM((count, width // 2), BF16),
            pltpu.VMEM((count, width // 2), BF16),
            pltpu.VMEM((count, hidden_units), BF16),
            pltpu.VMEM((count, 2 * hidden_units), BF16),
            pltpu.VMEM((count, width), F32),
            pltpu.VMEM(blocked, BF16),
            *ring,
            pltpu.VMEM((4, many, 2 * hidden_units), BF16),
            *sums_scratch(down_a, down_b),
            pltpu.SemaphoreType.DMA((chunk_count,)),
            pltpu.SemaphoreType.DMA,
            *pairs(2, chunk_count, chunk_count, 6, 6, 6, 6, 6, 6),
        ],
        compiler_params=pltpu.CompilerParams(vmem_limit_bytes=VMEM_LIMIT, collective_id=3, has_side_effects=True),
        name="ffn",
    )(second, cotangent, middle, ffn_gain.reshape(1, width), rest_full)
    same_core = [[device for device in range(peers) if device % 2 == core] for core in range(2)]
    grad_gate_up_part = lax.psum_scatter(
        gate_up_part.reshape(width // 2, 2 * hidden_units), "seq", scatter_dimension=0, axis_index_groups=same_core, tiled=True
    )
    grad_branch = grad_branch.reshape(count, width)
    (
        grad_projected, grad_sibling, grad_gate, grad_out_gain, grad_taps, grad_scales, first_out, first_gate, output,
    ) = pl.pallas_call(
        functools.partial(backward_kernel, heads, slab, groups),
        in_specs=[in_vmem, anywhere] + [in_vmem] * 6 + [in_smem] * 2 + [in_vmem] * 11,
        out_specs=[in_vmem] * 9,
        out_shape=[
            jax.ShapeDtypeStruct((count, convolved_wide), BF16),
            jax.ShapeDtypeStruct((count, convolved_wide), BF16),
            jax.ShapeDtypeStruct((count, gate_wide), BF16),
            jax.ShapeDtypeStruct((1, DV), F32),
            jax.ShapeDtypeStruct((KW, heads * CONV), F32),
            jax.ShapeDtypeStruct((8, LANES), F32),
            jax.ShapeDtypeStruct((slab, gate_wide), F32),
            jax.ShapeDtypeStruct((slab, gate_wide), F32),
            jax.ShapeDtypeStruct(blocked, BF16),
        ],
        scratch_shapes=[
            pltpu.VMEM((width, out_wide), BF16),
            pltpu.VMEM((count, width), BF16),
            pltpu.VMEM((count, width // 2), BF16),
            pltpu.VMEM((count, gate_wide), BF16),
            pltpu.VMEM((count, gate_wide), BF16),
            pltpu.VMEM((heads, count, DV), F32),
            pltpu.VMEM((units, *block), BF16),
            pltpu.VMEM((units, *block), BF16),
            pltpu.VMEM((units, *block), BF16),
            pltpu.VMEM((units, *block), F32),
            pltpu.VMEM((units, *block), F32),
            pltpu.VMEM(block, BF16),
            pltpu.VMEM((groups, *block), BF16),
            pltpu.VMEM((units, *block), BF16),
            pltpu.VMEM((units, *block), BF16),
            pltpu.VMEM((heads, count, count), F32),
            pltpu.VMEM((heads, count, DV), F32),
            pltpu.VMEM((heads, count, DV), F32),
            pltpu.VMEM((heads, count, count), F32),
            pltpu.VMEM((heads, count, DV), F32),
            pltpu.VMEM((heads, HALO, CONV), F32),
            pltpu.VMEM((heads, HALO, CONV), F32),
            pltpu.VMEM((heads, HALO, CONV), F32),
            *sums_scratch(gate_wide, gate_wide),
            landing(rows // 2, width),
            pltpu.VMEM((rows, width), F32),
            pltpu.SemaphoreType.DMA,
            *pairs(3, units, groups, units, heads, heads, heads, 1, 6, 6, 6, 6, 6, 6),
        ],
        compiler_params=pltpu.CompilerParams(vmem_limit_bytes=VMEM_LIMIT, collective_id=6, has_side_effects=True),
        name="backward",
    )(
        grad_branch,
        out_full,
        mixer_out,
        out_map,
        projected,
        gain_row,
        gated,
        conv_weight,
        decay_log,
        decay_bias,
        normed_split,
        normed_sibling,
        kept,
        totals,
        entering,
        queries,
        keys,
        values,
        inv,
        ffn_part,
        middle,
    )
    wide_a = -(-convolved_wide // (2 * LANES)) * LANES
    wide_b = convolved_wide - wide_a
    low, small, late, first_a, first_b = pl.pallas_call(
        functools.partial(last_kernel, slab),
        in_specs=[in_vmem] * 12 + [anywhere],
        out_specs=[in_vmem] * 5,
        out_shape=[
            jax.ShapeDtypeStruct(blocked, BF16),
            jax.ShapeDtypeStruct((8, width), F32),
            jax.ShapeDtypeStruct((8, width // 8), F32),
            jax.ShapeDtypeStruct((slab, wide_a), F32),
            jax.ShapeDtypeStruct((slab, wide_b), F32),
        ],
        scratch_shapes=[
            pltpu.VMEM((width, projections), BF16),
            pltpu.VMEM((8, width), F32),
            pltpu.VMEM((8, width // 8), F32),
            pltpu.VMEM(blocked, BF16),
            landing(rows // 2, width),
            pltpu.VMEM((rows, width), F32),
            pltpu.VMEM((7, 8, width), F32),
            pltpu.VMEM((7, 8, width), F32),
            pltpu.VMEM((7, 8, width // 8), F32),
            pltpu.VMEM((7, 8, width // 8), F32),
            *sums_scratch(wide_a, wide_b),
            pltpu.SemaphoreType.DMA((width // 256,)),
            *pairs(6, 6, 7, 7, 6, 6, 6, 6),
        ],
        compiler_params=pltpu.CompilerParams(vmem_limit_bytes=VMEM_LIMIT, collective_id=5, has_side_effects=True),
        name="last",
    )(
        grad_gate,
        tokens.reshape(blocked),
        grad_middle,
        mixer_gain.reshape(1, width),
        grad_ffn_gain,
        grad_out_gain,
        grad_scales,
        grad_taps,
        normed_split,
        normed_sibling,
        grad_projected,
        grad_sibling,
        first_full,
    )
    grad_in, grad_rate, grad_out, grad_gate_up_weight, grad_down, grad_tokens, grad_conv, *gains = call(
        functools.partial(finish_kernel, heads),
        [
            ((slab, heads, PROJ), F32),
            ((slab, 2, heads), F32),
            ((slab, heads, DV), F32),
            ((slab, 2, hidden_units), F32),
            ((slab, hidden_units), F32),
            ((count, width), F32),
            ((KW, heads, CONV), F32),
            ((width,), F32),
            ((width,), F32),
            ((DV,), F32),
        ],
        first_a,
        first_b,
        first_out,
        first_gate,
        grad_gate_up_part,
        grad_down_a,
        grad_down_b,
        low.reshape(count, width),
        small,
        late,
        name="finish",
    )
    return (
        output.reshape(count, width),
        grad_tokens,
        gains[0],
        grad_in,
        grad_rate,
        grad_conv,
        small[2, DV : DV + heads],
        small[2, DV + LANES : DV + LANES + heads],
        gains[2],
        grad_out,
        gains[1],
        grad_gate_up_weight,
        grad_down,
    )


def solution(mesh):
    in_specs = (
        P("seq", None),
        P(),
        P("seq", "head", None),
        P("seq", None, "head"),
        P(None, "head", None),
        P("head"),
        P("head"),
        P(),
        P("seq", "head", None),
        P(),
        P("seq", None, "head"),
        P("seq", "head"),
        P("seq", None),
    )
    out_specs = (
        P("seq", None),
        P("seq", None),
        P(),
        P("seq", "head", None),
        P("seq", None, "head"),
        P(None, "head", None),
        P("head"),
        P("head"),
        P(),
        P("seq", "head", None),
        P(),
        P("seq", None, "head"),
        P("seq", "head"),
    )
    return jax.shard_map(
        per_device, mesh=mesh, in_specs=in_specs, out_specs=out_specs, check_vma=False
    )
```

```python
import functools

import jax
import jax.numpy as jnp
from jax import lax
from jax.experimental import pallas as pl
from jax.experimental.pallas import tpu as pltpu
from jax.sharding import PartitionSpec as P

DK = 128
DV = 256
KW = 4
CONV = 512
PROJ = 768
LANES = 128
HALO = 16
HALVES = DV // DK
MESH = pl.DeviceIdType.MESH

F32 = jnp.float32
BF16 = jnp.bfloat16
EXACT = lax.Precision.HIGHEST
FINE = lax.Precision.HIGH
VMEM_LIMIT = 56 * 1024 * 1024


def dot(a, b, dims, precision=None):
    return lax.dot_general(a, b, (dims, ((), ())), precision=precision, preferred_element_type=F32)


def mm(a, b, precision=None):
    return dot(a, b, ((1,), (0,)), precision)


def mmt(a, b, precision=None):
    return dot(a, b, ((1,), (1,)), precision)


def mtm(a, b, precision=None):
    return dot(a, b, ((0,), (0,)), precision)


def iota(shape, dim):
    return lax.broadcasted_iota(jnp.int32, shape, dim)


def softplus(x):
    return jnp.maximum(x, 0.0) + jnp.log1p(jnp.exp(-jnp.abs(x)))


def split_by_core(values, slab):
    width = values.shape[1]
    lanes = iota((values.shape[0], 2 * slab), 1)
    firsts, seconds = [], []
    for at in range(0, width, 4 * slab):
        a, b = values[:, at : at + 2 * slab], values[:, at + 2 * slab : at + 4 * slab]
        firsts.append(jnp.where(lanes < slab, a, pltpu.roll(b, slab, 1)))
        seconds.append(jnp.where(lanes < slab, pltpu.roll(a, slab, 1), b))
    return jnp.concatenate(firsts + seconds, axis=1)


def triangles(size):
    rows, columns = iota((size, size), 0), iota((size, size), 1)
    return rows, columns


def lane_values(ref, heads):
    lanes = iota((1, LANES), 1)
    total = jnp.zeros((1, LANES), F32)
    for h in range(heads):
        total = total + jnp.where(lanes == h, ref[h], 0.0)
    return total


def gates(rates, log_ref, bias_ref, heads):
    size = rates.shape[0]
    pre = rates + lane_values(bias_ref, heads)
    beta = jax.nn.sigmoid(rates)
    decay = jnp.where(iota(rates.shape, 1) < heads, -jnp.exp(lane_values(log_ref, heads)) * softplus(pre), 0.0)
    rows, columns = triangles(size)
    gamma = mm((columns <= rows).astype(F32), decay, EXACT)
    return beta, decay, gamma, gamma.T, pre


def of_head(gate_values, head, heads):
    beta, _, gamma, gamma_row, _ = gate_values
    return beta[:, heads + head : heads + head + 1], gamma[:, head : head + 1], gamma_row[head : head + 1]


def decays_of(gamma, gamma_row):
    size = gamma.shape[0]
    rows, columns = triangles(size)
    inside = columns <= rows
    return jnp.where(inside, jnp.exp(jnp.where(inside, gamma - gamma_row, 0.0)), 0.0)


def inverse(lower, between):
    size = lower[0].shape[0]
    rows, columns = triangles(size)
    unit = (rows == columns).astype(F32)
    known = [unit - jnp.where(rows // 2 == columns // 2, a, 0.0) for a in lower]
    width = 2
    while width < size:
        fresh = (rows // (2 * width) == columns // (2 * width)) & (rows // width != columns // width)
        parts = [jnp.where(fresh, a, 0.0) for a in lower]
        first = [mm(c, x, FINE) for c, x in zip(parts, known)]
        known = [x - mm(x, y, FINE) for x, y in zip(known, first)]
        width *= 2
        between(width)
    return known


def convolved(extended, taps):
    total = None
    for j in range(KW):
        shift = KW - 1 - j
        moved = extended if shift == 0 else pltpu.roll(extended, shift, 0)
        term = taps[j : j + 1] * moved[HALO:]
        total = term if total is None else total + term
    return total


def unit_rows(values):
    return lax.rsqrt(jnp.sum(values * values, axis=-1, keepdims=True) + 1e-06)


def mixer_inputs(projected, taps):
    extended = projected[:, :CONV].astype(BF16).astype(F32)
    mixed = convolved(extended, taps)
    gate = jax.nn.sigmoid(mixed)
    active = mixed * gate
    q_raw, k_raw = active[:, :DK], active[:, DK : 2 * DK]
    q_scale, k_scale = unit_rows(q_raw), unit_rows(k_raw)
    queries = (q_raw * q_scale * DK ** (-0.5)).astype(BF16)
    keys = (k_raw * k_scale).astype(BF16)
    values = active[:, 2 * DK :].astype(BF16)
    return extended, mixed, gate, (q_raw, q_scale), (k_raw, k_scale), queries, keys, values


def gate_columns(heads, head):
    at = heads * CONV + LANES + head * DV
    return pl.ds(at, DV)


def whole_state(units_ref, head):
    return jnp.concatenate([units_ref[HALVES * head + half] for half in range(HALVES)], axis=1).astype(F32)


def weight_blocks(x, x_sib, y, y_sib, columns, target, slab, z_first):
    places = target.shape[0]
    many = places * slab
    own = lax.axis_index("seq") % 2 * (x.shape[1] // 2)

    @pl.loop(0, places)
    def _(block):
        at = pl.ds(pl.multiple_of(own + block * many, many), many)
        here = pl.ds(pl.multiple_of(block * many, many), many)
        part = (mtm(x[:, at], y[:, columns]) + mtm(x_sib[:, here], y_sib[:, columns])).astype(BF16)
        if z_first:
            rows = pl.ds(pl.multiple_of(block * slab, slab), slab)
            for place in range(places):
                target[place, rows] = part[place * slab : (place + 1) * slab]
        else:
            target[block] = part


def sum_both(first, second, part, middle, result, landing, landing_2, semaphores):
    places, many, wide = part.shape
    yield from ring_reduce(first, part, middle, landing, semaphores[0], semaphores[1])
    blocks = middle.reshape(places, many // places, wide)
    yield from ring_reduce(second, blocks, result, landing_2, semaphores[2], semaphores[3])


def norm_back(grad, values, scale):
    return scale * grad - values * (scale * scale * scale * jnp.sum(values * grad, axis=-1, keepdims=True))


def say_here(peers):
    barrier = pltpu.get_barrier_semaphore()
    for peer in peers:
        pl.semaphore_signal(barrier, inc=1, device_id=peer, device_id_type=MESH)

    def all_here():
        pl.semaphore_wait(barrier, len(peers))

    return all_here


def start_barrier(peers):
    say_here(peers)()


def send(source, target, sends, receives, slot, peer):
    copy = pltpu.make_async_remote_copy(
        src_ref=source,
        dst_ref=target,
        send_sem=sends.at[slot],
        recv_sem=receives.at[slot],
        device_id=peer,
        device_id_type=MESH,
    )
    copy.start()
    return copy


def twice(left, right):
    high = right.astype(BF16)
    low = (right - high.astype(F32)).astype(BF16)
    return mm(left, high) + mm(left, low)


def scan_places(members, groups):
    seq, head = lax.axis_index("seq"), lax.axis_index("head")
    member, group = seq % members, seq // members
    near = [(member + d) % members for d in range(members)]
    far = [(group + d) % groups for d in range(groups)]
    near_ids = [(group * members + place, head) for place in near]
    far_ids = [(place * members + member, head) for place in far]
    return member, group, near, near_ids, far_ids


def other_half(ref):
    half = ref.shape[1] // 2
    at = (1 - lax.axis_index("seq") % 2) * half
    return ref.at[:, pl.ds(pl.multiple_of(at, half), half)]


def ring_ids(axis):
    seq, head = lax.axis_index("seq"), lax.axis_index("head")
    size = {"x": lax.axis_size("seq") // 8, "y": lax.axis_size("head"), "z": 4}[axis]
    me = {"x": seq // 8, "y": head, "z": (seq // 2) % 4}[axis]

    def at(place):
        if axis == "y":
            return (seq, place)
        if axis == "x":
            return (place * 8 + seq % 8, head)
        return ((seq // 8) * 8 + place * 2 + seq % 2, head)

    right, left = lax.rem(me + 1, size), lax.rem(me + size - 1, size)
    return me, right, left, lax.rem(me + 2, size), at(right), at(left)


def add_into(target, pieces, rows):
    step = min(rows, 32)

    @pl.loop(0, rows // step)
    def _(k):
        part = pl.ds(pl.multiple_of(k * step, step), step)
        total = pieces[0][part].astype(F32)
        for piece in pieces[1:]:
            total = total + piece[part].astype(F32)
        target[part] = total.astype(target.dtype)


def ring_reduce(ring, blocks, result, landing, sends, receives):
    me, right, left, across, right_id, left_id = ring
    rows = blocks.shape[1]
    half = rows // 2
    upper, lower = pl.ds(0, half), pl.ds(half, half)
    by_right = send(blocks.at[across, upper], landing.at[0], sends, receives, 0, right_id)
    by_left = send(blocks.at[across, lower], landing.at[1], sends, receives, 1, left_id)
    plain_right = send(blocks.at[right, lower], landing.at[2], sends, receives, 2, right_id)
    plain_left = send(blocks.at[left, upper], landing.at[3], sends, receives, 3, left_id)
    yield
    by_right.wait()
    add_into(landing.at[0], [blocks.at[right, upper], landing.at[0]], half)
    summed_right = send(landing.at[0], landing.at[4], sends, receives, 4, right_id)
    by_left.wait()
    add_into(landing.at[1], [blocks.at[left, lower], landing.at[1]], half)
    summed_left = send(landing.at[1], landing.at[5], sends, receives, 5, left_id)
    yield
    plain_right.wait()
    plain_left.wait()
    summed_right.wait()
    summed_left.wait()
    add_into(result.at[upper], [blocks.at[me, upper], landing.at[4], landing.at[3]], half)
    add_into(result.at[lower], [blocks.at[me, lower], landing.at[2], landing.at[5]], half)


def ring_gather(ring, blocks, sends, receives):
    me, right, left, across, right_id, left_id = ring
    rows = blocks.shape[1]
    half = rows // 2
    upper, lower = pl.ds(0, half), pl.ds(half, half)

    def go(place, part, slot, peer):
        return send(blocks.at[place, part], blocks.at[place, part], sends, receives, slot, peer)

    upper_right = go(me, upper, 0, right_id)
    lower_left = go(me, lower, 1, left_id)
    lower_right = go(me, lower, 2, right_id)
    upper_left = go(me, upper, 3, left_id)
    yield
    upper_right.wait()
    far_right = go(left, upper, 4, right_id)
    lower_left.wait()
    far_left = go(right, lower, 5, left_id)
    yield
    for copy in (lower_right, upper_left, far_right, far_left):
        copy.wait()


def column_halves(width):
    return pl.ds(0, width // 2), pl.ds(width // 2, width // 2)


def finish(*generators):
    active = list(generators)
    while active:
        active = [g for g in active if next(g, active) is not active]


def rms_scale(values):
    return lax.rsqrt(jnp.mean(values * values, axis=-1, keepdims=True) + 1e-05)


def rms_back(grad, values, gain):
    scale = rms_scale(values)
    u = grad * gain
    back = scale * u - values * (scale * scale * scale * jnp.mean(u * values, axis=-1, keepdims=True))
    return back, jnp.sum(grad * values * scale, axis=0, keepdims=True)


def backward_kernel(
    heads, slab, groups, io, branch_ref, out_weight_ref, mixed_ref, map_ref, proj_ref, gain_ref, gated_ref, taps_ref, log_ref, bias_ref,
    normed_split_ref, normed_sib_ref, kept_ref, totals_ref, state_ref, q_ref, k_ref, v_ref, inv_ref, ffn_part_ref, middle_ref,
    out_ref, sibling_ref, gate_ref, gain_out_ref, taps_out_ref, scales_out_ref, first_out_ref, first_gate_ref, output_ref,
    out_weight, branch_split, branch_sib, gated_sib, gate_sib, grad_outs, pack, near_in, turned, before, after, far_out, far_in,
    back_out, back_in, sums_ref, spreads, residuals, writtens, grad_scores_all, partial, halo_out, halo_in, tails,
    part_o, part_g, land_o, land_g, mid_o, mid_g, land_o2, land_g2, land_f, sum_f,
    load_s, core_s, core_r, near_s, near_r, far_s, far_r, back_s, back_r, halo_s, halo_r, body_s, body_r, tail_s, tail_r,
    rate_s, rate_r, o1_s, o1_r, g1_s, g1_r, o2_s, o2_r, g2_s, g2_r, rf_s, rf_r, gf_s, gf_r,
):
    size = proj_ref.shape[0] - HALO
    seq, head_place = lax.axis_index("seq"), lax.axis_index("head")
    peers = lax.axis_size("seq")
    members = pack.shape[0]
    member, group, near, near_ids, far_ids = scan_places(members, groups)
    ring_x, ring_y, ring_z = ring_ids("x"), ring_ids("y"), ring_ids("z")
    previous, following = (lax.rem(seq + peers - 1, peers), head_place), (lax.rem(seq + 1, peers), head_place)
    sibling = (seq + 1 - 2 * (seq % 2), head_place)
    all_here = say_here([*near_ids[1:], *far_ids[1:], *ring_y[4:], previous, following])
    load = pltpu.make_async_copy(out_weight_ref, out_weight, load_s)
    load.start()
    io.arrive(branch_ref)
    branch_split[...] = split_by_core(branch_ref[...].astype(F32), slab).astype(BF16)
    all_here()
    io.arrive(gated_ref)
    first_aside = [
        send(other_half(branch_split), branch_sib, core_s, core_r, 0, sibling),
        send(gated_ref, gated_sib, core_s, core_r, 1, sibling),
    ]

    def output_sum():
        yield from ring_reduce(ring_y, ffn_part_ref, sum_f, land_f, rf_s, rf_r)
        output_ref[ring_y[0]] = (middle_ref[...] + sum_f[...]).astype(BF16)
        yield from ring_gather(ring_y, output_ref, gf_s, gf_r)

    output = output_sum()
    io.arrive(mixed_ref, map_ref, proj_ref, gain_ref)
    gain = gain_ref[...]
    gain_total = jnp.zeros_like(gain)
    load.wait()
    io.fetch(ffn_part_ref, kept_ref, totals_ref, normed_split_ref, normed_sib_ref, middle_ref)
    io.fetch(state_ref, q_ref, k_ref, v_ref, inv_ref, taps_ref)
    for h in range(heads):
        columns = slice(h * DV, (h + 1) * DV)
        grad = mm(branch_ref[...], out_weight[:, columns])
        mixer_out = mixed_ref[h]
        z = proj_ref[HALO:, gate_columns(heads, h)]
        scale = lax.rsqrt(jnp.mean(mixer_out * mixer_out, axis=-1, keepdims=True) + 1e-05)
        normal = mixer_out * scale
        s = jax.nn.sigmoid(z)
        silu = z * s
        gain_total = gain_total + jnp.sum(grad * normal * silu, axis=0, keepdims=True)
        gate_ref[:, columns] = (grad * normal * gain * s * (1.0 + z * (1.0 - s))).astype(BF16)
        u = grad * gain * silu
        grad_outs[h] = scale * u - normal * (scale * jnp.mean(u * normal, axis=-1, keepdims=True))
        carried = mtm(map_ref[h], grad_outs[h], FINE).astype(BF16)
        for half in range(HALVES):
            pack[HALVES * h + half] = carried[:, half * DK : (half + 1) * DK]
    gain_out_ref[...] = gain_total
    io.leave(gain_out_ref, gate_ref)
    io.arrive(kept_ref, totals_ref, q_ref, k_ref, v_ref, inv_ref, state_ref)
    io.arrive(normed_split_ref, normed_sib_ref, taps_ref)
    copies = [send(pack.at[near[d]], near_in.at[member], near_s, near_r, d, near_ids[d]) for d in range(1, members)]
    io.arrive(ffn_part_ref, middle_ref)
    next(output)
    gate_aside = send(gate_ref, gate_sib, core_s, core_r, 2, sibling)
    near_in[member] = pack[member]
    for copy in first_aside:
        copy.wait()
    weight_blocks(branch_split, branch_sib, gated_ref, gated_sib, pl.ds(0, part_o.shape[2]), part_o, slab, False)
    sum_o = sum_both(ring_x, ring_z, part_o, mid_o, first_out_ref, land_o, land_o2, (o1_s, o1_r, o2_s, o2_r))
    next(sum_o)
    unit = (iota((DK, DK), 0) == iota((DK, DK), 1)).astype(F32)
    passed, leading, ahead = unit, unit, []
    for j in range(members):
        turned[j] = kept_ref[j].astype(F32).T.astype(BF16)
    for j in range(members):
        ahead.append(leading)
        leading = mm(leading, turned[j].astype(F32), FINE)
        back = members - 1 - j
        before[back] = passed
        passed = twice(turned[back], passed)
    for copy in copies:
        copy.wait()
    total = near_in[0].astype(F32)
    for j in range(1, members):
        total = total + mm(ahead[j], near_in[j].astype(F32), FINE)
    far_out[...] = total.astype(BF16)
    copies = [send(far_out, far_in.at[group], far_s, far_r, d, far_ids[d]) for d in range(1, groups)]
    far_in[group] = far_out[...]

    rows, columns = triangles(size)
    strict = columns < rows
    rates = proj_ref[HALO:, heads * CONV : heads * CONV + LANES]
    gate_values = gates(rates, log_ref, bias_ref, heads)

    def without_leaving(h):
        kf = k_ref[h].astype(F32)
        beta, gamma, gamma_row = of_head(gate_values, h, heads)
        spread = decays_of(gamma, gamma_row)
        spreads[h] = spread
        residual = v_ref[h].astype(F32) - jnp.exp(gamma) * mm(kf, whole_state(state_ref, h))
        residuals[h] = residual
        written = mm(inv_ref[h], beta * residual, FINE)
        writtens[h] = written
        grad_scores_all[h] = mmt(grad_outs[h], written)
        partial[h] = mtm(spread * mmt(q_ref[h], k_ref[h]), grad_outs[h])

    total = jnp.zeros((DK, DK), F32)
    for j in reversed(range(members)):
        after[j] = total
        total = twice(turned[j], total) + near_in[j].astype(F32)
    without_leaving(0)
    gate_aside.wait()
    weight_blocks(normed_split_ref, normed_sib_ref, gate_ref, gate_sib, pl.ds(0, part_g.shape[2]), part_g, slab, True)
    sum_g = sum_both(ring_z, ring_x, part_g, mid_g, first_gate_ref, land_g, land_g2, (g1_s, g1_r, g2_s, g2_r))
    next(sum_g)
    turned_totals = [totals_ref[j].astype(F32).T.astype(BF16) for j in range(groups)]
    for copy in copies:
        copy.wait()
    state = jnp.zeros((DK, DK), F32)
    for j in reversed(range(groups)):
        fresh = twice(turned_totals[j], state) + far_in[j].astype(F32)
        state = jnp.where(j > group, fresh, state)
    for j in range(members):
        back_out[j] = (mm(before[j], state, FINE) + after[j]).astype(BF16)
    copies = [send(back_out.at[near[d]], back_in.at[member], back_s, back_r, d, near_ids[d]) for d in range(1, members)]
    back_in[member] = back_out[member]
    next(output)
    without_leaving(1)
    next(sum_o)
    without_leaving(2)
    next(output)
    without_leaving(3)
    next(sum_g)
    for copy in copies:
        copy.wait()

    lanes = iota((size, LANES), 1)
    grad_gammas = jnp.zeros((size, LANES), F32)
    grad_betas = jnp.zeros((size, LANES), F32)
    column_sums = []
    body = size - HALO
    copies = []
    beside = {0: [sum_o], 1: [sum_g, output], 2: [sum_o], 3: [sum_g]}
    for h in range(heads):
        queries, keys = q_ref[h], k_ref[h]
        qf, kf = queries.astype(F32), keys.astype(F32)
        beta, gamma, _ = of_head(gate_values, h, heads)
        spread, residual, written, grad_scores = spreads[h], residuals[h], writtens[h], grad_scores_all[h]
        growth = jnp.exp(gamma)
        final = gamma[size - 1 : size]
        fade = jnp.exp(final - gamma)
        state, leaving = whole_state(state_ref, h), whole_state(back_in, h)
        inv, grad = inv_ref[h], grad_outs[h]
        products = mmt(keys, keys)
        scores = spread * mmt(queries, keys)
        lower = jnp.where(strict, beta * spread * products, 0.0)
        faded = fade * kf
        grad_written = partial[h] + mm(faded, leaving)
        grad_targets = mtm(inv, grad_written, FINE)
        grad_lower = jnp.where(strict, -mmt(grad_targets, written), 0.0)
        grad_values = beta * grad_targets
        grad_beta = jnp.sum(grad_targets * residual, axis=-1, keepdims=True)
        grad_beta = grad_beta + jnp.sum(grad_lower * spread * products, axis=-1, keepdims=True)
        q_first = growth * mmt(grad, state)
        k_first = -growth * mmt(grad_values, state)
        spread_scores = spread * grad_scores
        spread_lower = grad_lower * beta * spread
        grad_faded = mmt(written, leaving)
        grad_queries = q_first + mm(spread_scores, kf)
        grad_keys = (
            k_first
            + mtm(spread_scores, qf)
            + mm(spread_lower, kf)
            + mtm(spread_lower, kf)
            + fade * grad_faded
        )
        energy = grad_scores * scores + grad_lower * lower
        fading = jnp.sum(grad_faded * faded, axis=-1, keepdims=True)
        grad_gamma = jnp.sum(qf * q_first + kf * k_first, axis=-1, keepdims=True) - fading
        grad_gamma = grad_gamma + jnp.sum(energy, axis=-1, keepdims=True)
        at_end = jnp.sum(fading, axis=0, keepdims=True) + jnp.exp(final) * jnp.sum(
            jnp.sum(state * leaving, axis=1, keepdims=True), axis=0, keepdims=True
        )
        grad_gamma = grad_gamma + jnp.where(iota((size, 1), 0) == size - 1, at_end, 0.0)
        column_sums.append(jnp.sum(energy, axis=0, keepdims=True))
        grad_gammas = grad_gammas + jnp.where(lanes == h, grad_gamma, 0.0)
        grad_betas = grad_betas + jnp.where(lanes == heads + h, grad_beta, 0.0)

        projected = proj_ref[:, h * CONV : (h + 1) * CONV]
        taps = taps_ref[:, h]
        extended, mixed, gate, (q_raw, q_scale), (k_raw, k_scale), *_ = mixer_inputs(projected, taps)
        grad_active = jnp.concatenate(
            [
                norm_back(grad_queries * DK ** (-0.5), q_raw, q_scale),
                norm_back(grad_keys, k_raw, k_scale),
                grad_values,
            ],
            axis=1,
        )
        grad_mixed = grad_active * gate * (1.0 + mixed * (1.0 - gate))
        padding = jnp.zeros((HALO, CONV), F32)
        full = jnp.concatenate([padding, grad_mixed, padding], axis=0)
        total = None
        for j in range(KW):
            shift = KW - 1 - j
            moved = full if shift == 0 else pltpu.roll(full, size + 2 * HALO - shift, 0)
            term = taps[j : j + 1] * moved[: size + HALO]
            total = term if total is None else total + term
            back = extended if shift == 0 else pltpu.roll(extended, shift, 0)
            taps_out_ref[j : j + 1, h * CONV : (h + 1) * CONV] = jnp.sum(
                grad_mixed * back[HALO:], axis=0, keepdims=True
            )
        halo_out[h] = total[:HALO]
        tails[h] = total[size:]
        out_ref[:, h * CONV : (h + 1) * CONV] = total[HALO:].astype(BF16)
        copies.append(send(halo_out.at[h], halo_in.at[h], halo_s, halo_r, h, previous))
        upper = (pl.ds(0, body), pl.ds(h * CONV, CONV))
        copies.append(send(out_ref.at[upper], sibling_ref.at[upper], body_s, body_r, h, sibling))
        for stage in beside[h]:
            next(stage)

    beta, decay, _, _, pre = gate_values
    sums_ref[...] = jnp.zeros_like(sums_ref)
    for h in range(heads):
        sums_ref[h : h + 1] = column_sums[h]
    wide = grad_gammas - sums_ref[...].T
    grad_decay = mm((columns >= rows).astype(F32), wide, EXACT)
    grad_pre = jnp.where(lanes < heads, -jnp.exp(lane_values(log_ref, heads)) * jax.nn.sigmoid(pre) * grad_decay, 0.0)
    out_ref[:, heads * CONV :] = (grad_pre + grad_betas * beta * (1.0 - beta)).astype(BF16)
    scales_out_ref[...] = jnp.zeros_like(scales_out_ref)
    scales_out_ref[0:1] = jnp.sum(grad_decay * decay, axis=0, keepdims=True)
    scales_out_ref[1:2] = jnp.sum(grad_pre, axis=0, keepdims=True)
    side = (pl.ds(0, size), pl.ds(heads * CONV, LANES))
    last = [send(out_ref.at[side], sibling_ref.at[side], rate_s, rate_r, 0, sibling)]
    for copy in copies:
        copy.wait()
    for h in range(heads):
        arrived = jnp.where(seq < peers - 1, halo_in[h], 0.0)
        fixed = tails[h] + arrived
        out_ref[body:, h * CONV : (h + 1) * CONV] = fixed.astype(BF16)
        lower = (pl.ds(body, HALO), pl.ds(h * CONV, CONV))
        last.append(send(out_ref.at[lower], sibling_ref.at[lower], tail_s, tail_r, h, sibling))
    for copy in last:
        copy.wait()
    io.leave(out_ref, sibling_ref, taps_out_ref, scales_out_ref)
    finish(output, sum_o, sum_g)


def chunks_of(units):
    return [(at, min(2 * LANES, units - at)) for at in range(0, units, 2 * LANES)]


def ffn_kernel(
    slab, io, second_ref, cotangent_ref, middle_ref, gain_ref, weights_ref,
    branch_ref, grad_ref, grad_gain_ref, ffn_ref, gate_up_ref, down_a_ref, down_b_ref,
    weights, down, hidden, grad_hidden, second_split, cotangent_split, second_sib, cotangent_sib, hidden_sib, grad_sib,
    part, landing, gate_up_part, part_a, part_b, land_a, land_b, mid_a, mid_b, land_a2, land_b2,
    load_s, down_s, store_s, half_s, half_r, hid_s, hid_r, gra_s, gra_r, red_s, red_r, gat_s, gat_r,
    a1_s, a1_r, b1_s, b1_r, a2_s, a2_r, b2_s, b2_r,
):
    seq, head = lax.axis_index("seq"), lax.axis_index("head")
    ring_x, ring_y, ring_z = ring_ids("x"), ring_ids("y"), ring_ids("z")
    sibling = (seq + 1 - 2 * (seq % 2), head)
    all_here = say_here(ring_x[4:] + ring_y[4:] + ring_z[4:] + (sibling,))
    count, width = second_ref.shape
    units = hidden.shape[1]
    chunks = chunks_of(units)
    ahead = 2

    def load(i):
        at, length = chunks[i]
        both, down_from = pl.ds(2 * at, 2 * length), pl.ds(2 * units + at, length)
        return [
            pltpu.make_async_copy(weights_ref.at[:, both], weights.at[:, both], load_s.at[i]),
            pltpu.make_async_copy(weights_ref.at[:, down_from], down.at[:, pl.ds(at, length)], down_s.at[i]),
        ]

    loads = [load(i) for i in range(len(chunks))]
    for copy in [copy for pair in loads[:ahead] for copy in pair]:
        copy.start()
    io.arrive(second_ref, cotangent_ref)
    second_split[...] = split_by_core(second_ref[...].astype(F32), slab).astype(BF16)
    cotangent_split[...] = split_by_core(cotangent_ref[...].astype(F32), slab).astype(BF16)
    all_here()
    aside = [
        send(other_half(second_split), second_sib, half_s, half_r, 0, sibling),
        send(other_half(cotangent_split), cotangent_sib, half_s, half_r, 1, sibling),
    ]
    step = 512
    for i, (at, length) in enumerate(chunks):
        if i + ahead < len(chunks):
            for copy in loads[i + ahead]:
                copy.start()
        for copy in loads[i]:
            copy.wait()
        z = mm(second_ref[...], weights[:, pl.ds(2 * at, length)])
        u = mm(second_ref[...], weights[:, pl.ds(2 * at + length, length)])
        here, both = pl.ds(at, length), pl.ds(2 * at, 2 * length)
        g = mm(cotangent_ref[...], down[:, here])
        s = jax.nn.sigmoid(z)
        silu = z * s
        hidden[:, here] = (silu * u).astype(BF16)
        grad_hidden[:, pl.ds(2 * at, length)] = (g * u * s * (1.0 + z * (1.0 - s))).astype(BF16)
        grad_hidden[:, pl.ds(2 * at + length, length)] = (g * silu).astype(BF16)
        aside.append(send(hidden.at[:, here], hidden_sib.at[:, here], hid_s, hid_r, i, sibling))
        aside.append(send(grad_hidden.at[:, both], grad_sib.at[:, both], gra_s, gra_r, i, sibling))
    reduces = []
    for k, columns in enumerate(column_halves(width)):

        @pl.loop(2 * k, 2 * k + 2)
        def _(n):
            rows = pl.ds(pl.multiple_of(n * step, step), step)
            product = mmt(grad_hidden[...], weights[rows])
            for p in range(part.shape[0]):
                m = part.shape[1]
                part[p, :, rows] = product[p * m : (p + 1) * m].astype(BF16)

        blocks, result = part.at[:, :, columns], grad_ref.at[:, columns]
        reduces.append(ring_reduce(ring_y, blocks, result, landing.at[k], red_s.at[k], red_r.at[k]))
        next(reduces[k])
    for copy in aside:
        copy.wait()
    wide_a, wide_b = part_a.shape[2], part_b.shape[2]
    weight_blocks(cotangent_split, cotangent_sib, hidden, hidden_sib, pl.ds(0, wide_a), part_a, slab, False)
    sum_a = sum_both(ring_x, ring_z, part_a, mid_a, down_a_ref, land_a, land_a2, (a1_s, a1_r, a2_s, a2_r))
    next(sum_a)
    weight_blocks(cotangent_split, cotangent_sib, hidden, hidden_sib, pl.ds(wide_a, wide_b), part_b, slab, True)
    sum_b = sum_both(ring_z, ring_x, part_b, mid_b, down_b_ref, land_b, land_b2, (b1_s, b1_r, b2_s, b2_r))
    next(sum_b)
    for reduce in reduces:
        next(reduce)

    @pl.loop(0, width // step)
    def _(n):
        rows = pl.ds(pl.multiple_of(n * step, step), step)
        product = mmt(hidden[...], down[rows])
        for p in range(ffn_ref.shape[0]):
            m = ffn_ref.shape[1]
            ffn_ref[p, :, rows] = product[p * m : (p + 1) * m].astype(BF16)

    io.leave(ffn_ref)
    io.arrive(middle_ref, gain_ref)
    finish(*reduces)
    back, grad_gain = rms_back(grad_ref[...], middle_ref[...], gain_ref[...])
    grad = cotangent_ref[pl.ds(pl.multiple_of(ring_y[0] * slab, slab), slab)].astype(F32) + back
    branch_ref[ring_y[0]] = grad.astype(BF16)
    gather = ring_gather(ring_y, branch_ref, gat_s, gat_r)
    next(gather)
    grad_ref[...] = grad
    grad_gain_ref[...] = grad_gain
    io.leave(grad_ref, grad_gain_ref)
    next(sum_a)
    next(sum_b)
    weight_blocks(
        second_split, second_sib, grad_hidden, grad_sib, pl.ds(0, grad_hidden.shape[1]), gate_up_part, slab, False
    )
    store = pltpu.make_async_copy(gate_up_part, gate_up_ref, store_s)
    store.start()
    next(gather)
    next(sum_a)
    next(sum_b)
    finish(gather)
    io.leave(branch_ref)
    finish(sum_a, sum_b)
    store.wait()


def small_sum(value, mask, outgoing, incoming, sends, receives, result):
    seq, head = lax.axis_index("seq"), lax.axis_index("head")
    x, z, core = seq // 8, (seq // 2) % 4, seq % 2
    stages = [
        ([(seq, lax.rem(head + d, 4)) for d in (1, 2, 3)], mask),
        ([(lax.rem(x + d, 4) * 8 + seq % 8, head) for d in (1, 2, 3)], None),
        ([(x * 8 + lax.rem(z + d, 4) * 2 + core, head) for d in (1, 2, 3)], None),
        ([(seq + 1 - 2 * core, head)], None),
    ]
    slot = 0
    for stage, (peers, only) in enumerate(stages):
        outgoing[stage] = value
        copies = []
        for peer in peers:
            copies.append((slot, send(outgoing.at[stage], incoming.at[slot], sends, receives, slot, peer)))
            slot += 1
        yield
        for at, copy in copies:
            copy.wait()
            value = value + (incoming[at] if only is None else jnp.where(only, incoming[at], 0.0))
    result[...] = value


def last_kernel(
    slab, io, gate_ref, tokens_ref, middle_grad_ref, gain_ref, ffn_gain_ref, out_gain_ref, scales_ref, taps_ref,
    split_ref, split_sib_ref, proj_ref, proj_sib_ref, weights_ref,
    low_ref, small_out_ref, late_out_ref, first_a_ref, first_b_ref,
    weights, small_ref, late_ref, part_n, land_n, sum_n, swap_out, swap_in, late_out, late_in, part_a, part_b, land_a, land_b, mid_a, mid_b, land_a2, land_b2,
    load_s, rn_s, rn_r, gn_s, gn_r, sw_s, sw_r, la_s, la_r, a1_s, a1_r, b1_s, b1_r, a2_s, a2_r, b2_s, b2_r,
):
    seq, head = lax.axis_index("seq"), lax.axis_index("head")
    ring_x, ring_y, ring_z = ring_ids("x"), ring_ids("y"), ring_ids("z")
    sibling = (seq + 1 - 2 * (seq % 2), head)
    across = (
        (lax.rem(seq + 16, 32), head),
        (seq, lax.rem(head + 2, 4)),
        ((seq // 8) * 8 + lax.rem((seq // 2) % 4 + 2, 4) * 2 + seq % 2, head),
    )
    all_here = say_here(ring_x[4:] + ring_y[4:] + ring_z[4:] + across + (sibling,))
    width, wide = weights.shape
    step = 512

    def load(k):
        rows = pl.ds(pl.multiple_of(k * step, step), step)
        return pltpu.make_async_copy(weights_ref.at[rows, pl.ds(0, wide)], weights.at[rows], load_s.at[k])

    io.arrive(ffn_gain_ref, out_gain_ref, scales_ref, taps_ref)
    small_ref[...] = jnp.zeros_like(small_ref)
    small_ref[1:2] = ffn_gain_ref[...]
    small_ref[2:3, :DV] = out_gain_ref[...]
    small_ref[2:3, DV : DV + LANES] = scales_ref[0:1]
    small_ref[2:3, DV + LANES : DV + 2 * LANES] = scales_ref[1:2]
    small_ref[3 : 3 + KW] = taps_ref[...]
    me = ring_y[0]
    wide_a, wide_b = part_a.shape[2], part_b.shape[2]
    narrow = proj_ref.shape[1]
    io.arrive(split_ref, split_sib_ref, proj_ref, proj_sib_ref)
    io.fetch(gate_ref, gain_ref, tokens_ref, middle_grad_ref)
    for k in range(width // step):
        load(k).start()
    weight_blocks(split_ref, split_sib_ref, proj_ref, proj_sib_ref, pl.ds(0, wide_a), part_a, slab, False)
    all_here()
    sum_a = sum_both(ring_x, ring_z, part_a, mid_a, first_a_ref, land_a, land_a2, (a1_s, a1_r, a2_s, a2_r))
    next(sum_a)
    weight_blocks(split_ref, split_sib_ref, proj_ref, proj_sib_ref, pl.ds(wide_a, wide_b), part_b, slab, True)
    sum_b = sum_both(ring_z, ring_x, part_b, mid_b, first_b_ref, land_b, land_b2, (b1_s, b1_r, b2_s, b2_r))
    next(sum_b)
    rows8, lanes = iota(small_ref.shape, 0), iota(small_ref.shape, 1)
    shared = (rows8 < 2) | ((rows8 == 2) & (lanes < DV))
    small = small_sum(small_ref[...], shared, swap_out, swap_in, sw_s, sw_r, small_out_ref)
    next(small)
    io.arrive(gate_ref, tokens_ref, middle_grad_ref, gain_ref)
    reduces = []
    for k, columns in enumerate(column_halves(width)):

        @pl.loop(2 * k, 2 * k + 2)
        def _(n):
            load(n).wait()
            rows = pl.ds(pl.multiple_of(n * step, step), step)
            product = mmt(proj_ref[...], weights[rows, :narrow]) + mmt(gate_ref[...], weights[rows, narrow:])
            for p in range(part_n.shape[0]):
                m = part_n.shape[1]
                part_n[p, :, rows] = product[p * m : (p + 1) * m].astype(BF16)

        blocks, result = part_n.at[:, :, columns], sum_n.at[:, columns]
        reduces.append(ring_reduce(ring_y, blocks, result, land_n.at[k], rn_s.at[k], rn_r.at[k]))
        next(reduces[k])
    next(small)
    for reduce in reduces:
        next(reduce)
    next(sum_a)
    next(sum_b)
    next(small)
    finish(*reduces)
    back, grad_gain = rms_back(sum_n[...], tokens_ref[me].astype(F32), gain_ref[...])
    low_ref[me] = (middle_grad_ref[...] + back).astype(BF16)
    gather_n = ring_gather(ring_y, low_ref, gn_s, gn_r)
    next(gather_n)
    wide_late = late_ref.shape[1]
    for r in range(late_ref.shape[0]):
        late_ref[r : r + 1] = grad_gain[:, r * wide_late : (r + 1) * wide_late]
    late = small_sum(late_ref[...], None, late_out, late_in, la_s, la_r, late_out_ref)
    next(late)
    next(small)
    next(sum_a)
    next(sum_b)
    next(late)
    next(gather_n)
    next(late)
    next(sum_a)
    next(sum_b)
    next(late)
    finish(late, small, gather_n, sum_a, sum_b)


def finish_kernel(
    heads, io, first_a_ref, first_b_ref, first_out_ref, first_gate_ref, gate_up_in_ref, down_a_ref, down_b_ref, low_ref, small_ref, late_ref, output_in_ref,
    in_ref, rate_ref, out_ref, gate_up_ref, down_ref, tokens_ref, taps_ref, mixer_gain_ref, ffn_gain_ref, out_gain_ref,
    log_out_ref, bias_out_ref, output_ref,
):
    io.arrive(low_ref)
    tokens_ref[...] = low_ref[...].astype(F32)
    io.leave(tokens_ref)
    io.arrive(gate_up_in_ref)
    for at, length in chunks_of(down_ref.shape[1]):
        for g in range(2):
            gate_up_ref[:, g, at : at + length] = gate_up_in_ref[:, pl.ds(2 * at + g * length, length)].astype(F32)
    io.leave(gate_up_ref)
    io.arrive(first_a_ref, first_b_ref, first_gate_ref, first_out_ref, small_ref, late_ref, down_a_ref, down_b_ref)
    both = jnp.concatenate([first_a_ref[...], first_b_ref[...]], axis=1)
    for h in range(heads):
        in_ref[:, h, :CONV] = both[:, h * CONV : (h + 1) * CONV]
        in_ref[:, h, CONV:] = first_gate_ref[:, h * DV : (h + 1) * DV]
        out_ref[:, h] = first_out_ref[:, h * DV : (h + 1) * DV]
        taps_ref[:, h] = small_ref[3 : 3 + KW, h * CONV : (h + 1) * CONV]
    io.leave(in_ref, out_ref)
    rates = heads * CONV
    turned = both[:, rates : rates + LANES].T
    for g in range(2):
        rate_ref[g] = turned[g * heads : (g + 1) * heads]
    io.arrive(output_in_ref)
    output_ref[...] = output_in_ref[...]
    io.leave(output_ref)
    log_out_ref[...] = small_ref[2, DV : DV + heads]
    bias_out_ref[...] = small_ref[2, DV + LANES : DV + LANES + heads]
    down_ref[:, : down_a_ref.shape[1]] = down_a_ref[...]
    down_ref[:, down_a_ref.shape[1] :] = down_b_ref[...]
    for r in range(late_ref.shape[0]):
        mixer_gain_ref[pl.ds(r * late_ref.shape[1], late_ref.shape[1])] = late_ref[r]
    ffn_gain_ref[...] = small_ref[1]
    out_gain_ref[...] = small_ref[2, :DV]


def gather_rings(slab_ref, full_ref, core_s, core_r, ring_s, ring_r, done):
    seq, head = lax.axis_index("seq"), lax.axis_index("head")
    core = seq % 2
    sibling = (seq + 1 - 2 * core, head)
    ring_x, ring_z = ring_ids("x"), ring_ids("z")
    x, z = ring_x[0], ring_z[0]
    rows, wide = slab_ref.shape
    cut = -(-wide // (2 * LANES)) * LANES
    counts = {"core": 0, "ring": 0}

    def slot(kind):
        counts[kind] += 1
        return counts[kind] - 1

    def across(source, target):
        return send(source, target, core_s, core_r, slot("core"), sibling)

    own_across = across(slab_ref, full_ref.at[x, z, core])
    half = rows // 2
    upper, lower, everything = pl.ds(0, half), pl.ds(half, half), pl.ds(0, rows)

    def round_ring(ring, at, source, arrived, ended):
        me, right, left, opposite, right_id, left_id = ring

        def go(place, part, peer):
            origin = source(part) if place is me else at(place, part)
            return send(origin, at(place, part), ring_s, ring_r, slot("ring"), peer)

        upper_right = go(me, upper, right_id)
        lower_left = go(me, lower, left_id)
        lower_right = go(me, lower, right_id)
        upper_left = go(me, upper, left_id)
        yield
        upper_right.wait()
        far_right = go(left, upper, right_id)
        lower_left.wait()
        far_left = go(right, lower, left_id)
        yield
        lower_right.wait()
        arrived(left)
        upper_left.wait()
        arrived(right)
        yield
        far_right.wait()
        far_left.wait()
        arrived(opposite)
        ended()

    active = []
    for ring_1, ring_2, columns, x_first in (
        (ring_x, ring_z, pl.ds(0, cut), True),
        (ring_z, ring_x, pl.ds(cut, wide - cut), False),
    ):
        def place_of(first, second, part, columns=columns, x_first=x_first):
            where = (first, second) if x_first else (second, first)
            return full_ref.at[where[0], where[1], core, part, columns]

        def start_second(first, copies, source=None, ring_2=ring_2, place_of=place_of, x_first=x_first, columns=columns):
            def at(place, part):
                return place_of(first, place, part)

            def arrived(place):
                copies.append(across(at(place, everything), at(place, everything)))

            def ended():
                done(x_first, first, columns, copies)

            ring = round_ring(ring_2, at, source or (lambda part: at(ring_2[0], part)), arrived, ended)
            next(ring)
            active.append(ring)

        def at_first(place, part, ring_2=ring_2, place_of=place_of):
            return place_of(place, ring_2[0], part)

        def arrived_first(place, at_first=at_first, start_second=start_second):
            start_second(place, [across(at_first(place, everything), at_first(place, everything))])

        def mine(part, columns=columns):
            return slab_ref.at[part, columns]

        ring = round_ring(ring_1, at_first, mine, arrived_first, lambda: None)
        next(ring)
        active.append(ring)
        start_second(ring_1[0], [own_across] if x_first else [], mine)
    while active:
        yield
        ended = []
        for stage in list(active):
            if next(stage, active) is active:
                ended.append(stage)
        active[:] = [stage for stage in active if stage not in ended]


def project_kernel(
    heads, io, in_ref, rate_ref, out_weight_ref, gate_up_ref, down_ref, tokens_ref, gain_ref,
    full_ref, proj_ref, split_ref, split_sib_ref, out_slab_ref, rest_ref,
    slab_ref, turned, weights, normed, halo_in, own_s, store_s, halo_s, halo_r, half_s, half_r, core_s, core_r, ring_s, ring_r,
):
    seq, head = lax.axis_index("seq"), lax.axis_index("head")
    peers = lax.axis_size("seq")
    core = seq % 2
    sibling = (seq + 1 - 2 * core, head)
    before, after = (lax.rem(seq + peers - 1, peers), head), (lax.rem(seq + 1, peers), head)
    ring_x, ring_z = ring_ids("x"), ring_ids("z")
    rows, wide = slab_ref.shape
    count, width = tokens_ref.shape
    all_here = say_here(ring_x[4:] + ring_z[4:] + (sibling, before, after))
    io.arrive(in_ref, rate_ref)
    gate_at = heads * CONV + LANES
    mixer = in_ref[...].astype(F32)
    rates = rate_ref[...].astype(F32)
    turned[...] = jnp.zeros_like(turned)
    for g in range(2):
        turned[g * heads : (g + 1) * heads] = rates[g]
    slab_ref[:, heads * CONV : gate_at] = turned[...].T.astype(BF16)
    for h in range(heads):
        slab_ref[:, h * CONV : (h + 1) * CONV] = mixer[:, h, :CONV].astype(BF16)
        slab_ref[:, gate_at + h * DV : gate_at + (h + 1) * DV] = mixer[:, h, CONV:].astype(BF16)
    own = pltpu.make_async_copy(slab_ref, weights.at[ring_x[0], ring_z[0], core], own_s)
    own.start()
    all_here()
    ready = []
    gather = gather_rings(slab_ref, weights, core_s, core_r, ring_s, ring_r, lambda *group: ready.append(group))
    next(gather)
    io.arrive(tokens_ref, gain_ref)
    halo = send(tokens_ref.at[pl.ds(count - HALO, HALO)], halo_in, halo_s, halo_r, 0, after)

    def norm(values):
        return values * rms_scale(values) * gain_ref[...]

    fresh = norm(tokens_ref[...].astype(F32))
    normed[HALO:] = fresh.astype(BF16)
    split_ref[...] = split_by_core(normed[HALO:].astype(F32), rows).astype(BF16)
    half = send(other_half(split_ref), split_sib_ref, half_s, half_r, 0, sibling)
    io.leave(split_ref)
    io.arrive(out_weight_ref, gate_up_ref, down_ref)
    out_weight = out_weight_ref[...].astype(F32)
    for h in range(heads):
        out_slab_ref[:, h * DV : (h + 1) * DV] = out_weight[:, h].astype(BF16)
    gate_up = gate_up_ref[...].astype(F32)
    for at, length in chunks_of(down_ref.shape[1]):
        here = slice(at, at + length)
        for g in range(2):
            rest_ref[:, 2 * at + g * length : 2 * at + (g + 1) * length] = gate_up[:, g, here].astype(BF16)
    rest_ref[:, 2 * down_ref.shape[1] :] = down_ref[...]
    io.leave(out_slab_ref, rest_ref)
    halo.wait()
    normed[:HALO] = jnp.where(seq > 0, norm(halo_in[...].astype(F32)), 0.0).astype(BF16)
    own.wait()
    half.wait()
    io.leave(split_sib_ref)
    stores, started = [], set()
    slabs = 2 * rows
    chip_rows = 4 * slabs

    def use(group):
        x_first, place, columns, copies = group
        for copy in copies:
            copy.wait()
        if x_first:
            left = normed[:, pl.ds(pl.multiple_of(place * chip_rows, chip_rows), chip_rows)]
            source, target = weights.at[place], full_ref.at[place]
        else:
            left = jnp.concatenate(
                [
                    normed[:, pl.ds(pl.multiple_of(k * chip_rows + place * slabs, slabs), slabs)]
                    for k in range(width // chip_rows)
                ],
                axis=1,
            )
            source, target = weights.at[:, place], full_ref.at[:, place]
        region = (slice(None), slice(None), slice(None), columns)
        store = pltpu.make_async_copy(source.at[region], target.at[region], store_s.at[len(stores)])
        store.start()
        stores.append(store)
        at, end = columns.start, columns.start + columns.size
        first_use = x_first not in started
        started.add(x_first)
        while at < end:
            length = min(4 * LANES, end - at)
            here = pl.ds(at, length)
            right = source[:, :, :, here].reshape(chip_rows, length)
            product = mm(left, right)
            if first_use:
                proj_ref[:, here] = product
            else:
                proj_ref[:, here] += product
            at += length

    running = True
    while running or ready:
        if running:
            running = next(gather, gather) is not gather
        if ready:
            use(ready.pop(0))
    for store in stores:
        store.wait()


def forward_kernel(
    heads, slab, groups, io, proj_ref, taps_ref, log_ref, bias_ref, out_gain_ref, slab_ref, tokens_ref, ffn_gain_ref,
    q_ref, k_ref, v_ref, inv_ref, map_ref, mixed_ref, gated_ref, entering_ref, kept_ref, totals_ref,
    out_full_ref, second_ref, middle_ref,
    weights, out_local, pack, near_in, before, far_out, far_in, back_out, back_in, part, landing,
    own_s, store_s, core_s, core_r, ring_s, ring_r,
    near_s, near_r, far_s, far_r, back_s, back_r, red_s, red_r, gat_s, gat_r,
):
    size = proj_ref.shape[0] - HALO
    members = pack.shape[0]
    member, group, near, near_ids, far_ids = scan_places(members, groups)
    ring_y = ring_ids("y")
    all_here = say_here([*near_ids[1:], *far_ids[1:], *ring_y[4:]])
    io.arrive(slab_ref)
    own = pltpu.make_async_copy(
        slab_ref, weights.at[lax.axis_index("seq") // 8, (lax.axis_index("seq") // 2) % 4, lax.axis_index("seq") % 2], own_s
    )
    own.start()
    rows, columns = triangles(size)
    io.arrive(proj_ref, taps_ref)
    rates = proj_ref[HALO:, heads * CONV : heads * CONV + LANES]
    gate_values = gates(rates, log_ref, bias_ref, heads)
    arrived = []
    gather = gather_rings(slab_ref, weights, core_s, core_r, ring_s, ring_r, lambda *group: arrived.extend(group[3]))
    lower, kept = [], []
    for h in range(heads):
        projected = proj_ref[:, h * CONV : (h + 1) * CONV]
        taps = taps_ref[:, h]
        *_, queries, keys, values = mixer_inputs(projected, taps)
        q_ref[h], k_ref[h], v_ref[h] = queries, keys, values
        beta, gamma, gamma_row = of_head(gate_values, h, heads)
        spread = decays_of(gamma, gamma_row)
        lower.append(jnp.where(columns < rows, beta * spread * mmt(keys, keys), 0.0))
        kept.append((queries, keys, values, beta, gamma, spread))
        if h == 0:
            all_here()
            next(gather)

    io.leave(q_ref, k_ref, v_ref)

    def between(width):
        if width in (32, 128):
            next(gather, None)

    inverses = inverse(lower, between)
    written = []
    for h in range(heads):
        queries, keys, values, beta, gamma, spread = kept[h]
        inv_ref[h] = inverses[h]
        growth = jnp.exp(gamma)
        targets = jnp.concatenate([growth * beta * keys.astype(F32), beta * values.astype(F32)], axis=1)
        written.append(mm(inverses[h], targets, FINE))
        final = gamma[size - 1 : size]
        faded = jnp.exp(final - gamma) * keys.astype(F32)
        summary = mtm(faded, written[h], FINE)
        unit = (iota((DK, DK), 0) == iota((DK, DK), 1)).astype(F32)
        passed = (jnp.exp(final) * unit - summary[:, :DK]).astype(BF16)
        for half in range(HALVES):
            pack[HALVES * h + half, :, :DK] = passed
            pack[HALVES * h + half, :, DK:] = summary[:, (half + 1) * DK : (half + 2) * DK].astype(BF16)
    io.leave(inv_ref)
    copies = [send(pack.at[near[d]], near_in.at[member], near_s, near_r, d, near_ids[d]) for d in range(1, members)]
    near_in[member] = pack[member]
    next(gather, None)
    for h in range(heads):
        queries, keys, values, beta, gamma, spread = kept[h]
        through = mm(spread * mmt(queries, keys), written[h])
        map_ref[h] = jnp.exp(gamma) * queries.astype(F32) - through[:, :DK]
        out_local[h] = through[:, DK:]
    io.leave(map_ref)
    for copy in copies:
        copy.wait()
    unit = (iota((DK, DK), 0) == iota((DK, DK), 1)).astype(F32)

    def after_this(later, earlier):
        moved = mm(later[:, :DK], earlier, FINE)
        return jnp.concatenate([moved[:, :DK], moved[:, DK:] + later[:, DK:]], axis=1)

    tree = [near_in[j].astype(F32) for j in range(members)]
    while len(tree) > 1:
        tree = [after_this(tree[k + 1], tree[k]) for k in range(0, len(tree), 2)]
    total = tree[0]
    far_out[...] = total.astype(BF16)
    copies = [send(far_out, far_in.at[group], far_s, far_r, d, far_ids[d]) for d in range(1, groups)]
    far_in[group] = far_out[...]
    next(gather, None)
    total = jnp.concatenate([unit, jnp.zeros((DK, DK), F32)], axis=1)
    for j in range(members):
        before[j] = total
        kept_ref[j] = near_in[j, :, :DK]
        moved = twice(near_in[j, :, :DK], total)
        total = jnp.concatenate([moved[:, :DK], moved[:, DK:] + near_in[j, :, DK:].astype(F32)], axis=1)
    for copy in copies:
        copy.wait()
    state = jnp.zeros((DK, DK), F32)
    for j in range(groups):
        totals_ref[j] = far_in[j, :, :DK]
        fresh = twice(far_in[j, :, :DK], state) + far_in[j, :, DK:].astype(F32)
        state = jnp.where(j < group, fresh, state)
    io.leave(kept_ref, totals_ref)
    for j in range(members):
        back_out[j] = (mm(before[j, :, :DK], state, FINE) + before[j, :, DK:]).astype(BF16)
    copies = [send(back_out.at[near[d]], back_in.at[member], back_s, back_r, d, near_ids[d]) for d in range(1, members)]
    back_in[member] = back_out[member]
    finish(gather)
    for copy in arrived:
        copy.wait()
    own.wait()
    store = pltpu.make_async_copy(weights, out_full_ref, store_s)
    store.start()
    for copy in copies:
        copy.wait()
    entering_ref[...] = back_in[...]
    io.leave(entering_ref)
    io.arrive(out_gain_ref)
    gain = out_gain_ref[...]
    for h in range(heads):
        mixer_out = out_local[h] + mm(map_ref[h], whole_state(back_in, h))
        mixed_ref[h] = mixer_out
        gate = proj_ref[HALO:, gate_columns(heads, h)]
        scale = lax.rsqrt(jnp.mean(mixer_out * mixer_out, axis=-1, keepdims=True) + 1e-05)
        gated = mixer_out * scale * gain * (gate * jax.nn.sigmoid(gate))
        gated_ref[:, h * DV : (h + 1) * DV] = gated.astype(BF16)
    io.leave(mixed_ref, gated_ref)
    chip_rows = 8 * slab
    halves = [(part.at[:, :, columns_], middle_ref.at[:, columns_]) for columns_ in column_halves(part.shape[2])]
    reduces = []
    for k, (blocks, result) in enumerate(halves):

        @pl.loop(2 * k, 2 * k + 2)
        def _(x):
            right = weights[x].reshape(chip_rows, heads * DV)
            product = mmt(gated_ref[...], right)
            at = pl.ds(pl.multiple_of(x * chip_rows, chip_rows), chip_rows)
            for p in range(part.shape[0]):
                n = part.shape[1]
                part[p, :, at] = product[p * n : (p + 1) * n].astype(BF16)

        reduces.append(ring_reduce(ring_y, blocks, result, landing.at[k], red_s.at[k], red_r.at[k]))
        next(reduces[k])
    me = ring_y[0]
    io.arrive(tokens_ref, ffn_gain_ref)
    finish(*reduces)
    middle = tokens_ref[me].astype(F32) + middle_ref[...]
    second_ref[me] = (middle * rms_scale(middle) * ffn_gain_ref[...]).astype(BF16)
    gather_y = ring_gather(ring_y, second_ref, gat_s, gat_r)
    next(gather_y)
    middle_ref[...] = middle
    io.leave(middle_ref)
    finish(gather_y)
    store.wait()


class Staging:
    def __init__(self):
        self.later, self.inputs, self.outputs, self.leaving = {}, {}, {}, []

    def fetch(self, *refs):
        for ref in refs:
            self.inputs[id(ref)] = self.later.pop(id(ref))
            self.inputs[id(ref)].start()

    def arrive(self, *refs):
        for ref in refs:
            self.inputs.pop(id(ref)).wait()

    def leave(self, *refs):
        for ref in refs:
            copy = self.outputs.pop(id(ref))
            copy.start()
            self.leaving.append(copy)

    def end(self):
        for copy in self.inputs.values():
            copy.wait()
        for copy in self.outputs.values():
            copy.start()
        for copy in [*self.leaving, *self.outputs.values()]:
            copy.wait()


def staged_call(kernel, in_specs, out_specs, out_shape, scratch_shapes, compiler_params, name, later=()):
    def is_staged(spec):
        return spec.memory_space == pltpu.VMEM

    anywhere = pl.BlockSpec(memory_space=pl.ANY)

    def run(*args):
        ins = [i for i, spec in enumerate(in_specs) if is_staged(spec)]
        outs = [i for i, spec in enumerate(out_specs) if is_staged(spec)]

        def body(*refs):
            refs = list(refs)
            results = len(args) + len(out_specs)
            staged = refs[results : results + len(ins) + len(outs)]
            in_s, out_s, *rest = refs[results + len(ins) + len(outs) :]
            io = Staging()
            for k, i in enumerate(ins):
                io.later[id(staged[k])] = pltpu.make_async_copy(refs[i], staged[k], in_s.at[k])
                refs[i] = staged[k]
                if i not in later:
                    io.fetch(staged[k])
            for k, i in enumerate(outs):
                at, held = len(args) + i, staged[len(ins) + k]
                io.outputs[id(held)] = pltpu.make_async_copy(held, refs[at], out_s.at[k])
                refs[at] = held
            kernel(io, *refs[:results], *rest)
            io.end()

        return pl.pallas_call(
            body,
            in_specs=[anywhere if is_staged(spec) else spec for spec in in_specs],
            out_specs=[anywhere if is_staged(spec) else spec for spec in out_specs],
            out_shape=out_shape,
            scratch_shapes=[
                *[pltpu.VMEM(args[i].shape, args[i].dtype) for i in ins],
                *[pltpu.VMEM(out_shape[i].shape, out_shape[i].dtype) for i in outs],
                pltpu.SemaphoreType.DMA((len(ins),)),
                pltpu.SemaphoreType.DMA((len(outs),)),
                *scratch_shapes,
            ],
            compiler_params=compiler_params,
            name=name,
        )(*args)

    return run


def pairs(*sizes):
    return [pltpu.SemaphoreType.DMA(size if isinstance(size, tuple) else (size,)) for size in sizes for _ in range(2)]


def per_device(
    tokens,
    mixer_gain,
    in_weight,
    rate_weight,
    conv_weight,
    decay_log,
    decay_bias,
    out_gain,
    out_weight,
    ffn_gain,
    gate_up_weight,
    down_weight,
    cotangent,
):
    count, width = tokens.shape
    heads = in_weight.shape[1]
    hidden_units = down_weight.shape[1]
    slab = in_weight.shape[0]
    projections = heads * PROJ + LANES
    units = heads * HALVES
    peers, sharers = lax.axis_size("seq"), lax.axis_size("head")
    groups = peers // units
    rows = count // sharers

    convolved_wide = heads * CONV + LANES
    out_wide = heads * DV
    anywhere = pl.BlockSpec(memory_space=pl.ANY)
    in_vmem = pl.BlockSpec(memory_space=pltpu.VMEM)

    def landing(*shape):
        return pltpu.VMEM((6, *shape), BF16)

    blocked = (sharers, rows, width)
    stacked = (4, 4, 2, slab)
    first_full, projected, normed_split, normed_sibling, out_slab, rest = staged_call(
        functools.partial(project_kernel, heads),
        in_specs=[in_vmem] * 7,
        out_specs=[anywhere] + [in_vmem] * 5,
        out_shape=[
            jax.ShapeDtypeStruct((*stacked, projections), BF16),
            jax.ShapeDtypeStruct((HALO + count, projections), F32),
            jax.ShapeDtypeStruct((count, width), BF16),
            jax.ShapeDtypeStruct((count, width // 2), BF16),
            jax.ShapeDtypeStruct((slab, out_wide), BF16),
            jax.ShapeDtypeStruct((slab, 3 * hidden_units), BF16),
        ],
        scratch_shapes=[
            pltpu.VMEM((slab, projections), BF16),
            pltpu.VMEM((LANES, slab), F32),
            pltpu.VMEM((*stacked, projections), BF16),
            pltpu.VMEM((HALO + count, width), BF16),
            pltpu.VMEM((HALO, width), BF16),
            pltpu.SemaphoreType.DMA,
            pltpu.SemaphoreType.DMA((8,)),
            *pairs(1, 1, 31, 60),
        ],
        compiler_params=pltpu.CompilerParams(vmem_limit_bytes=VMEM_LIMIT, collective_id=7, has_side_effects=True),
        name="project",
    )(in_weight, jnp.transpose(rate_weight, (1, 2, 0)), out_weight, gate_up_weight, down_weight, tokens, mixer_gain.reshape(1, width))
    rest_full = lax.all_gather(rest, "seq", axis=0, tiled=True)
    first_full = first_full.reshape(width, projections)

    in_smem = pl.BlockSpec(memory_space=pltpu.SMEM)
    gain_row = out_gain.reshape(1, DV)
    block = (DK, DK)
    double = (DK, 2 * DK)
    (
        queries, keys, values, inv, out_map, mixer_out, gated, entering, kept, totals, out_full, second, middle,
    ) = staged_call(
        functools.partial(forward_kernel, heads, slab, groups),
        in_specs=[in_vmem] * 2 + [in_smem] * 2 + [in_vmem] * 4,
        out_specs=[in_vmem] * 10 + [anywhere] + [in_vmem] * 2,
        out_shape=[
            jax.ShapeDtypeStruct((heads, count, DK), BF16),
            jax.ShapeDtypeStruct((heads, count, DK), BF16),
            jax.ShapeDtypeStruct((heads, count, DV), BF16),
            jax.ShapeDtypeStruct((heads, count, count), F32),
            jax.ShapeDtypeStruct((heads, count, DK), F32),
            jax.ShapeDtypeStruct((heads, count, DV), F32),
            jax.ShapeDtypeStruct((count, out_wide), BF16),
            jax.ShapeDtypeStruct((units, *block), BF16),
            jax.ShapeDtypeStruct((units, *block), BF16),
            jax.ShapeDtypeStruct((groups, *block), BF16),
            jax.ShapeDtypeStruct((*stacked, out_wide), BF16),
            jax.ShapeDtypeStruct(blocked, BF16),
            jax.ShapeDtypeStruct((rows, width), F32),
        ],
        scratch_shapes=[
            pltpu.VMEM((*stacked, out_wide), BF16),
            pltpu.VMEM((heads, count, DV), F32),
            pltpu.VMEM((units, *double), BF16),
            pltpu.VMEM((units, *double), BF16),
            pltpu.VMEM((units, *double), F32),
            pltpu.VMEM(double, BF16),
            pltpu.VMEM((groups, *double), BF16),
            pltpu.VMEM((units, *block), BF16),
            pltpu.VMEM((units, *block), BF16),
            pltpu.VMEM(blocked, BF16),
            pltpu.VMEM((2, 6, rows // 2, width // 2), BF16),
            pltpu.SemaphoreType.DMA,
            pltpu.SemaphoreType.DMA,
            *pairs(31, 60, units, groups, units, (2, 6), 6),
        ],
        compiler_params=pltpu.CompilerParams(vmem_limit_bytes=VMEM_LIMIT, collective_id=1, has_side_effects=True),
        name="forward",
    )(
        projected,
        conv_weight,
        decay_log,
        decay_bias,
        gain_row,
        out_slab,
        tokens.reshape(blocked),
        ffn_gain.reshape(1, width),
    )
    out_full = out_full.reshape(width, out_wide)
    second = second.reshape(count, width)
    gate_wide = heads * DV
    many = 4 * slab

    def sums_scratch(wide_1, wide_2):
        return [
            pltpu.VMEM((4, many, wide_1), BF16),
            pltpu.VMEM((4, many, wide_2), BF16),
            landing(many // 2, wide_1),
            landing(many // 2, wide_2),
            pltpu.VMEM((many, wide_1), BF16),
            pltpu.VMEM((many, wide_2), BF16),
            landing(slab // 2, wide_1),
            landing(slab // 2, wide_2),
        ]

    down_a = -(-hidden_units // (2 * LANES)) * LANES
    down_b = hidden_units - down_a
    chunk_count = len(chunks_of(hidden_units))
    grad_branch, grad_middle, grad_ffn_gain, ffn_part, gate_up_part, grad_down_a, grad_down_b = staged_call(
        functools.partial(ffn_kernel, slab),
        in_specs=[in_vmem] * 4 + [anywhere],
        out_specs=[in_vmem] * 4 + [anywhere] + [in_vmem] * 2,
        out_shape=[
            jax.ShapeDtypeStruct(blocked, BF16),
            jax.ShapeDtypeStruct((rows, width), F32),
            jax.ShapeDtypeStruct((1, width), F32),
            jax.ShapeDtypeStruct(blocked, BF16),
            jax.ShapeDtypeStruct((4, many, 2 * hidden_units), BF16),
            jax.ShapeDtypeStruct((slab, down_a), F32),
            jax.ShapeDtypeStruct((slab, down_b), F32),
        ],
        scratch_shapes=[
            pltpu.VMEM((width, 2 * hidden_units), BF16),
            pltpu.VMEM((width, hidden_units), BF16),
            pltpu.VMEM((count, hidden_units), BF16),
            pltpu.VMEM((count, 2 * hidden_units), BF16),
            pltpu.VMEM((count, width), BF16),
            pltpu.VMEM((count, width), BF16),
            pltpu.VMEM((count, width // 2), BF16),
            pltpu.VMEM((count, width // 2), BF16),
            pltpu.VMEM((count, hidden_units), BF16),
            pltpu.VMEM((count, 2 * hidden_units), BF16),
            pltpu.VMEM(blocked, BF16),
            pltpu.VMEM((2, 6, rows // 2, width // 2), BF16),
            pltpu.VMEM((4, many, 2 * hidden_units), BF16),
            *sums_scratch(down_a, down_b),
            pltpu.SemaphoreType.DMA((chunk_count,)),
            pltpu.SemaphoreType.DMA((chunk_count,)),
            pltpu.SemaphoreType.DMA,
            *pairs(2, chunk_count, chunk_count, (2, 6), 6, 6, 6, 6, 6),
        ],
        compiler_params=pltpu.CompilerParams(vmem_limit_bytes=VMEM_LIMIT, collective_id=3, has_side_effects=True),
        name="ffn",
    )(second, cotangent, middle, ffn_gain.reshape(1, width), rest_full)
    same_core = [[device for device in range(peers) if device % 2 == core] for core in range(2)]
    grad_gate_up_part = lax.psum_scatter(
        gate_up_part.reshape(width // 2, 2 * hidden_units), "seq", scatter_dimension=0, axis_index_groups=same_core, tiled=True
    )
    grad_branch = grad_branch.reshape(count, width)
    (
        grad_projected, grad_sibling, grad_gate, grad_out_gain, grad_taps, grad_scales, first_out, first_gate, output,
    ) = staged_call(
        functools.partial(backward_kernel, heads, slab, groups),
        in_specs=[in_vmem, anywhere] + [in_vmem] * 6 + [in_smem] * 2 + [in_vmem] * 11,
        out_specs=[in_vmem] * 9,
        out_shape=[
            jax.ShapeDtypeStruct((count, convolved_wide), BF16),
            jax.ShapeDtypeStruct((count, convolved_wide), BF16),
            jax.ShapeDtypeStruct((count, gate_wide), BF16),
            jax.ShapeDtypeStruct((1, DV), F32),
            jax.ShapeDtypeStruct((KW, heads * CONV), F32),
            jax.ShapeDtypeStruct((8, LANES), F32),
            jax.ShapeDtypeStruct((slab, gate_wide), F32),
            jax.ShapeDtypeStruct((slab, gate_wide), F32),
            jax.ShapeDtypeStruct(blocked, BF16),
        ],
        scratch_shapes=[
            pltpu.VMEM((width, out_wide), BF16),
            pltpu.VMEM((count, width), BF16),
            pltpu.VMEM((count, width // 2), BF16),
            pltpu.VMEM((count, gate_wide), BF16),
            pltpu.VMEM((count, gate_wide), BF16),
            pltpu.VMEM((heads, count, DV), F32),
            pltpu.VMEM((units, *block), BF16),
            pltpu.VMEM((units, *block), BF16),
            pltpu.VMEM((units, *block), BF16),
            pltpu.VMEM((units, *block), F32),
            pltpu.VMEM((units, *block), F32),
            pltpu.VMEM(block, BF16),
            pltpu.VMEM((groups, *block), BF16),
            pltpu.VMEM((units, *block), BF16),
            pltpu.VMEM((units, *block), BF16),
            pltpu.VMEM((LANES, count), F32),
            pltpu.VMEM((heads, count, count), F32),
            pltpu.VMEM((heads, count, DV), F32),
            pltpu.VMEM((heads, count, DV), F32),
            pltpu.VMEM((heads, count, count), F32),
            pltpu.VMEM((heads, count, DV), F32),
            pltpu.VMEM((heads, HALO, CONV), F32),
            pltpu.VMEM((heads, HALO, CONV), F32),
            pltpu.VMEM((heads, HALO, CONV), F32),
            *sums_scratch(gate_wide, gate_wide),
            landing(rows // 2, width),
            pltpu.VMEM((rows, width), F32),
            pltpu.SemaphoreType.DMA,
            *pairs(3, units, groups, units, heads, heads, heads, 1, 6, 6, 6, 6, 6, 6),
        ],
        compiler_params=pltpu.CompilerParams(vmem_limit_bytes=VMEM_LIMIT, collective_id=6, has_side_effects=True),
        name="backward",
        later=(7, 10, 11, 12, 13, 14, 15, 16, 17, 18, 19, 20),
    )(
        grad_branch,
        out_full,
        mixer_out,
        out_map,
        projected,
        gain_row,
        gated,
        conv_weight,
        decay_log,
        decay_bias,
        normed_split,
        normed_sibling,
        kept,
        totals,
        entering,
        queries,
        keys,
        values,
        inv,
        ffn_part,
        middle,
    )
    wide_a = -(-convolved_wide // (2 * LANES)) * LANES
    wide_b = convolved_wide - wide_a
    low, small, late, first_a, first_b = staged_call(
        functools.partial(last_kernel, slab),
        in_specs=[in_vmem] * 12 + [anywhere],
        out_specs=[in_vmem] * 5,
        out_shape=[
            jax.ShapeDtypeStruct(blocked, BF16),
            jax.ShapeDtypeStruct((8, width), F32),
            jax.ShapeDtypeStruct((8, width // 8), F32),
            jax.ShapeDtypeStruct((slab, wide_a), F32),
            jax.ShapeDtypeStruct((slab, wide_b), F32),
        ],
        scratch_shapes=[
            pltpu.VMEM((width, projections), BF16),
            pltpu.VMEM((8, width), F32),
            pltpu.VMEM((8, width // 8), F32),
            pltpu.VMEM(blocked, BF16),
            pltpu.VMEM((2, 6, rows // 2, width // 2), BF16),
            pltpu.VMEM((rows, width), F32),
            pltpu.VMEM((4, 8, width), F32),
            pltpu.VMEM((10, 8, width), F32),
            pltpu.VMEM((4, 8, width // 8), F32),
            pltpu.VMEM((10, 8, width // 8), F32),
            *sums_scratch(wide_a, wide_b),
            pltpu.SemaphoreType.DMA((width // 512,)),
            *pairs((2, 6), 6, 10, 10, 6, 6, 6, 6),
        ],
        compiler_params=pltpu.CompilerParams(vmem_limit_bytes=VMEM_LIMIT, collective_id=5, has_side_effects=True),
        name="last",
        later=(0, 1, 2, 3),
    )(
        grad_gate,
        tokens.reshape(blocked),
        grad_middle,
        mixer_gain.reshape(1, width),
        grad_ffn_gain,
        grad_out_gain,
        grad_scales,
        grad_taps,
        normed_split,
        normed_sibling,
        grad_projected,
        grad_sibling,
        first_full,
    )
    finished = [
        ((slab, heads, PROJ), F32),
        ((2, heads, slab), F32),
        ((slab, heads, DV), F32),
        ((slab, 2, hidden_units), F32),
        ((slab, hidden_units), F32),
        ((count, width), F32),
        ((KW, heads, CONV), F32),
        ((width,), F32),
        ((width,), F32),
        ((DV,), F32),
        ((heads,), F32),
        ((heads,), F32),
        ((count, width), BF16),
    ]
    grad_in, grad_rate, grad_out, grad_gate_up_weight, grad_down, grad_tokens, grad_conv, *gains = staged_call(
        functools.partial(finish_kernel, heads),
        in_specs=[in_vmem] * 11,
        out_specs=[in_vmem if len(shape) > 1 else pl.BlockSpec() for shape, _ in finished],
        out_shape=[jax.ShapeDtypeStruct(shape, kind) for shape, kind in finished],
        scratch_shapes=[],
        compiler_params=pltpu.CompilerParams(vmem_limit_bytes=VMEM_LIMIT),
        name="finish",
    )(
        first_a,
        first_b,
        first_out,
        first_gate,
        grad_gate_up_part,
        grad_down_a,
        grad_down_b,
        low.reshape(count, width),
        small,
        late,
        output.reshape(count, width),
    )
    return (
        gains[5],
        grad_tokens,
        gains[0],
        grad_in,
        jnp.transpose(grad_rate, (2, 0, 1)),
        grad_conv,
        gains[3],
        gains[4],
        gains[2],
        grad_out,
        gains[1],
        grad_gate_up_weight,
        grad_down,
    )


def solution(mesh):
    in_specs = (
        P("seq", None),
        P(),
        P("seq", "head", None),
        P("seq", None, "head"),
        P(None, "head", None),
        P("head"),
        P("head"),
        P(),
        P("seq", "head", None),
        P(),
        P("seq", None, "head"),
        P("seq", "head"),
        P("seq", None),
    )
    out_specs = (
        P("seq", None),
        P("seq", None),
        P(),
        P("seq", "head", None),
        P("seq", None, "head"),
        P(None, "head", None),
        P("head"),
        P("head"),
        P(),
        P("seq", "head", None),
        P(),
        P("seq", None, "head"),
        P("seq", "head"),
    )
    return jax.shard_map(
        per_device, mesh=mesh, in_specs=in_specs, out_specs=out_specs, check_vma=False
    )
```

```python
import functools

import jax
import jax.numpy as jnp
from jax import lax
from jax.experimental import pallas as pl
from jax.experimental.pallas import tpu as pltpu
from jax.sharding import PartitionSpec as P

DK = 128
DV = 256
KW = 4
CONV = 512
PROJ = 768
LANES = 128
HALO = 16
HALVES = DV // DK
MESH = pl.DeviceIdType.MESH

F32 = jnp.float32
BF16 = jnp.bfloat16
EXACT = lax.Precision.HIGHEST
FINE = lax.Precision.HIGH
VMEM_LIMIT = 56 * 1024 * 1024


def dot(a, b, dims, precision=None):
    return lax.dot_general(a, b, (dims, ((), ())), precision=precision, preferred_element_type=F32)


def mm(a, b, precision=None):
    return dot(a, b, ((1,), (0,)), precision)


def mmt(a, b, precision=None):
    return dot(a, b, ((1,), (1,)), precision)


def mtm(a, b, precision=None):
    return dot(a, b, ((0,), (0,)), precision)


def iota(shape, dim):
    return lax.broadcasted_iota(jnp.int32, shape, dim)


def softplus(x):
    return jnp.maximum(x, 0.0) + jnp.log1p(jnp.exp(-jnp.abs(x)))


def split_by_core(values, slab):
    width = values.shape[1]
    lanes = iota((values.shape[0], 2 * slab), 1)
    firsts, seconds = [], []
    for at in range(0, width, 4 * slab):
        a, b = values[:, at : at + 2 * slab], values[:, at + 2 * slab : at + 4 * slab]
        firsts.append(jnp.where(lanes < slab, a, pltpu.roll(b, slab, 1)))
        seconds.append(jnp.where(lanes < slab, pltpu.roll(a, slab, 1), b))
    return jnp.concatenate(firsts + seconds, axis=1)


def triangles(size):
    rows, columns = iota((size, size), 0), iota((size, size), 1)
    return rows, columns


def lane_values(ref, heads):
    lanes = iota((1, LANES), 1)
    total = jnp.zeros((1, LANES), F32)
    for h in range(heads):
        total = total + jnp.where(lanes == h, ref[h], 0.0)
    return total


def gates(rates, log_ref, bias_ref, heads):
    size = rates.shape[0]
    pre = rates + lane_values(bias_ref, heads)
    beta = jax.nn.sigmoid(rates)
    decay = jnp.where(iota(rates.shape, 1) < heads, -jnp.exp(lane_values(log_ref, heads)) * softplus(pre), 0.0)
    rows, columns = triangles(size)
    gamma = mm((columns <= rows).astype(F32), decay, EXACT)
    return beta, decay, gamma, gamma.T, pre


def of_head(gate_values, head, heads):
    beta, _, gamma, gamma_row, _ = gate_values
    return beta[:, heads + head : heads + head + 1], gamma[:, head : head + 1], gamma_row[head : head + 1]


def decays_of(gamma, gamma_row):
    size = gamma.shape[0]
    rows, columns = triangles(size)
    inside = columns <= rows
    return jnp.where(inside, jnp.exp(jnp.where(inside, gamma - gamma_row, 0.0)), 0.0)


def inverse(lower, between):
    size = lower[0].shape[0]
    rows, columns = triangles(size)
    unit = (rows == columns).astype(F32)
    known = [unit - jnp.where(rows // 2 == columns // 2, a, 0.0) for a in lower]
    width = 2
    while width < size:
        fresh = (rows // (2 * width) == columns // (2 * width)) & (rows // width != columns // width)
        parts = [jnp.where(fresh, a, 0.0) for a in lower]
        first = [mm(c, x, FINE) for c, x in zip(parts, known)]
        known = [x - mm(x, y, FINE) for x, y in zip(known, first)]
        width *= 2
        between(width)
    return known


def convolved(extended, taps):
    total = None
    for j in range(KW):
        shift = KW - 1 - j
        moved = extended if shift == 0 else pltpu.roll(extended, shift, 0)
        term = taps[j : j + 1] * moved[HALO:]
        total = term if total is None else total + term
    return total


def unit_rows(values):
    return lax.rsqrt(jnp.sum(values * values, axis=-1, keepdims=True) + 1e-06)


def mixer_inputs(projected, taps):
    extended = projected[:, :CONV].astype(BF16).astype(F32)
    mixed = convolved(extended, taps)
    gate = jax.nn.sigmoid(mixed)
    active = mixed * gate
    q_raw, k_raw = active[:, :DK], active[:, DK : 2 * DK]
    q_scale, k_scale = unit_rows(q_raw), unit_rows(k_raw)
    queries = (q_raw * q_scale * DK ** (-0.5)).astype(BF16)
    keys = (k_raw * k_scale).astype(BF16)
    values = active[:, 2 * DK :].astype(BF16)
    return extended, mixed, gate, (q_raw, q_scale), (k_raw, k_scale), queries, keys, values


def gate_columns(heads, head):
    at = heads * CONV + LANES + head * DV
    return pl.ds(at, DV)


def whole_state(units_ref, head):
    return jnp.concatenate([units_ref[HALVES * head + half] for half in range(HALVES)], axis=1).astype(F32)


def weight_blocks(x, x_sib, y, y_sib, columns, target, slab, z_first):
    places = target.shape[0]
    many = places * slab
    own = lax.axis_index("seq") % 2 * (x.shape[1] // 2)

    @pl.loop(0, places)
    def _(block):
        at = pl.ds(pl.multiple_of(own + block * many, many), many)
        here = pl.ds(pl.multiple_of(block * many, many), many)
        part = (mtm(x[:, at], y[:, columns]) + mtm(x_sib[:, here], y_sib[:, columns])).astype(BF16)
        if z_first:
            rows = pl.ds(pl.multiple_of(block * slab, slab), slab)
            for place in range(places):
                target[place, rows] = part[place * slab : (place + 1) * slab]
        else:
            target[block] = part


def sum_both(first, second, part, middle, result, landing, landing_2, semaphores):
    places, many, wide = part.shape
    yield from ring_reduce(first, part, middle, landing, semaphores[0], semaphores[1])
    blocks = middle.reshape(places, many // places, wide)
    yield from ring_reduce(second, blocks, result, landing_2, semaphores[2], semaphores[3])


def norm_back(grad, values, scale):
    return scale * grad - values * (scale * scale * scale * jnp.sum(values * grad, axis=-1, keepdims=True))


def say_here(peers):
    barrier = pltpu.get_barrier_semaphore()
    for peer in peers:
        pl.semaphore_signal(barrier, inc=1, device_id=peer, device_id_type=MESH)

    def all_here():
        pl.semaphore_wait(barrier, len(peers))

    return all_here


def start_barrier(peers):
    say_here(peers)()


def send(source, target, sends, receives, slot, peer):
    copy = pltpu.make_async_remote_copy(
        src_ref=source,
        dst_ref=target,
        send_sem=sends.at[slot],
        recv_sem=receives.at[slot],
        device_id=peer,
        device_id_type=MESH,
    )
    copy.start()
    return copy


def twice(left, right):
    high = right.astype(BF16)
    low = (right - high.astype(F32)).astype(BF16)
    return mm(left, high) + mm(left, low)


def scan_places(members, groups):
    seq, head = lax.axis_index("seq"), lax.axis_index("head")
    member, group = seq % members, seq // members
    near = [(member + d) % members for d in range(members)]
    far = [(group + d) % groups for d in range(groups)]
    near_ids = [(group * members + place, head) for place in near]
    far_ids = [(place * members + member, head) for place in far]
    return member, group, near, near_ids, far_ids


def other_half(ref):
    half = ref.shape[1] // 2
    at = (1 - lax.axis_index("seq") % 2) * half
    return ref.at[:, pl.ds(pl.multiple_of(at, half), half)]


def ring_ids(axis):
    seq, head = lax.axis_index("seq"), lax.axis_index("head")
    size = {"x": lax.axis_size("seq") // 8, "y": lax.axis_size("head"), "z": 4}[axis]
    me = {"x": seq // 8, "y": head, "z": (seq // 2) % 4}[axis]

    def at(place):
        if axis == "y":
            return (seq, place)
        if axis == "x":
            return (place * 8 + seq % 8, head)
        return ((seq // 8) * 8 + place * 2 + seq % 2, head)

    right, left = lax.rem(me + 1, size), lax.rem(me + size - 1, size)
    return me, right, left, lax.rem(me + 2, size), at(right), at(left)


def add_into(target, pieces, rows):
    step = min(rows, 32)

    @pl.loop(0, rows // step)
    def _(k):
        part = pl.ds(pl.multiple_of(k * step, step), step)
        total = pieces[0][part].astype(F32)
        for piece in pieces[1:]:
            total = total + piece[part].astype(F32)
        target[part] = total.astype(target.dtype)


def ring_reduce(ring, blocks, result, landing, sends, receives):
    me, right, left, across, right_id, left_id = ring
    rows = blocks.shape[1]
    half = rows // 2
    upper, lower = pl.ds(0, half), pl.ds(half, half)
    by_right = send(blocks.at[across, upper], landing.at[0], sends, receives, 0, right_id)
    by_left = send(blocks.at[across, lower], landing.at[1], sends, receives, 1, left_id)
    plain_right = send(blocks.at[right, lower], landing.at[2], sends, receives, 2, right_id)
    plain_left = send(blocks.at[left, upper], landing.at[3], sends, receives, 3, left_id)
    yield
    by_right.wait()
    add_into(landing.at[0], [blocks.at[right, upper], landing.at[0]], half)
    summed_right = send(landing.at[0], landing.at[4], sends, receives, 4, right_id)
    by_left.wait()
    add_into(landing.at[1], [blocks.at[left, lower], landing.at[1]], half)
    summed_left = send(landing.at[1], landing.at[5], sends, receives, 5, left_id)
    yield
    plain_right.wait()
    plain_left.wait()
    summed_right.wait()
    summed_left.wait()
    add_into(result.at[upper], [blocks.at[me, upper], landing.at[4], landing.at[3]], half)
    add_into(result.at[lower], [blocks.at[me, lower], landing.at[2], landing.at[5]], half)


def ring_gather(ring, blocks, sends, receives):
    me, right, left, across, right_id, left_id = ring
    rows = blocks.shape[1]
    half = rows // 2
    upper, lower = pl.ds(0, half), pl.ds(half, half)

    def go(place, part, slot, peer):
        return send(blocks.at[place, part], blocks.at[place, part], sends, receives, slot, peer)

    upper_right = go(me, upper, 0, right_id)
    lower_left = go(me, lower, 1, left_id)
    lower_right = go(me, lower, 2, right_id)
    upper_left = go(me, upper, 3, left_id)
    yield
    upper_right.wait()
    far_right = go(left, upper, 4, right_id)
    lower_left.wait()
    far_left = go(right, lower, 5, left_id)
    yield
    for copy in (lower_right, upper_left, far_right, far_left):
        copy.wait()


def column_halves(width):
    return pl.ds(0, width // 2), pl.ds(width // 2, width // 2)


def finish(*generators):
    active = list(generators)
    while active:
        active = [g for g in active if next(g, active) is not active]


def rms_scale(values):
    return lax.rsqrt(jnp.mean(values * values, axis=-1, keepdims=True) + 1e-05)


def rms_back(grad, values, gain):
    scale = rms_scale(values)
    u = grad * gain
    back = scale * u - values * (scale * scale * scale * jnp.mean(u * values, axis=-1, keepdims=True))
    return back, jnp.sum(grad * values * scale, axis=0, keepdims=True)


def backward_kernel(
    heads, slab, groups, io, branch_ref, out_weight_ref, mixed_ref, map_ref, projected_ref, gain_ref, gated_ref, taps_ref, log_ref, bias_ref,
    normed_split_ref, normed_sib_ref, kept_ref, totals_ref, state_ref, q_ref, k_ref, v_ref, inv_ref, ffn_part_ref, middle_ref, piece_1_ref, piece_2_ref,
    out_ref, sibling_ref, gate_ref, gain_out_ref, taps_out_ref, scales_out_ref, first_out_ref, first_gate_ref, output_ref, up_1_ref, up_2_ref,
    proj_ref, out_weight, branch_split, branch_sib, gated_sib, gate_sib, grad_outs, pack, near_in, turned, before, after, far_out, far_in,
    back_out, back_in, sums_ref, spreads, residuals, writtens, grad_scores_all, partial, halo_out, halo_in, tails,
    part_o, part_g, land_o, land_g, mid_o, mid_g, land_o2, land_g2, land_f, sum_f,
    part_1, part_2, land_1, land_2, mid_1, mid_2, land_12, land_22,
    load_s, piece_s, proj_s, core_s, core_r, near_s, near_r, far_s, far_r, back_s, back_r, halo_s, halo_r, body_s, body_r, tail_s, tail_r,
    rate_s, rate_r, o1_s, o1_r, g1_s, g1_r, o2_s, o2_r, g2_s, g2_r, rf_s, rf_r, gf_s, gf_r,
    p1_s, p1_r, q1_s, q1_r, p2_s, p2_r, q2_s, q2_r,
):
    size = proj_ref.shape[0] - HALO
    seq, head_place = lax.axis_index("seq"), lax.axis_index("head")
    peers = lax.axis_size("seq")
    members = pack.shape[0]
    member, group, near, near_ids, far_ids = scan_places(members, groups)
    ring_x, ring_y, ring_z = ring_ids("x"), ring_ids("y"), ring_ids("z")
    previous, following = (lax.rem(seq + peers - 1, peers), head_place), (lax.rem(seq + 1, peers), head_place)
    sibling = (seq + 1 - 2 * (seq % 2), head_place)
    all_here = say_here([*near_ids[1:], *far_ids[1:], *ring_y[4:], previous, following])
    load = pltpu.make_async_copy(out_weight_ref, out_weight, load_s)
    load.start()
    loads = [
        pltpu.make_async_copy(source, target, piece_s.at[k])
        for k, (source, target) in enumerate(((piece_1_ref, part_1), (piece_2_ref, part_2)))
    ]
    for copy in loads:
        copy.start()
    narrow = heads * CONV + LANES
    parts = (pl.ds(narrow, heads * DV), pl.ds(0, narrow))
    proj_loads = [
        pltpu.make_async_copy(projected_ref.at[:, part], proj_ref.at[:, part], proj_s.at[k]) for k, part in enumerate(parts)
    ]
    proj_loads[0].start()
    io.arrive(branch_ref)
    branch_split[...] = split_by_core(branch_ref[...].astype(F32), slab).astype(BF16)
    all_here()
    io.arrive(gated_ref)
    first_aside = [
        send(other_half(branch_split), branch_sib, core_s, core_r, 0, sibling),
        send(gated_ref, gated_sib, core_s, core_r, 1, sibling),
    ]

    def output_sum():
        yield from ring_reduce(ring_y, ffn_part_ref, sum_f, land_f, rf_s, rf_r)
        output_ref[ring_y[0]] = (middle_ref[...] + sum_f[...]).astype(BF16)
        yield from ring_gather(ring_y, output_ref, gf_s, gf_r)

    for copy in loads:
        copy.wait()
    sum_1 = sum_both(ring_x, ring_z, part_1, mid_1, up_1_ref, land_1, land_12, (p1_s, p1_r, q1_s, q1_r))
    sum_2 = sum_both(ring_z, ring_x, part_2, mid_2, up_2_ref, land_2, land_22, (p2_s, p2_r, q2_s, q2_r))
    next(sum_1)
    next(sum_2)
    output = output_sum()
    io.arrive(mixed_ref, map_ref, gain_ref)
    proj_loads[0].wait()
    gain = gain_ref[...]
    gain_total = jnp.zeros_like(gain)
    load.wait()
    io.fetch(ffn_part_ref, kept_ref, totals_ref, normed_split_ref, normed_sib_ref, middle_ref)
    proj_loads[1].start()
    io.fetch(state_ref, q_ref, k_ref, v_ref, inv_ref, taps_ref)
    for h in range(heads):
        columns = slice(h * DV, (h + 1) * DV)
        grad = mm(branch_ref[...], out_weight[:, columns])
        mixer_out = mixed_ref[h]
        z = proj_ref[HALO:, gate_columns(heads, h)]
        scale = lax.rsqrt(jnp.mean(mixer_out * mixer_out, axis=-1, keepdims=True) + 1e-05)
        normal = mixer_out * scale
        s = jax.nn.sigmoid(z)
        silu = z * s
        gain_total = gain_total + jnp.sum(grad * normal * silu, axis=0, keepdims=True)
        gate_ref[:, columns] = (grad * normal * gain * s * (1.0 + z * (1.0 - s))).astype(BF16)
        u = grad * gain * silu
        grad_outs[h] = scale * u - normal * (scale * jnp.mean(u * normal, axis=-1, keepdims=True))
        carried = mtm(map_ref[h], grad_outs[h], FINE).astype(BF16)
        for half in range(HALVES):
            pack[HALVES * h + half] = carried[:, half * DK : (half + 1) * DK]
    gain_out_ref[...] = gain_total
    io.leave(gain_out_ref, gate_ref)
    io.arrive(kept_ref, totals_ref, q_ref, k_ref, v_ref, inv_ref, state_ref)
    io.arrive(normed_split_ref, normed_sib_ref, taps_ref)
    proj_loads[1].wait()
    copies = [send(pack.at[near[d]], near_in.at[member], near_s, near_r, d, near_ids[d]) for d in range(1, members)]
    io.arrive(ffn_part_ref, middle_ref)
    next(output)
    gate_aside = send(gate_ref, gate_sib, core_s, core_r, 2, sibling)
    near_in[member] = pack[member]
    for copy in first_aside:
        copy.wait()
    weight_blocks(branch_split, branch_sib, gated_ref, gated_sib, pl.ds(0, part_o.shape[2]), part_o, slab, False)
    sum_o = sum_both(ring_x, ring_z, part_o, mid_o, first_out_ref, land_o, land_o2, (o1_s, o1_r, o2_s, o2_r))
    next(sum_o)
    unit = (iota((DK, DK), 0) == iota((DK, DK), 1)).astype(F32)
    passed, leading, ahead = unit, unit, []
    for j in range(members):
        turned[j] = kept_ref[j].astype(F32).T.astype(BF16)
    for j in range(members):
        ahead.append(leading)
        leading = mm(leading, turned[j].astype(F32), FINE)
        back = members - 1 - j
        before[back] = passed
        passed = twice(turned[back], passed)
    next(sum_1)
    next(sum_2)
    for copy in copies:
        copy.wait()
    total = near_in[0].astype(F32)
    for j in range(1, members):
        total = total + mm(ahead[j], near_in[j].astype(F32), FINE)
    far_out[...] = total.astype(BF16)
    copies = [send(far_out, far_in.at[group], far_s, far_r, d, far_ids[d]) for d in range(1, groups)]
    far_in[group] = far_out[...]

    rows, columns = triangles(size)
    strict = columns < rows
    rates = proj_ref[HALO:, heads * CONV : heads * CONV + LANES]
    gate_values = gates(rates, log_ref, bias_ref, heads)

    def without_leaving(h):
        kf = k_ref[h].astype(F32)
        beta, gamma, gamma_row = of_head(gate_values, h, heads)
        spread = decays_of(gamma, gamma_row)
        spreads[h] = spread
        residual = v_ref[h].astype(F32) - jnp.exp(gamma) * mm(kf, whole_state(state_ref, h))
        residuals[h] = residual
        written = mm(inv_ref[h], beta * residual, FINE)
        writtens[h] = written
        grad_scores_all[h] = mmt(grad_outs[h], written)
        partial[h] = mtm(spread * mmt(q_ref[h], k_ref[h]), grad_outs[h])

    total = jnp.zeros((DK, DK), F32)
    for j in reversed(range(members)):
        after[j] = total
        total = twice(turned[j], total) + near_in[j].astype(F32)
    without_leaving(0)
    gate_aside.wait()
    weight_blocks(normed_split_ref, normed_sib_ref, gate_ref, gate_sib, pl.ds(0, part_g.shape[2]), part_g, slab, True)
    sum_g = sum_both(ring_z, ring_x, part_g, mid_g, first_gate_ref, land_g, land_g2, (g1_s, g1_r, g2_s, g2_r))
    next(sum_g)
    next(sum_1)
    next(sum_2)
    turned_totals = [totals_ref[j].astype(F32).T.astype(BF16) for j in range(groups)]
    for copy in copies:
        copy.wait()
    state = jnp.zeros((DK, DK), F32)
    for j in reversed(range(groups)):
        fresh = twice(turned_totals[j], state) + far_in[j].astype(F32)
        state = jnp.where(j > group, fresh, state)
    for j in range(members):
        back_out[j] = (mm(before[j], state, FINE) + after[j]).astype(BF16)
    copies = [send(back_out.at[near[d]], back_in.at[member], back_s, back_r, d, near_ids[d]) for d in range(1, members)]
    back_in[member] = back_out[member]
    next(output)
    without_leaving(1)
    next(sum_o)
    without_leaving(2)
    next(output)
    without_leaving(3)
    next(sum_1)
    next(sum_2)
    for copy in copies:
        copy.wait()

    lanes = iota((size, LANES), 1)
    grad_gammas = jnp.zeros((size, LANES), F32)
    grad_betas = jnp.zeros((size, LANES), F32)
    column_sums = []
    body = size - HALO
    copies = []
    beside = {0: [sum_g, sum_1, sum_2], 1: [sum_o, output], 2: [sum_g, sum_o], 3: [sum_g]}
    for h in range(heads):
        queries, keys = q_ref[h], k_ref[h]
        qf, kf = queries.astype(F32), keys.astype(F32)
        beta, gamma, _ = of_head(gate_values, h, heads)
        spread, residual, written, grad_scores = spreads[h], residuals[h], writtens[h], grad_scores_all[h]
        growth = jnp.exp(gamma)
        final = gamma[size - 1 : size]
        fade = jnp.exp(final - gamma)
        state, leaving = whole_state(state_ref, h), whole_state(back_in, h)
        inv, grad = inv_ref[h], grad_outs[h]
        products = mmt(keys, keys)
        scores = spread * mmt(queries, keys)
        lower = jnp.where(strict, beta * spread * products, 0.0)
        faded = fade * kf
        grad_written = partial[h] + mm(faded, leaving)
        grad_targets = mtm(inv, grad_written, FINE)
        grad_lower = jnp.where(strict, -mmt(grad_targets, written), 0.0)
        grad_values = beta * grad_targets
        grad_beta = jnp.sum(grad_targets * residual, axis=-1, keepdims=True)
        grad_beta = grad_beta + jnp.sum(grad_lower * spread * products, axis=-1, keepdims=True)
        q_first = growth * mmt(grad, state)
        k_first = -growth * mmt(grad_values, state)
        spread_scores = spread * grad_scores
        spread_lower = grad_lower * beta * spread
        grad_faded = mmt(written, leaving)
        grad_queries = q_first + mm(spread_scores, kf)
        grad_keys = (
            k_first
            + mtm(spread_scores, qf)
            + mm(spread_lower, kf)
            + mtm(spread_lower, kf)
            + fade * grad_faded
        )
        energy = grad_scores * scores + grad_lower * lower
        fading = jnp.sum(grad_faded * faded, axis=-1, keepdims=True)
        grad_gamma = jnp.sum(qf * q_first + kf * k_first, axis=-1, keepdims=True) - fading
        grad_gamma = grad_gamma + jnp.sum(energy, axis=-1, keepdims=True)
        at_end = jnp.sum(fading, axis=0, keepdims=True) + jnp.exp(final) * jnp.sum(
            jnp.sum(state * leaving, axis=1, keepdims=True), axis=0, keepdims=True
        )
        grad_gamma = grad_gamma + jnp.where(iota((size, 1), 0) == size - 1, at_end, 0.0)
        column_sums.append(jnp.sum(energy, axis=0, keepdims=True))
        grad_gammas = grad_gammas + jnp.where(lanes == h, grad_gamma, 0.0)
        grad_betas = grad_betas + jnp.where(lanes == heads + h, grad_beta, 0.0)

        projected = proj_ref[:, h * CONV : (h + 1) * CONV]
        taps = taps_ref[:, h]
        extended, mixed, gate, (q_raw, q_scale), (k_raw, k_scale), *_ = mixer_inputs(projected, taps)
        grad_active = jnp.concatenate(
            [
                norm_back(grad_queries * DK ** (-0.5), q_raw, q_scale),
                norm_back(grad_keys, k_raw, k_scale),
                grad_values,
            ],
            axis=1,
        )
        grad_mixed = grad_active * gate * (1.0 + mixed * (1.0 - gate))
        padding = jnp.zeros((HALO, CONV), F32)
        full = jnp.concatenate([padding, grad_mixed, padding], axis=0)
        total = None
        for j in range(KW):
            shift = KW - 1 - j
            moved = full if shift == 0 else pltpu.roll(full, size + 2 * HALO - shift, 0)
            term = taps[j : j + 1] * moved[: size + HALO]
            total = term if total is None else total + term
            back = extended if shift == 0 else pltpu.roll(extended, shift, 0)
            taps_out_ref[j : j + 1, h * CONV : (h + 1) * CONV] = jnp.sum(
                grad_mixed * back[HALO:], axis=0, keepdims=True
            )
        halo_out[h] = total[:HALO]
        tails[h] = total[size:]
        out_ref[:, h * CONV : (h + 1) * CONV] = total[HALO:].astype(BF16)
        copies.append(send(halo_out.at[h], halo_in.at[h], halo_s, halo_r, h, previous))
        upper = (pl.ds(0, body), pl.ds(h * CONV, CONV))
        copies.append(send(out_ref.at[upper], sibling_ref.at[upper], body_s, body_r, h, sibling))
        for stage in beside[h]:
            next(stage, None)

    beta, decay, _, _, pre = gate_values
    sums_ref[...] = jnp.zeros_like(sums_ref)
    for h in range(heads):
        sums_ref[h : h + 1] = column_sums[h]
    wide = grad_gammas - sums_ref[...].T
    grad_decay = mm((columns >= rows).astype(F32), wide, EXACT)
    grad_pre = jnp.where(lanes < heads, -jnp.exp(lane_values(log_ref, heads)) * jax.nn.sigmoid(pre) * grad_decay, 0.0)
    out_ref[:, heads * CONV :] = (grad_pre + grad_betas * beta * (1.0 - beta)).astype(BF16)
    scales_out_ref[...] = jnp.zeros_like(scales_out_ref)
    scales_out_ref[0:1] = jnp.sum(grad_decay * decay, axis=0, keepdims=True)
    scales_out_ref[1:2] = jnp.sum(grad_pre, axis=0, keepdims=True)
    side = (pl.ds(0, size), pl.ds(heads * CONV, LANES))
    last = [send(out_ref.at[side], sibling_ref.at[side], rate_s, rate_r, 0, sibling)]
    for copy in copies:
        copy.wait()
    for h in range(heads):
        arrived = jnp.where(seq < peers - 1, halo_in[h], 0.0)
        fixed = tails[h] + arrived
        out_ref[body:, h * CONV : (h + 1) * CONV] = fixed.astype(BF16)
        lower = (pl.ds(body, HALO), pl.ds(h * CONV, CONV))
        last.append(send(out_ref.at[lower], sibling_ref.at[lower], tail_s, tail_r, h, sibling))
    for copy in last:
        copy.wait()
    io.leave(out_ref, sibling_ref, taps_out_ref, scales_out_ref)
    finish(output, sum_o, sum_g)


def chunks_of(units):
    return [(at, min(2 * LANES, units - at)) for at in range(0, units, 2 * LANES)]


def ffn_kernel(
    slab, io, second_ref, cotangent_ref, middle_ref, gain_ref, weights_ref,
    branch_ref, grad_ref, grad_gain_ref, ffn_ref, piece_1_ref, piece_2_ref, down_a_ref, down_b_ref, up_a_ref, up_b_ref,
    weights, down, to_gate, to_up, hidden, grad_hidden, second_split, cotangent_split, second_sib, cotangent_sib, hidden_sib, grad_sib,
    part, landing, piece_1, piece_2, part_a, part_b, land_a, land_b, mid_a, mid_b, land_a2, land_b2,
    part_1, part_2, land_1, land_2, mid_1, mid_2, land_12, land_22,
    load_s, down_s, store_s, half_s, half_r, hid_s, hid_r, gra_s, gra_r, red_s, red_r, gat_s, gat_r,
    a1_s, a1_r, b1_s, b1_r, a2_s, a2_r, b2_s, b2_r, p1_s, p1_r, q1_s, q1_r, p2_s, p2_r, q2_s, q2_r,
):
    seq, head = lax.axis_index("seq"), lax.axis_index("head")
    ring_x, ring_y, ring_z = ring_ids("x"), ring_ids("y"), ring_ids("z")
    sibling = (seq + 1 - 2 * (seq % 2), head)
    all_here = say_here(ring_x[4:] + ring_y[4:] + ring_z[4:] + (sibling,))
    count, width = second_ref.shape
    units = hidden.shape[1]
    chunks = chunks_of(units)
    ahead = 2

    def load(i):
        at, length = chunks[i % len(chunks)]
        if i < len(chunks):
            both = pl.ds(2 * at, 2 * length)
            return pltpu.make_async_copy(weights_ref.at[:, both], weights.at[:, both], load_s.at[i])
        from_at, here = pl.ds(2 * units + at, length), pl.ds(at, length)
        return pltpu.make_async_copy(weights_ref.at[:, from_at], down.at[:, here], down_s.at[i - len(chunks)])

    loads = [load(i) for i in range(2 * len(chunks))]
    for copy in loads[:ahead]:
        copy.start()
    io.arrive(second_ref, cotangent_ref)
    second_split[...] = split_by_core(second_ref[...].astype(F32), slab).astype(BF16)
    cotangent_split[...] = split_by_core(cotangent_ref[...].astype(F32), slab).astype(BF16)
    all_here()
    aside = [
        send(other_half(second_split), second_sib, half_s, half_r, 0, sibling),
        send(other_half(cotangent_split), cotangent_sib, half_s, half_r, 1, sibling),
    ]
    step = 512

    def next_load(i):
        if i + ahead < len(loads):
            loads[i + ahead].start()
        loads[i].wait()

    for i, (at, length) in enumerate(chunks):
        next_load(i)
        z = mm(second_ref[...], weights[:, pl.ds(2 * at, length)])
        u = mm(second_ref[...], weights[:, pl.ds(2 * at + length, length)])
        s = jax.nn.sigmoid(z)
        silu = z * s
        here = pl.ds(at, length)
        hidden[:, here] = (silu * u).astype(BF16)
        to_gate[:, here] = u * s * (1.0 + z * (1.0 - s))
        to_up[:, here] = silu
        aside.append(send(hidden.at[:, here], hidden_sib.at[:, here], hid_s, hid_r, i, sibling))
    late = []
    for i, (at, length) in enumerate(chunks):
        next_load(len(chunks) + i)
        here, both = pl.ds(at, length), pl.ds(2 * at, 2 * length)
        g = mm(cotangent_ref[...], down[:, here])
        grad_hidden[:, pl.ds(2 * at, length)] = (g * to_gate[:, here]).astype(BF16)
        grad_hidden[:, pl.ds(2 * at + length, length)] = (g * to_up[:, here]).astype(BF16)
        late.append(send(grad_hidden.at[:, both], grad_sib.at[:, both], gra_s, gra_r, i, sibling))
        if i == 0:
            for copy in aside:
                copy.wait()
            wide_a, wide_b = part_a.shape[2], part_b.shape[2]
            weight_blocks(cotangent_split, cotangent_sib, hidden, hidden_sib, pl.ds(0, wide_a), part_a, slab, False)
            sum_a = sum_both(ring_x, ring_z, part_a, mid_a, down_a_ref, land_a, land_a2, (a1_s, a1_r, a2_s, a2_r))
            next(sum_a)
            weight_blocks(cotangent_split, cotangent_sib, hidden, hidden_sib, pl.ds(wide_a, wide_b), part_b, slab, True)
            sum_b = sum_both(ring_z, ring_x, part_b, mid_b, down_b_ref, land_b, land_b2, (b1_s, b1_r, b2_s, b2_r))
            next(sum_b)
    reduces = []
    for k, columns in enumerate(column_halves(width)):

        @pl.loop(2 * k, 2 * k + 2)
        def _(n):
            rows = pl.ds(pl.multiple_of(n * step, step), step)
            product = mmt(grad_hidden[...], weights[rows])
            for p in range(part.shape[0]):
                m = part.shape[1]
                part[p, :, rows] = product[p * m : (p + 1) * m].astype(BF16)

        blocks, result = part.at[:, :, columns], grad_ref.at[:, columns]
        reduces.append(ring_reduce(ring_y, blocks, result, landing.at[k], red_s.at[k], red_r.at[k]))
        next(reduces[k])
    for copy in late:
        copy.wait()
    next(sum_a)
    next(sum_b)
    sent, wide_1, wide_2 = piece_1.shape[2] + piece_2.shape[2], part_1.shape[2], part_2.shape[2]
    weight_blocks(second_split, second_sib, grad_hidden, grad_sib, pl.ds(sent, wide_1), part_1, slab, False)
    sum_1 = sum_both(ring_x, ring_z, part_1, mid_1, up_a_ref, land_1, land_12, (p1_s, p1_r, q1_s, q1_r))
    next(sum_1)
    weight_blocks(second_split, second_sib, grad_hidden, grad_sib, pl.ds(sent + wide_1, wide_2), part_2, slab, True)
    sum_2 = sum_both(ring_z, ring_x, part_2, mid_2, up_b_ref, land_2, land_22, (p2_s, p2_r, q2_s, q2_r))
    next(sum_2)
    for reduce in reduces:
        next(reduce)

    @pl.loop(0, width // step)
    def _(n):
        rows = pl.ds(pl.multiple_of(n * step, step), step)
        product = mmt(hidden[...], down[rows])
        for p in range(ffn_ref.shape[0]):
            m = ffn_ref.shape[1]
            ffn_ref[p, :, rows] = product[p * m : (p + 1) * m].astype(BF16)

    io.leave(ffn_ref)
    next(sum_a)
    next(sum_b)
    io.arrive(middle_ref, gain_ref)
    finish(*reduces)
    back, grad_gain = rms_back(grad_ref[...], middle_ref[...], gain_ref[...])
    grad = cotangent_ref[pl.ds(pl.multiple_of(ring_y[0] * slab, slab), slab)].astype(F32) + back
    branch_ref[ring_y[0]] = grad.astype(BF16)
    gather = ring_gather(ring_y, branch_ref, gat_s, gat_r)
    next(gather)
    grad_ref[...] = grad
    grad_gain_ref[...] = grad_gain
    io.leave(grad_ref, grad_gain_ref)
    stores, at = [], 0
    for k, (piece, piece_ref) in enumerate(((piece_1, piece_1_ref), (piece_2, piece_2_ref))):
        columns = pl.ds(at, piece.shape[2])
        weight_blocks(second_split, second_sib, grad_hidden, grad_sib, columns, piece, slab, k == 1)
        stores.append(pltpu.make_async_copy(piece, piece_ref, store_s.at[k]))
        stores[k].start()
        at += piece.shape[2]
    next(sum_1)
    next(sum_2)
    next(sum_a)
    next(sum_b)
    next(gather)
    next(sum_1)
    next(sum_2)
    finish(sum_a, sum_b)
    finish(gather)
    io.leave(branch_ref)
    finish(sum_1, sum_2)
    for store in stores:
        store.wait()


def small_sum(value, mask, outgoing, incoming, sends, receives, result):
    seq, head = lax.axis_index("seq"), lax.axis_index("head")
    x, z, core = seq // 8, (seq // 2) % 4, seq % 2
    stages = [
        ([(seq, lax.rem(head + d, 4)) for d in (1, 2, 3)], mask),
        ([(lax.rem(x + d, 4) * 8 + seq % 8, head) for d in (1, 2, 3)], None),
        ([(x * 8 + lax.rem(z + d, 4) * 2 + core, head) for d in (1, 2, 3)], None),
        ([(seq + 1 - 2 * core, head)], None),
    ]
    slot = 0
    for stage, (peers, only) in enumerate(stages):
        outgoing[stage] = value
        copies = []
        for peer in peers:
            copies.append((slot, send(outgoing.at[stage], incoming.at[slot], sends, receives, slot, peer)))
            slot += 1
        yield
        for at, copy in copies:
            copy.wait()
            value = value + (incoming[at] if only is None else jnp.where(only, incoming[at], 0.0))
    result[...] = value


def last_kernel(
    slab, io, gate_ref, tokens_ref, middle_grad_ref, gain_ref, ffn_gain_ref, out_gain_ref, scales_ref, taps_ref,
    split_ref, split_sib_ref, proj_ref, proj_sib_ref, weights_ref,
    low_ref, small_out_ref, late_out_ref, first_a_ref, first_b_ref,
    weights, small_ref, late_ref, part_n, land_n, sum_n, swap_out, swap_in, late_out, late_in, part_a, part_b, land_a, land_b, mid_a, mid_b, land_a2, land_b2,
    load_s, rn_s, rn_r, gn_s, gn_r, sw_s, sw_r, la_s, la_r, a1_s, a1_r, b1_s, b1_r, a2_s, a2_r, b2_s, b2_r,
):
    seq, head = lax.axis_index("seq"), lax.axis_index("head")
    ring_x, ring_y, ring_z = ring_ids("x"), ring_ids("y"), ring_ids("z")
    sibling = (seq + 1 - 2 * (seq % 2), head)
    across = (
        (lax.rem(seq + 16, 32), head),
        (seq, lax.rem(head + 2, 4)),
        ((seq // 8) * 8 + lax.rem((seq // 2) % 4 + 2, 4) * 2 + seq % 2, head),
    )
    all_here = say_here(ring_x[4:] + ring_y[4:] + ring_z[4:] + across + (sibling,))
    width, wide = weights.shape
    step = 512

    def load(k):
        rows = pl.ds(pl.multiple_of(k * step, step), step)
        return pltpu.make_async_copy(weights_ref.at[rows, pl.ds(0, wide)], weights.at[rows], load_s.at[k])

    io.arrive(ffn_gain_ref, out_gain_ref, scales_ref, taps_ref)
    small_ref[...] = jnp.zeros_like(small_ref)
    small_ref[1:2] = ffn_gain_ref[...]
    small_ref[2:3, :DV] = out_gain_ref[...]
    small_ref[2:3, DV : DV + LANES] = scales_ref[0:1]
    small_ref[2:3, DV + LANES : DV + 2 * LANES] = scales_ref[1:2]
    small_ref[3 : 3 + KW] = taps_ref[...]
    me = ring_y[0]
    wide_a, wide_b = part_a.shape[2], part_b.shape[2]
    narrow = proj_ref.shape[1]
    io.arrive(split_ref, split_sib_ref, proj_ref, proj_sib_ref)
    io.fetch(gate_ref, gain_ref, tokens_ref, middle_grad_ref)
    for k in range(width // step):
        load(k).start()
    weight_blocks(split_ref, split_sib_ref, proj_ref, proj_sib_ref, pl.ds(0, wide_a), part_a, slab, False)
    all_here()
    sum_a = sum_both(ring_x, ring_z, part_a, mid_a, first_a_ref, land_a, land_a2, (a1_s, a1_r, a2_s, a2_r))
    next(sum_a)
    weight_blocks(split_ref, split_sib_ref, proj_ref, proj_sib_ref, pl.ds(wide_a, wide_b), part_b, slab, True)
    sum_b = sum_both(ring_z, ring_x, part_b, mid_b, first_b_ref, land_b, land_b2, (b1_s, b1_r, b2_s, b2_r))
    next(sum_b)
    rows8, lanes = iota(small_ref.shape, 0), iota(small_ref.shape, 1)
    shared = (rows8 < 2) | ((rows8 == 2) & (lanes < DV))
    small = small_sum(small_ref[...], shared, swap_out, swap_in, sw_s, sw_r, small_out_ref)
    next(small)
    io.arrive(gate_ref, tokens_ref, middle_grad_ref, gain_ref)
    reduces = []
    for k, columns in enumerate(column_halves(width)):

        @pl.loop(2 * k, 2 * k + 2)
        def _(n):
            load(n).wait()
            rows = pl.ds(pl.multiple_of(n * step, step), step)
            product = mmt(proj_ref[...], weights[rows, :narrow]) + mmt(gate_ref[...], weights[rows, narrow:])
            for p in range(part_n.shape[0]):
                m = part_n.shape[1]
                part_n[p, :, rows] = product[p * m : (p + 1) * m].astype(BF16)

        blocks, result = part_n.at[:, :, columns], sum_n.at[:, columns]
        reduces.append(ring_reduce(ring_y, blocks, result, land_n.at[k], rn_s.at[k], rn_r.at[k]))
        next(reduces[k])
    next(small)
    for reduce in reduces:
        next(reduce)
    next(sum_a)
    next(sum_b)
    next(small)
    finish(*reduces)
    back, grad_gain = rms_back(sum_n[...], tokens_ref[me].astype(F32), gain_ref[...])
    low_ref[me] = (middle_grad_ref[...] + back).astype(BF16)
    gather_n = ring_gather(ring_y, low_ref, gn_s, gn_r)
    next(gather_n)
    wide_late = late_ref.shape[1]
    for r in range(late_ref.shape[0]):
        late_ref[r : r + 1] = grad_gain[:, r * wide_late : (r + 1) * wide_late]
    late = small_sum(late_ref[...], None, late_out, late_in, la_s, la_r, late_out_ref)
    next(late)
    next(small)
    next(sum_a)
    next(sum_b)
    next(late)
    next(gather_n)
    next(late)
    next(sum_a)
    next(sum_b)
    next(late)
    finish(late, small, gather_n, sum_a, sum_b)


def finish_kernel(
    heads, io, first_a_ref, first_b_ref, first_out_ref, first_gate_ref, up_1_ref, up_2_ref, up_3_ref, up_4_ref, down_a_ref, down_b_ref, low_ref, small_ref, late_ref, output_in_ref,
    in_ref, rate_ref, out_ref, gate_up_ref, down_ref, tokens_ref, taps_ref, mixer_gain_ref, ffn_gain_ref, out_gain_ref,
    log_out_ref, bias_out_ref, output_ref,
):
    io.arrive(low_ref)
    tokens_ref[...] = low_ref[...].astype(F32)
    io.leave(tokens_ref)
    io.arrive(up_1_ref, up_2_ref, up_3_ref, up_4_ref)
    up_in = jnp.concatenate([up_1_ref[...], up_2_ref[...], up_3_ref[...], up_4_ref[...]], axis=1)
    for at, length in chunks_of(down_ref.shape[1]):
        for g in range(2):
            gate_up_ref[:, g, at : at + length] = up_in[:, 2 * at + g * length : 2 * at + (g + 1) * length]
    io.leave(gate_up_ref)
    io.arrive(first_a_ref, first_b_ref, first_gate_ref, first_out_ref, small_ref, late_ref, down_a_ref, down_b_ref)
    both = jnp.concatenate([first_a_ref[...], first_b_ref[...]], axis=1)
    for h in range(heads):
        in_ref[:, h, :CONV] = both[:, h * CONV : (h + 1) * CONV]
        in_ref[:, h, CONV:] = first_gate_ref[:, h * DV : (h + 1) * DV]
        out_ref[:, h] = first_out_ref[:, h * DV : (h + 1) * DV]
        taps_ref[:, h] = small_ref[3 : 3 + KW, h * CONV : (h + 1) * CONV]
    io.leave(in_ref, out_ref)
    rates = heads * CONV
    turned = both[:, rates : rates + LANES].T
    for g in range(2):
        rate_ref[g] = turned[g * heads : (g + 1) * heads]
    io.arrive(output_in_ref)
    output_ref[...] = output_in_ref[...]
    io.leave(output_ref)
    log_out_ref[...] = small_ref[2, DV : DV + heads]
    bias_out_ref[...] = small_ref[2, DV + LANES : DV + LANES + heads]
    down_ref[:, : down_a_ref.shape[1]] = down_a_ref[...]
    down_ref[:, down_a_ref.shape[1] :] = down_b_ref[...]
    for r in range(late_ref.shape[0]):
        mixer_gain_ref[pl.ds(r * late_ref.shape[1], late_ref.shape[1])] = late_ref[r]
    ffn_gain_ref[...] = small_ref[1]
    out_gain_ref[...] = small_ref[2, :DV]


def gather_rings(slab_ref, full_ref, core_s, core_r, ring_s, ring_r, done):
    seq, head = lax.axis_index("seq"), lax.axis_index("head")
    core = seq % 2
    sibling = (seq + 1 - 2 * core, head)
    ring_x, ring_z = ring_ids("x"), ring_ids("z")
    x, z = ring_x[0], ring_z[0]
    rows, wide = slab_ref.shape
    cut = -(-wide // (2 * LANES)) * LANES
    counts = {"core": 0, "ring": 0}

    def slot(kind):
        counts[kind] += 1
        return counts[kind] - 1

    def across(source, target):
        return send(source, target, core_s, core_r, slot("core"), sibling)

    own_across = across(slab_ref, full_ref.at[x, z, core])
    half = rows // 2
    upper, lower, everything = pl.ds(0, half), pl.ds(half, half), pl.ds(0, rows)

    def round_ring(ring, at, source, arrived, ended):
        me, right, left, opposite, right_id, left_id = ring

        def go(place, part, peer):
            origin = source(part) if place is me else at(place, part)
            return send(origin, at(place, part), ring_s, ring_r, slot("ring"), peer)

        upper_right = go(me, upper, right_id)
        lower_left = go(me, lower, left_id)
        lower_right = go(me, lower, right_id)
        upper_left = go(me, upper, left_id)
        yield
        upper_right.wait()
        far_right = go(left, upper, right_id)
        lower_left.wait()
        far_left = go(right, lower, left_id)
        yield
        lower_right.wait()
        arrived(left)
        upper_left.wait()
        arrived(right)
        yield
        far_right.wait()
        far_left.wait()
        arrived(opposite)
        ended()

    active = []
    for ring_1, ring_2, columns, x_first in (
        (ring_x, ring_z, pl.ds(0, cut), True),
        (ring_z, ring_x, pl.ds(cut, wide - cut), False),
    ):
        def place_of(first, second, part, columns=columns, x_first=x_first):
            where = (first, second) if x_first else (second, first)
            return full_ref.at[where[0], where[1], core, part, columns]

        def start_second(first, copies, source=None, ring_2=ring_2, place_of=place_of, x_first=x_first, columns=columns):
            def at(place, part):
                return place_of(first, place, part)

            def arrived(place):
                copies.append(across(at(place, everything), at(place, everything)))

            def ended():
                done(x_first, first, columns, copies)

            ring = round_ring(ring_2, at, source or (lambda part: at(ring_2[0], part)), arrived, ended)
            next(ring)
            active.append(ring)

        def at_first(place, part, ring_2=ring_2, place_of=place_of):
            return place_of(place, ring_2[0], part)

        def arrived_first(place, at_first=at_first, start_second=start_second):
            start_second(place, [across(at_first(place, everything), at_first(place, everything))])

        def mine(part, columns=columns):
            return slab_ref.at[part, columns]

        ring = round_ring(ring_1, at_first, mine, arrived_first, lambda: None)
        next(ring)
        active.append(ring)
        start_second(ring_1[0], [own_across] if x_first else [], mine)
    while active:
        yield
        ended = []
        for stage in list(active):
            if next(stage, active) is active:
                ended.append(stage)
        active[:] = [stage for stage in active if stage not in ended]


def project_kernel(
    heads, io, in_ref, rate_ref, out_weight_ref, gate_up_ref, down_ref, tokens_ref, gain_ref,
    full_ref, projected_ref, split_ref, split_sib_ref, out_slab_ref, rest_ref,
    proj_ref, slab_ref, turned, weights, normed, halo_in, own_s, store_s, proj_s, halo_s, halo_r, half_s, half_r, core_s, core_r, ring_s, ring_r,
):
    seq, head = lax.axis_index("seq"), lax.axis_index("head")
    peers = lax.axis_size("seq")
    core = seq % 2
    sibling = (seq + 1 - 2 * core, head)
    before, after = (lax.rem(seq + peers - 1, peers), head), (lax.rem(seq + 1, peers), head)
    ring_x, ring_z = ring_ids("x"), ring_ids("z")
    rows, wide = slab_ref.shape
    count, width = tokens_ref.shape
    all_here = say_here(ring_x[4:] + ring_z[4:] + (sibling, before, after))
    io.arrive(in_ref, rate_ref)
    gate_at = heads * CONV + LANES
    mixer = in_ref[...].astype(F32)
    rates = rate_ref[...].astype(F32)
    turned[...] = jnp.zeros_like(turned)
    for g in range(2):
        turned[g * heads : (g + 1) * heads] = rates[g]
    slab_ref[:, heads * CONV : gate_at] = turned[...].T.astype(BF16)
    for h in range(heads):
        slab_ref[:, h * CONV : (h + 1) * CONV] = mixer[:, h, :CONV].astype(BF16)
        slab_ref[:, gate_at + h * DV : gate_at + (h + 1) * DV] = mixer[:, h, CONV:].astype(BF16)
    own = pltpu.make_async_copy(slab_ref, weights.at[ring_x[0], ring_z[0], core], own_s)
    own.start()
    all_here()
    ready = []
    gather = gather_rings(slab_ref, weights, core_s, core_r, ring_s, ring_r, lambda *group: ready.append(group))
    next(gather)
    io.arrive(tokens_ref, gain_ref)
    halo = send(tokens_ref.at[pl.ds(count - HALO, HALO)], halo_in, halo_s, halo_r, 0, after)

    def norm(values):
        return values * rms_scale(values) * gain_ref[...]

    fresh = norm(tokens_ref[...].astype(F32))
    normed[HALO:] = fresh.astype(BF16)
    split_ref[...] = split_by_core(normed[HALO:].astype(F32), rows).astype(BF16)
    half = send(other_half(split_ref), split_sib_ref, half_s, half_r, 0, sibling)
    io.leave(split_ref)
    io.arrive(out_weight_ref, gate_up_ref, down_ref)
    out_weight = out_weight_ref[...].astype(F32)
    for h in range(heads):
        out_slab_ref[:, h * DV : (h + 1) * DV] = out_weight[:, h].astype(BF16)
    gate_up = gate_up_ref[...].astype(F32)
    for at, length in chunks_of(down_ref.shape[1]):
        here = slice(at, at + length)
        for g in range(2):
            rest_ref[:, 2 * at + g * length : 2 * at + (g + 1) * length] = gate_up[:, g, here].astype(BF16)
    rest_ref[:, 2 * down_ref.shape[1] :] = down_ref[...]
    io.leave(out_slab_ref, rest_ref)
    halo.wait()
    normed[:HALO] = jnp.where(seq > 0, norm(halo_in[...].astype(F32)), 0.0).astype(BF16)
    own.wait()
    half.wait()
    io.leave(split_sib_ref)
    final = []
    stores, uses = [], {True: 0, False: 0}
    slabs = 2 * rows
    chip_rows = 4 * slabs

    def use(group):
        x_first, place, columns, copies = group
        for copy in copies:
            copy.wait()
        if x_first:
            left = normed[:, pl.ds(pl.multiple_of(place * chip_rows, chip_rows), chip_rows)]
            source, target = weights.at[place], full_ref.at[place]
        else:
            left = jnp.concatenate(
                [
                    normed[:, pl.ds(pl.multiple_of(k * chip_rows + place * slabs, slabs), slabs)]
                    for k in range(width // chip_rows)
                ],
                axis=1,
            )
            source, target = weights.at[:, place], full_ref.at[:, place]
        region = (slice(None), slice(None), slice(None), columns)
        store = pltpu.make_async_copy(source.at[region], target.at[region], store_s.at[len(stores)])
        store.start()
        stores.append(store)
        at, end = columns.start, columns.start + columns.size
        first_use = uses[x_first] == 0
        uses[x_first] += 1
        while at < end:
            length = min(4 * LANES, end - at)
            here = pl.ds(at, length)
            right = source[:, :, :, here].reshape(chip_rows, length)
            product = mm(left, right)
            if first_use:
                proj_ref[:, here] = product
            else:
                proj_ref[:, here] += product
            at += length
        if uses[x_first] == 4:
            store = pltpu.make_async_copy(
                proj_ref.at[:, columns], projected_ref.at[:, columns], proj_s.at[0 if x_first else 1]
            )
            store.start()
            final.append(store)

    running = True
    while running or ready:
        if running:
            running = next(gather, gather) is not gather
        if ready:
            use(ready.pop(0))
    for store in stores + final:
        store.wait()


def forward_kernel(
    heads, slab, groups, io, proj_ref, taps_ref, log_ref, bias_ref, out_gain_ref, slab_ref, tokens_ref, ffn_gain_ref,
    q_ref, k_ref, v_ref, inv_ref, map_ref, mixed_ref, gated_ref, entering_ref, kept_ref, totals_ref,
    out_full_ref, second_ref, middle_ref,
    weights, out_local, pack, near_in, before, far_out, far_in, back_out, back_in, part, landing,
    own_s, store_s, core_s, core_r, ring_s, ring_r,
    near_s, near_r, far_s, far_r, back_s, back_r, red_s, red_r, gat_s, gat_r,
):
    size = proj_ref.shape[0] - HALO
    members = pack.shape[0]
    member, group, near, near_ids, far_ids = scan_places(members, groups)
    ring_y = ring_ids("y")
    all_here = say_here([*near_ids[1:], *far_ids[1:], *ring_y[4:]])
    io.arrive(slab_ref)
    own = pltpu.make_async_copy(
        slab_ref, weights.at[lax.axis_index("seq") // 8, (lax.axis_index("seq") // 2) % 4, lax.axis_index("seq") % 2], own_s
    )
    own.start()
    rows, columns = triangles(size)
    io.arrive(proj_ref, taps_ref)
    rates = proj_ref[HALO:, heads * CONV : heads * CONV + LANES]
    gate_values = gates(rates, log_ref, bias_ref, heads)
    arrived = []
    gather = gather_rings(slab_ref, weights, core_s, core_r, ring_s, ring_r, lambda *group: arrived.extend(group[3]))
    lower, kept = [], []
    for h in range(heads):
        projected = proj_ref[:, h * CONV : (h + 1) * CONV]
        taps = taps_ref[:, h]
        *_, queries, keys, values = mixer_inputs(projected, taps)
        q_ref[h], k_ref[h], v_ref[h] = queries, keys, values
        beta, gamma, gamma_row = of_head(gate_values, h, heads)
        spread = decays_of(gamma, gamma_row)
        lower.append(jnp.where(columns < rows, beta * spread * mmt(keys, keys), 0.0))
        kept.append((queries, keys, values, beta, gamma, spread))
        if h == 0:
            all_here()
            next(gather)

    io.leave(q_ref, k_ref, v_ref)

    def between(width):
        if width in (32, 128):
            next(gather, None)

    inverses = inverse(lower, between)
    written = []
    for h in range(heads):
        queries, keys, values, beta, gamma, spread = kept[h]
        inv_ref[h] = inverses[h]
        growth = jnp.exp(gamma)
        targets = jnp.concatenate([growth * beta * keys.astype(F32), beta * values.astype(F32)], axis=1)
        written.append(mm(inverses[h], targets, FINE))
        final = gamma[size - 1 : size]
        faded = jnp.exp(final - gamma) * keys.astype(F32)
        summary = mtm(faded, written[h], FINE)
        unit = (iota((DK, DK), 0) == iota((DK, DK), 1)).astype(F32)
        passed = (jnp.exp(final) * unit - summary[:, :DK]).astype(BF16)
        for half in range(HALVES):
            pack[HALVES * h + half, :, :DK] = passed
            pack[HALVES * h + half, :, DK:] = summary[:, (half + 1) * DK : (half + 2) * DK].astype(BF16)
    io.leave(inv_ref)
    copies = [send(pack.at[near[d]], near_in.at[member], near_s, near_r, d, near_ids[d]) for d in range(1, members)]
    near_in[member] = pack[member]
    next(gather, None)
    for h in range(heads):
        queries, keys, values, beta, gamma, spread = kept[h]
        through = mm(spread * mmt(queries, keys), written[h])
        map_ref[h] = jnp.exp(gamma) * queries.astype(F32) - through[:, :DK]
        out_local[h] = through[:, DK:]
    io.leave(map_ref)
    for copy in copies:
        copy.wait()
    unit = (iota((DK, DK), 0) == iota((DK, DK), 1)).astype(F32)

    def after_this(later, earlier):
        moved = mm(later[:, :DK], earlier, FINE)
        return jnp.concatenate([moved[:, :DK], moved[:, DK:] + later[:, DK:]], axis=1)

    tree = [near_in[j].astype(F32) for j in range(members)]
    while len(tree) > 1:
        tree = [after_this(tree[k + 1], tree[k]) for k in range(0, len(tree), 2)]
    total = tree[0]
    far_out[...] = total.astype(BF16)
    copies = [send(far_out, far_in.at[group], far_s, far_r, d, far_ids[d]) for d in range(1, groups)]
    far_in[group] = far_out[...]
    next(gather, None)
    total = jnp.concatenate([unit, jnp.zeros((DK, DK), F32)], axis=1)
    for j in range(members):
        before[j] = total
        kept_ref[j] = near_in[j, :, :DK]
        moved = twice(near_in[j, :, :DK], total)
        total = jnp.concatenate([moved[:, :DK], moved[:, DK:] + near_in[j, :, DK:].astype(F32)], axis=1)
    for copy in copies:
        copy.wait()
    state = jnp.zeros((DK, DK), F32)
    for j in range(groups):
        totals_ref[j] = far_in[j, :, :DK]
        fresh = twice(far_in[j, :, :DK], state) + far_in[j, :, DK:].astype(F32)
        state = jnp.where(j < group, fresh, state)
    io.leave(kept_ref, totals_ref)
    for j in range(members):
        back_out[j] = (mm(before[j, :, :DK], state, FINE) + before[j, :, DK:]).astype(BF16)
    copies = [send(back_out.at[near[d]], back_in.at[member], back_s, back_r, d, near_ids[d]) for d in range(1, members)]
    back_in[member] = back_out[member]
    finish(gather)
    for copy in arrived:
        copy.wait()
    own.wait()
    store = pltpu.make_async_copy(weights, out_full_ref, store_s)
    store.start()
    for copy in copies:
        copy.wait()
    entering_ref[...] = back_in[...]
    io.leave(entering_ref)
    io.arrive(out_gain_ref)
    gain = out_gain_ref[...]
    for h in range(heads):
        mixer_out = out_local[h] + mm(map_ref[h], whole_state(back_in, h))
        mixed_ref[h] = mixer_out
        gate = proj_ref[HALO:, gate_columns(heads, h)]
        scale = lax.rsqrt(jnp.mean(mixer_out * mixer_out, axis=-1, keepdims=True) + 1e-05)
        gated = mixer_out * scale * gain * (gate * jax.nn.sigmoid(gate))
        gated_ref[:, h * DV : (h + 1) * DV] = gated.astype(BF16)
    io.leave(mixed_ref, gated_ref)
    chip_rows = 8 * slab
    halves = [(part.at[:, :, columns_], middle_ref.at[:, columns_]) for columns_ in column_halves(part.shape[2])]
    reduces = []
    for k, (blocks, result) in enumerate(halves):

        @pl.loop(2 * k, 2 * k + 2)
        def _(x):
            right = weights[x].reshape(chip_rows, heads * DV)
            product = mmt(gated_ref[...], right)
            at = pl.ds(pl.multiple_of(x * chip_rows, chip_rows), chip_rows)
            for p in range(part.shape[0]):
                n = part.shape[1]
                part[p, :, at] = product[p * n : (p + 1) * n].astype(BF16)

        reduces.append(ring_reduce(ring_y, blocks, result, landing.at[k], red_s.at[k], red_r.at[k]))
        next(reduces[k])
    me = ring_y[0]
    io.arrive(tokens_ref, ffn_gain_ref)
    finish(*reduces)
    middle = tokens_ref[me].astype(F32) + middle_ref[...]
    second_ref[me] = (middle * rms_scale(middle) * ffn_gain_ref[...]).astype(BF16)
    gather_y = ring_gather(ring_y, second_ref, gat_s, gat_r)
    next(gather_y)
    middle_ref[...] = middle
    io.leave(middle_ref)
    finish(gather_y)
    store.wait()


class Staging:
    def __init__(self):
        self.later, self.inputs, self.outputs, self.leaving = {}, {}, {}, []

    def fetch(self, *refs):
        for ref in refs:
            self.inputs[id(ref)] = self.later.pop(id(ref))
            self.inputs[id(ref)].start()

    def arrive(self, *refs):
        for ref in refs:
            self.inputs.pop(id(ref)).wait()

    def leave(self, *refs):
        for ref in refs:
            copy = self.outputs.pop(id(ref))
            copy.start()
            self.leaving.append(copy)

    def end(self):
        for copy in self.inputs.values():
            copy.wait()
        for copy in self.outputs.values():
            copy.start()
        for copy in [*self.leaving, *self.outputs.values()]:
            copy.wait()


def staged_call(kernel, in_specs, out_specs, out_shape, scratch_shapes, compiler_params, name, later=()):
    def is_staged(spec):
        return spec.memory_space == pltpu.VMEM

    anywhere = pl.BlockSpec(memory_space=pl.ANY)

    def run(*args):
        ins = [i for i, spec in enumerate(in_specs) if is_staged(spec)]
        outs = [i for i, spec in enumerate(out_specs) if is_staged(spec)]

        def body(*refs):
            refs = list(refs)
            results = len(args) + len(out_specs)
            staged = refs[results : results + len(ins) + len(outs)]
            in_s, out_s, *rest = refs[results + len(ins) + len(outs) :]
            io = Staging()
            for k, i in enumerate(ins):
                io.later[id(staged[k])] = pltpu.make_async_copy(refs[i], staged[k], in_s.at[k])
                refs[i] = staged[k]
                if i not in later:
                    io.fetch(staged[k])
            for k, i in enumerate(outs):
                at, held = len(args) + i, staged[len(ins) + k]
                io.outputs[id(held)] = pltpu.make_async_copy(held, refs[at], out_s.at[k])
                refs[at] = held
            kernel(io, *refs[:results], *rest)
            io.end()

        return pl.pallas_call(
            body,
            in_specs=[anywhere if is_staged(spec) else spec for spec in in_specs],
            out_specs=[anywhere if is_staged(spec) else spec for spec in out_specs],
            out_shape=out_shape,
            scratch_shapes=[
                *[pltpu.VMEM(args[i].shape, args[i].dtype) for i in ins],
                *[pltpu.VMEM(out_shape[i].shape, out_shape[i].dtype) for i in outs],
                pltpu.SemaphoreType.DMA((len(ins),)),
                pltpu.SemaphoreType.DMA((len(outs),)),
                *scratch_shapes,
            ],
            compiler_params=compiler_params,
            name=name,
        )(*args)

    return run


def pairs(*sizes):
    return [pltpu.SemaphoreType.DMA(size if isinstance(size, tuple) else (size,)) for size in sizes for _ in range(2)]


def per_device(
    tokens,
    mixer_gain,
    in_weight,
    rate_weight,
    conv_weight,
    decay_log,
    decay_bias,
    out_gain,
    out_weight,
    ffn_gain,
    gate_up_weight,
    down_weight,
    cotangent,
):
    count, width = tokens.shape
    heads = in_weight.shape[1]
    hidden_units = down_weight.shape[1]
    slab = in_weight.shape[0]
    projections = heads * PROJ + LANES
    units = heads * HALVES
    peers, sharers = lax.axis_size("seq"), lax.axis_size("head")
    groups = peers // units
    rows = count // sharers

    convolved_wide = heads * CONV + LANES
    out_wide = heads * DV
    anywhere = pl.BlockSpec(memory_space=pl.ANY)
    in_vmem = pl.BlockSpec(memory_space=pltpu.VMEM)

    def landing(*shape):
        return pltpu.VMEM((6, *shape), BF16)

    blocked = (sharers, rows, width)
    stacked = (4, 4, 2, slab)
    first_full, projected, normed_split, normed_sibling, out_slab, rest = staged_call(
        functools.partial(project_kernel, heads),
        in_specs=[in_vmem] * 7,
        out_specs=[anywhere] * 2 + [in_vmem] * 4,
        out_shape=[
            jax.ShapeDtypeStruct((*stacked, projections), BF16),
            jax.ShapeDtypeStruct((HALO + count, projections), F32),
            jax.ShapeDtypeStruct((count, width), BF16),
            jax.ShapeDtypeStruct((count, width // 2), BF16),
            jax.ShapeDtypeStruct((slab, out_wide), BF16),
            jax.ShapeDtypeStruct((slab, 3 * hidden_units), BF16),
        ],
        scratch_shapes=[
            pltpu.VMEM((HALO + count, projections), F32),
            pltpu.VMEM((slab, projections), BF16),
            pltpu.VMEM((LANES, slab), F32),
            pltpu.VMEM((*stacked, projections), BF16),
            pltpu.VMEM((HALO + count, width), BF16),
            pltpu.VMEM((HALO, width), BF16),
            pltpu.SemaphoreType.DMA,
            pltpu.SemaphoreType.DMA((8,)),
            pltpu.SemaphoreType.DMA((2,)),
            *pairs(1, 1, 31, 60),
        ],
        compiler_params=pltpu.CompilerParams(vmem_limit_bytes=VMEM_LIMIT, collective_id=7, has_side_effects=True),
        name="project",
    )(in_weight, jnp.transpose(rate_weight, (1, 2, 0)), out_weight, gate_up_weight, down_weight, tokens, mixer_gain.reshape(1, width))
    rest_full = lax.all_gather(rest, "seq", axis=0, tiled=True)
    first_full = first_full.reshape(width, projections)

    in_smem = pl.BlockSpec(memory_space=pltpu.SMEM)
    gain_row = out_gain.reshape(1, DV)
    block = (DK, DK)
    double = (DK, 2 * DK)
    (
        queries, keys, values, inv, out_map, mixer_out, gated, entering, kept, totals, out_full, second, middle,
    ) = staged_call(
        functools.partial(forward_kernel, heads, slab, groups),
        in_specs=[in_vmem] * 2 + [in_smem] * 2 + [in_vmem] * 4,
        out_specs=[in_vmem] * 10 + [anywhere] + [in_vmem] * 2,
        out_shape=[
            jax.ShapeDtypeStruct((heads, count, DK), BF16),
            jax.ShapeDtypeStruct((heads, count, DK), BF16),
            jax.ShapeDtypeStruct((heads, count, DV), BF16),
            jax.ShapeDtypeStruct((heads, count, count), F32),
            jax.ShapeDtypeStruct((heads, count, DK), F32),
            jax.ShapeDtypeStruct((heads, count, DV), F32),
            jax.ShapeDtypeStruct((count, out_wide), BF16),
            jax.ShapeDtypeStruct((units, *block), BF16),
            jax.ShapeDtypeStruct((units, *block), BF16),
            jax.ShapeDtypeStruct((groups, *block), BF16),
            jax.ShapeDtypeStruct((*stacked, out_wide), BF16),
            jax.ShapeDtypeStruct(blocked, BF16),
            jax.ShapeDtypeStruct((rows, width), F32),
        ],
        scratch_shapes=[
            pltpu.VMEM((*stacked, out_wide), BF16),
            pltpu.VMEM((heads, count, DV), F32),
            pltpu.VMEM((units, *double), BF16),
            pltpu.VMEM((units, *double), BF16),
            pltpu.VMEM((units, *double), F32),
            pltpu.VMEM(double, BF16),
            pltpu.VMEM((groups, *double), BF16),
            pltpu.VMEM((units, *block), BF16),
            pltpu.VMEM((units, *block), BF16),
            pltpu.VMEM(blocked, BF16),
            pltpu.VMEM((2, 6, rows // 2, width // 2), BF16),
            pltpu.SemaphoreType.DMA,
            pltpu.SemaphoreType.DMA,
            *pairs(31, 60, units, groups, units, (2, 6), 6),
        ],
        compiler_params=pltpu.CompilerParams(vmem_limit_bytes=VMEM_LIMIT, collective_id=1, has_side_effects=True),
        name="forward",
    )(
        projected,
        conv_weight,
        decay_log,
        decay_bias,
        gain_row,
        out_slab,
        tokens.reshape(blocked),
        ffn_gain.reshape(1, width),
    )
    out_full = out_full.reshape(width, out_wide)
    second = second.reshape(count, width)
    gate_wide = heads * DV
    many = 4 * slab

    def sums_scratch(wide_1, wide_2):
        return [
            pltpu.VMEM((4, many, wide_1), BF16),
            pltpu.VMEM((4, many, wide_2), BF16),
            landing(many // 2, wide_1),
            landing(many // 2, wide_2),
            pltpu.VMEM((many, wide_1), BF16),
            pltpu.VMEM((many, wide_2), BF16),
            landing(slab // 2, wide_1),
            landing(slab // 2, wide_2),
        ]

    down_a = -(-hidden_units // (2 * LANES)) * LANES
    down_b = hidden_units - down_a
    chunk_count = len(chunks_of(hidden_units))
    summed_here = 9 * LANES
    sent_wide = 2 * hidden_units - summed_here
    piece_a = -(-sent_wide // (2 * LANES)) * LANES
    piece_b = sent_wide - piece_a
    up_a = -(-summed_here // (2 * LANES)) * LANES
    up_b = summed_here - up_a
    grad_branch, grad_middle, grad_ffn_gain, ffn_part, piece_1, piece_2, grad_down_a, grad_down_b, *grad_up = staged_call(
        functools.partial(ffn_kernel, slab),
        in_specs=[in_vmem] * 4 + [anywhere],
        out_specs=[in_vmem] * 4 + [anywhere] * 2 + [in_vmem] * 4,
        out_shape=[
            jax.ShapeDtypeStruct(blocked, BF16),
            jax.ShapeDtypeStruct((rows, width), F32),
            jax.ShapeDtypeStruct((1, width), F32),
            jax.ShapeDtypeStruct(blocked, BF16),
            *[jax.ShapeDtypeStruct((4, many, wide), BF16) for wide in (piece_a, piece_b)],
            jax.ShapeDtypeStruct((slab, down_a), F32),
            jax.ShapeDtypeStruct((slab, down_b), F32),
            jax.ShapeDtypeStruct((slab, up_a), F32),
            jax.ShapeDtypeStruct((slab, up_b), F32),
        ],
        scratch_shapes=[
            pltpu.VMEM((width, 2 * hidden_units), BF16),
            pltpu.VMEM((width, hidden_units), BF16),
            pltpu.VMEM((count, hidden_units), F32),
            pltpu.VMEM((count, hidden_units), F32),
            pltpu.VMEM((count, hidden_units), BF16),
            pltpu.VMEM((count, 2 * hidden_units), BF16),
            pltpu.VMEM((count, width), BF16),
            pltpu.VMEM((count, width), BF16),
            pltpu.VMEM((count, width // 2), BF16),
            pltpu.VMEM((count, width // 2), BF16),
            pltpu.VMEM((count, hidden_units), BF16),
            pltpu.VMEM((count, 2 * hidden_units), BF16),
            pltpu.VMEM(blocked, BF16),
            pltpu.VMEM((2, 6, rows // 2, width // 2), BF16),
            *[pltpu.VMEM((4, many, wide), BF16) for wide in (piece_a, piece_b)],
            *sums_scratch(down_a, down_b),
            *sums_scratch(up_a, up_b),
            pltpu.SemaphoreType.DMA((chunk_count,)),
            pltpu.SemaphoreType.DMA((chunk_count,)),
            pltpu.SemaphoreType.DMA((2,)),
            *pairs(2, chunk_count, chunk_count, (2, 6), 6, 6, 6, 6, 6, 6, 6, 6, 6),
        ],
        compiler_params=pltpu.CompilerParams(vmem_limit_bytes=VMEM_LIMIT, collective_id=3, has_side_effects=True),
        name="ffn",
    )(second, cotangent, middle, ffn_gain.reshape(1, width), rest_full)
    grad_branch = grad_branch.reshape(count, width)
    (
        grad_projected, grad_sibling, grad_gate, grad_out_gain, grad_taps, grad_scales, first_out, first_gate, output, *grad_up_first,
    ) = staged_call(
        functools.partial(backward_kernel, heads, slab, groups),
        in_specs=[in_vmem, anywhere] + [in_vmem] * 2 + [anywhere] + [in_vmem] * 3 + [in_smem] * 2 + [in_vmem] * 11 + [anywhere] * 2,
        out_specs=[in_vmem] * 11,
        out_shape=[
            jax.ShapeDtypeStruct((count, convolved_wide), BF16),
            jax.ShapeDtypeStruct((count, convolved_wide), BF16),
            jax.ShapeDtypeStruct((count, gate_wide), BF16),
            jax.ShapeDtypeStruct((1, DV), F32),
            jax.ShapeDtypeStruct((KW, heads * CONV), F32),
            jax.ShapeDtypeStruct((8, LANES), F32),
            jax.ShapeDtypeStruct((slab, gate_wide), F32),
            jax.ShapeDtypeStruct((slab, gate_wide), F32),
            jax.ShapeDtypeStruct(blocked, BF16),
            jax.ShapeDtypeStruct((slab, piece_a), F32),
            jax.ShapeDtypeStruct((slab, piece_b), F32),
        ],
        scratch_shapes=[
            pltpu.VMEM((HALO + count, projections), F32),
            pltpu.VMEM((width, out_wide), BF16),
            pltpu.VMEM((count, width), BF16),
            pltpu.VMEM((count, width // 2), BF16),
            pltpu.VMEM((count, gate_wide), BF16),
            pltpu.VMEM((count, gate_wide), BF16),
            pltpu.VMEM((heads, count, DV), F32),
            pltpu.VMEM((units, *block), BF16),
            pltpu.VMEM((units, *block), BF16),
            pltpu.VMEM((units, *block), BF16),
            pltpu.VMEM((units, *block), F32),
            pltpu.VMEM((units, *block), F32),
            pltpu.VMEM(block, BF16),
            pltpu.VMEM((groups, *block), BF16),
            pltpu.VMEM((units, *block), BF16),
            pltpu.VMEM((units, *block), BF16),
            pltpu.VMEM((LANES, count), F32),
            pltpu.VMEM((heads, count, count), F32),
            pltpu.VMEM((heads, count, DV), F32),
            pltpu.VMEM((heads, count, DV), F32),
            pltpu.VMEM((heads, count, count), F32),
            pltpu.VMEM((heads, count, DV), F32),
            pltpu.VMEM((heads, HALO, CONV), F32),
            pltpu.VMEM((heads, HALO, CONV), F32),
            pltpu.VMEM((heads, HALO, CONV), F32),
            *sums_scratch(gate_wide, gate_wide),
            landing(rows // 2, width),
            pltpu.VMEM((rows, width), F32),
            *sums_scratch(piece_a, piece_b),
            pltpu.SemaphoreType.DMA,
            pltpu.SemaphoreType.DMA((2,)),
            pltpu.SemaphoreType.DMA((2,)),
            *pairs(3, units, groups, units, heads, heads, heads, 1, 6, 6, 6, 6, 6, 6, 6, 6, 6, 6),
        ],
        compiler_params=pltpu.CompilerParams(vmem_limit_bytes=VMEM_LIMIT, collective_id=6, has_side_effects=True),
        name="backward",
        later=(7, 10, 11, 12, 13, 14, 15, 16, 17, 18, 19, 20),
    )(
        grad_branch,
        out_full,
        mixer_out,
        out_map,
        projected,
        gain_row,
        gated,
        conv_weight,
        decay_log,
        decay_bias,
        normed_split,
        normed_sibling,
        kept,
        totals,
        entering,
        queries,
        keys,
        values,
        inv,
        ffn_part,
        middle,
        piece_1,
        piece_2,
    )
    wide_a = -(-convolved_wide // (2 * LANES)) * LANES
    wide_b = convolved_wide - wide_a
    low, small, late, first_a, first_b = staged_call(
        functools.partial(last_kernel, slab),
        in_specs=[in_vmem] * 12 + [anywhere],
        out_specs=[in_vmem] * 5,
        out_shape=[
            jax.ShapeDtypeStruct(blocked, BF16),
            jax.ShapeDtypeStruct((8, width), F32),
            jax.ShapeDtypeStruct((8, width // 8), F32),
            jax.ShapeDtypeStruct((slab, wide_a), F32),
            jax.ShapeDtypeStruct((slab, wide_b), F32),
        ],
        scratch_shapes=[
            pltpu.VMEM((width, projections), BF16),
            pltpu.VMEM((8, width), F32),
            pltpu.VMEM((8, width // 8), F32),
            pltpu.VMEM(blocked, BF16),
            pltpu.VMEM((2, 6, rows // 2, width // 2), BF16),
            pltpu.VMEM((rows, width), F32),
            pltpu.VMEM((4, 8, width), F32),
            pltpu.VMEM((10, 8, width), F32),
            pltpu.VMEM((4, 8, width // 8), F32),
            pltpu.VMEM((10, 8, width // 8), F32),
            *sums_scratch(wide_a, wide_b),
            pltpu.SemaphoreType.DMA((width // 512,)),
            *pairs((2, 6), 6, 10, 10, 6, 6, 6, 6),
        ],
        compiler_params=pltpu.CompilerParams(vmem_limit_bytes=VMEM_LIMIT, collective_id=5, has_side_effects=True),
        name="last",
        later=(0, 1, 2, 3),
    )(
        grad_gate,
        tokens.reshape(blocked),
        grad_middle,
        mixer_gain.reshape(1, width),
        grad_ffn_gain,
        grad_out_gain,
        grad_scales,
        grad_taps,
        normed_split,
        normed_sibling,
        grad_projected,
        grad_sibling,
        first_full,
    )
    finished = [
        ((slab, heads, PROJ), F32),
        ((2, heads, slab), F32),
        ((slab, heads, DV), F32),
        ((slab, 2, hidden_units), F32),
        ((slab, hidden_units), F32),
        ((count, width), F32),
        ((KW, heads, CONV), F32),
        ((width,), F32),
        ((width,), F32),
        ((DV,), F32),
        ((heads,), F32),
        ((heads,), F32),
        ((count, width), BF16),
    ]
    grad_in, grad_rate, grad_out, grad_gate_up_weight, grad_down, grad_tokens, grad_conv, *gains = staged_call(
        functools.partial(finish_kernel, heads),
        in_specs=[in_vmem] * 14,
        out_specs=[in_vmem] * len(finished),
        out_shape=[jax.ShapeDtypeStruct(shape, kind) for shape, kind in finished],
        scratch_shapes=[],
        compiler_params=pltpu.CompilerParams(vmem_limit_bytes=VMEM_LIMIT),
        name="finish",
    )(
        first_a,
        first_b,
        first_out,
        first_gate,
        *grad_up_first,
        *grad_up,
        grad_down_a,
        grad_down_b,
        low.reshape(count, width),
        small,
        late,
        output.reshape(count, width),
    )
    return (
        gains[5],
        grad_tokens,
        gains[0],
        grad_in,
        jnp.transpose(grad_rate, (2, 0, 1)),
        grad_conv,
        gains[3],
        gains[4],
        gains[2],
        grad_out,
        gains[1],
        grad_gate_up_weight,
        grad_down,
    )


def solution(mesh):
    in_specs = (
        P("seq", None),
        P(),
        P("seq", "head", None),
        P("seq", None, "head"),
        P(None, "head", None),
        P("head"),
        P("head"),
        P(),
        P("seq", "head", None),
        P(),
        P("seq", None, "head"),
        P("seq", "head"),
        P("seq", None),
    )
    out_specs = (
        P("seq", None),
        P("seq", None),
        P(),
        P("seq", "head", None),
        P("seq", None, "head"),
        P(None, "head", None),
        P("head"),
        P("head"),
        P(),
        P("seq", "head", None),
        P(),
        P("seq", None, "head"),
        P("seq", "head"),
    )
    return jax.shard_map(
        per_device, mesh=mesh, in_specs=in_specs, out_specs=out_specs, check_vma=False
    )
```
